32 devices in a mesh: dp: 8 (over z, y), tensor: 4 (over x, core).
Axes of the slice: x: 2, y: 2, z: 4, core: 2. Of those that a mesh axis runs over, the one named last changes fastest.
Arguments:
- tokens: bfloat16 [8192, 768], P(('dp', 'tensor')), may hold values from -6 to 6
- out_grad: bfloat16 [8192, 768], P(('dp', 'tensor')), may hold values from -6 to 6
- segments: int32 [8, 1024], P('dp'), may hold values from 0 to 8, as said below
- neighbours: bfloat16 [128, 256, 768], P('dp'), may hold values from -6 to 6
- norm_gains: bfloat16 [3, 768], replicated, may hold values from 0.5 to 1.5
- norm_biases: bfloat16 [3, 768], replicated, may hold values from -1.25 to 1.25
- self_qkv: bfloat16 [3, 768, 768], P(None, None, 'tensor'), may hold values from -0.21875 to 0.21875
- self_out: bfloat16 [768, 768], P('tensor'), may hold values from -1.75 to 1.75
- cross_q: bfloat16 [768, 768], P(None, 'tensor'), may hold values from -0.21875 to 0.21875
- cross_kv: bfloat16 [2, 768, 768], P(None, None, 'tensor'), may hold values from -0.21875 to 0.21875
- cross_out: bfloat16 [768, 768], P('tensor'), may hold values from -1.75 to 1.75
- mlp_in: bfloat16 [768, 3072], P(None, 'tensor'), may hold values from -0.21875 to 0.21875
- mlp_in_bias: bfloat16 [3072], P('tensor'), may hold values from -1.75 to 1.75
- mlp_out: bfloat16 [3072, 768], P('tensor'), may hold values from -0.109375 to 0.109375
- mlp_out_bias: bfloat16 [768], replicated, may hold values from -1.75 to 1.75
Outputs:
- output: bfloat16 [8192, 768], P(('dp', 'tensor'))
- tokens_grad: bfloat16 [8192, 768], P(('dp', 'tensor'))
- neighbours_grad: bfloat16 [128, 256, 768], P(('dp', 'tensor'))
- norm_gains_grad: float32 [3, 768], replicated
- norm_biases_grad: float32 [3, 768], replicated
- self_qkv_grad: float32 [3, 768, 768], P(None, None, 'tensor')
- self_out_grad: float32 [768, 768], P('tensor')
- cross_q_grad: float32 [768, 768], P(None, 'tensor')
- cross_kv_grad: float32 [2, 768, 768], P(None, None, 'tensor')
- cross_out_grad: float32 [768, 768], P('tensor')
- mlp_in_grad: float32 [768, 3072], P(None, 'tensor')
- mlp_in_bias_grad: float32 [3072], P('tensor')
- mlp_out_grad: float32 [3072, 768], P('tensor')
- mlp_out_bias_grad: float32 [768], replicated
The draws below stay inside these ranges and needn't reach their ends.
Inputs may be any that keep to these rules, and one draw needn't show every extreme that they name: `segments`: ids never fall along a sequence; every sequence has one document that starts before token 128 and ends after token 896; the last token's id is 8.
All inputs are finite; a program needn't handle non-finite values.
Results may differ from the reference program's by a relative error of at most 0.03.
Values may be sent and summed in bfloat16 or wider, within the bound.
No kernel may reach another device: no remote copies, remote signals or barrier semaphores. Data moves between devices by JAX's collectives and lax.ppermute only.
A program may use at most 128 MiB of HBM per device.

```python
import jax
import jax.numpy as jnp
from jax import lax

D = 768
HEADS = 12
HEAD_DIM = 64
FF = 3072
SPAN = 64
SEQ = 1024
NBTOK = 256
SPANS = 16
SEQUENCES = 8
TOKENS = 8192


def draw_segments(key, part):

    def one_sequence(seq_key):
        key_start, key_finish, key_front, key_back = jax.random.split(seq_key, 4)
        eighth = SEQ // 8
        start_cut = jax.random.randint(key_start, (), 1, eighth)
        finish_cut = SEQ - jax.random.randint(key_finish, (), 1, eighth)
        front_cuts = jax.random.randint(key_front, (3,), 1, start_cut + 1)
        back_cuts = jax.random.randint(key_back, (3,), finish_cut, SEQ)
        all_cuts = jnp.concatenate([front_cuts, start_cut[None], finish_cut[None], back_cuts])
        places = jnp.arange(SEQ, dtype=jnp.int32)
        return jnp.sum((all_cuts[None, :] <= places[:, None]).astype(jnp.int32), axis=1)
    seq_keys = jax.random.split(key, SEQUENCES)
    return jax.vmap(one_sequence)(seq_keys).astype(jnp.int32)


def shard_levels(own_key, shape, cuts, low, high):
    loudness = 1.0
    for position, parts in cuts:
        draws = jax.random.uniform(jax.random.fold_in(jax.random.fold_in(own_key, 6), position), (parts,), jnp.float32, low / len(cuts), high / len(cuts))
        loudness = loudness * jnp.repeat(jnp.exp(draws), shape[position] // parts).reshape((-1,) + (1,) * (len(shape) - 1 - position))
    return loudness


def gaussian(key, shape, width, bound, pieces=(), kind=jnp.bfloat16):
    values = jax.random.normal(key, shape, jnp.float32) * width
    if len(pieces) > 0:
        values = shard_levels(key, shape, pieces, -0.22, 0.18) * values
    return jnp.clip(values, min=-bound, max=bound).astype(kind)


def setup_inputs(seed: int = 0) -> dict:
    key_of = jax.random.split(jax.random.key(seed), 16)
    tokens = gaussian(key_of[0], (TOKENS, D), 1.0, 6.0, ((0, 32),))
    out_grad = gaussian(key_of[1], (TOKENS, D), 1.0, 6.0, ((0, 32),))
    segments = draw_segments(jax.random.fold_in(key_of[15], 71), 0)
    neighbours = gaussian(key_of[3], (SEQUENCES * SPANS, NBTOK, D), 1.0, 6.0, ((0, 8),))
    norm_gains = jnp.clip(1.0 + 0.1 * jax.random.normal(key_of[4], (3, D), jnp.float32), 0.5, 1.5).astype(jnp.bfloat16)
    norm_biases = gaussian(key_of[5], (3, D), 0.2, 1.25)
    self_qkv = gaussian(key_of[6], (3, D, D), D ** -0.5, 0.21875, ((2, 4),))
    self_out = gaussian(key_of[7], (D, D), (max(D * 16 // SEQ, 1)) ** -0.5, 1.75, ((0, 4),))
    cross_q = gaussian(key_of[8], (D, D), D ** -0.5, 0.21875, ((1, 4),))
    cross_kv = gaussian(key_of[9], (2, D, D), D ** -0.5, 0.21875, ((2, 4),))
    cross_out = gaussian(key_of[10], (D, D), (max(D * 4 // NBTOK, 1)) ** -0.5, 1.75, ((0, 4),))
    mlp_in = gaussian(key_of[11], (D, FF), D ** -0.5, 0.21875, ((1, 4),))
    mlp_in_bias = gaussian(key_of[12], (FF,), 0.3, 1.75, ((0, 4),))
    mlp_out = gaussian(key_of[13], (FF, D), FF ** -0.5, 0.109375, ((0, 4),))
    mlp_out_bias = gaussian(key_of[14], (D,), 0.3, 1.75)
    return {"tokens": tokens, "out_grad": out_grad, "segments": segments, "neighbours": neighbours, "norm_gains": norm_gains, "norm_biases": norm_biases, "self_qkv": self_qkv, "self_out": self_out, "cross_q": cross_q, "cross_kv": cross_kv, "cross_out": cross_out, "mlp_in": mlp_in, "mlp_in_bias": mlp_in_bias, "mlp_out": mlp_out, "mlp_out_bias": mlp_out_bias}


@jax.custom_vjp
def low(v):
    return lax.optimization_barrier(v.astype(jnp.bfloat16)).astype(jnp.float32)

@jax.custom_vjp
def low_back(v):
    return v

def low_keep(v):
    return (low(v), None)

def low_pass(kept, grad):
    return (grad,)

def back_keep(v):
    return (v, None)

def back_low(kept, grad):
    return (low(grad),)
low.defvjp(low_keep, low_pass)
low_back.defvjp(back_keep, back_low)
norm_epsilon = 1e-05
masked_fill = -1e+30
highest = lax.Precision.HIGHEST

def layer_norm(values, gain, bias):
    center = values - lax.optimization_barrier(jnp.mean(values, -1, keepdims=True))
    spread = lax.optimization_barrier(jnp.mean(center * center, -1, keepdims=True))
    return center * lax.rsqrt(spread + norm_epsilon) * gain + bias

def rope_tables(length, dim_size):
    half_size = dim_size // 2
    places = jnp.arange(length).astype(jnp.float32)
    frequency = 10000.0 ** (-(jnp.arange(half_size).astype(jnp.float32) * 2.0 / dim_size))
    angles = places[:, None] * frequency[None, :]
    return (jnp.cos(angles)[:, None, :], jnp.sin(angles)[:, None, :])

def rotate(values, cosine, sine_part):
    half_size = values.shape[-1] // 2
    first_half = values[..., :half_size]
    second_half = values[..., half_size:]
    return jnp.concatenate([first_half * cosine - second_half * sine_part, second_half * cosine + first_half * sine_part], -1)

def gelu_tanh(values):
    return jax.nn.gelu(values, approximate=True)

def matmul(left, right):
    return jnp.dot(left, right, precision=highest)

def block_forward(segment, tokens, neighbours, gains, biases, self_qkv, self_out, cross_q, cross_kv, cross_out, mlp_in, mlp_in_bias, mlp_out, mlp_out_bias):
    seq_len = tokens.shape[0]
    normed_one = low(layer_norm(tokens, gains[0], biases[0]))
    cosine, sine_part = rope_tables(seq_len, HEAD_DIM)
    query_raw = low_back(matmul(normed_one, self_qkv[0])).reshape(seq_len, HEADS, HEAD_DIM)
    key_raw = low_back(matmul(normed_one, self_qkv[1])).reshape(seq_len, HEADS, HEAD_DIM)
    queries = low(rotate(query_raw, cosine, sine_part))
    keys_rot = low(rotate(key_raw, cosine, sine_part))
    values = low(low_back(matmul(normed_one, self_qkv[2]))).reshape(seq_len, HEADS, HEAD_DIM)
    block_rows = min(512, seq_len)
    key_places = jnp.arange(seq_len)

    def attend(block_index):
        first_row = block_index * block_rows
        query_block = lax.dynamic_slice_in_dim(queries, first_row, block_rows, 0)
        segment_block = lax.dynamic_slice_in_dim(segment, first_row, block_rows, 0)
        row_places = first_row + jnp.arange(block_rows)
        allowed = (row_places[:, None] >= key_places[None, :]) & (segment_block[:, None] == segment[None, :])
        scores = low_back(jnp.einsum('qhe,khe->hqk', query_block, keys_rot, precision=highest) * 0.125)
        scores = jnp.where(allowed[None], scores, masked_fill)
        probs = jax.nn.softmax(scores, -1)
        return low(low_back(jnp.einsum('hqk,khe->qhe', low(probs), values, precision=highest)))
    attended = lax.map(jax.checkpoint(attend), jnp.arange(seq_len // block_rows)).reshape(seq_len, D)
    resid_one = tokens + low_back(matmul(attended, self_out))
    normed_two = low(layer_norm(resid_one, gains[1], biases[1]))
    cross_queries = low(low_back(matmul(normed_two, cross_q)))
    pool_keys = low(low_back(jnp.einsum('pnd,de->pne', neighbours, cross_kv[0], precision=highest)))
    pool_values = low(low_back(jnp.einsum('pnd,de->pne', neighbours, cross_kv[1], precision=highest)))
    span_keys = pool_keys.reshape(SPANS, NBTOK, HEADS, HEAD_DIM)
    span_values = pool_values.reshape(SPANS, NBTOK, HEADS, HEAD_DIM)
    shift_rows = SPAN - 1
    shifted = jnp.concatenate([cross_queries[shift_rows:], jnp.zeros((shift_rows, D), jnp.float32)], 0)
    shifted = shifted.reshape(SPANS, SPAN, HEADS, HEAD_DIM)
    cross_scores = low_back(jnp.einsum('cqhe,cnhe->chqn', shifted, span_keys, precision=highest) * 0.125)
    cross_probs = jax.nn.softmax(cross_scores, -1)
    cross_mixed = low(low_back(jnp.einsum('chqn,cnhe->cqhe', low(cross_probs), span_values, precision=highest)))
    cross_mixed = cross_mixed.reshape(seq_len, D)
    cross_full = jnp.concatenate([jnp.zeros((shift_rows, D), jnp.float32), cross_mixed[:seq_len - shift_rows]], 0)
    resid_two = resid_one + low_back(matmul(cross_full, cross_out))
    normed_three = low(layer_norm(resid_two, gains[2], biases[2]))
    pre_act = low_back(matmul(normed_three, mlp_in) + mlp_in_bias)
    hidden = low(gelu_tanh(pre_act))
    return resid_two + matmul(hidden, mlp_out) + mlp_out_bias

def reference(tokens, out_grad, segments, neighbours, norm_gains, norm_biases, self_qkv, self_out, cross_q, cross_kv, cross_out, mlp_in, mlp_in_bias, mlp_out, mlp_out_bias):
    seq_tokens = tokens.astype(jnp.float32).reshape(SEQUENCES, SEQ, D)
    seq_neighbours = neighbours.astype(jnp.float32).reshape(SEQUENCES, SPANS, NBTOK, D)
    cotangent = out_grad.astype(jnp.float32).reshape(SEQUENCES, SEQ, D)
    params = (norm_gains, norm_biases, self_qkv, self_out, cross_q, cross_kv, cross_out, mlp_in, mlp_in_bias, mlp_out, mlp_out_bias)
    params = tuple((item.astype(jnp.float32) for item in params))
    checked = jax.checkpoint(block_forward)

    def forward(all_tokens, all_neighbours, *weights):

        def one_sequence(items):
            seq_index, seq_input, seq_nb = items
            return checked(segments[seq_index], seq_input, seq_nb, *weights)
        return lax.map(one_sequence, (jnp.arange(SEQUENCES), all_tokens, all_neighbours))
    result, pullback = jax.vjp(forward, seq_tokens, seq_neighbours, *params)
    grads = pullback(cotangent)
    output = result.reshape(TOKENS, D).astype(jnp.bfloat16)
    tokens_grad = grads[0].reshape(TOKENS, D).astype(jnp.bfloat16)
    neighbours_grad = grads[1].reshape(SEQUENCES * SPANS, NBTOK, D).astype(jnp.bfloat16)
    return (output, tokens_grad, neighbours_grad, grads[2], grads[3], grads[4], grads[5], grads[6], grads[7], grads[8], grads[9], grads[10], grads[11], grads[12])
```

```python
import jax
import jax.numpy as jnp
from jax import lax
from jax.sharding import PartitionSpec as P

HEAD_DIM = 64
SPAN = 64
EPS = 1e-05
MASKED = -1e30
BF = jnp.bfloat16
F32 = jnp.float32


def norm_rows(values):
    center = values - jnp.mean(values, -1, keepdims=True)
    inverse = lax.rsqrt(jnp.mean(center * center, -1, keepdims=True) + EPS)
    return center * inverse, inverse


def norm_back(upstream, normed, inverse, gain):
    scaled = upstream * gain
    return inverse * (
        scaled
        - jnp.mean(scaled, -1, keepdims=True)
        - normed * jnp.mean(scaled * normed, -1, keepdims=True)
    )


def rope_tables(length):
    half = HEAD_DIM // 2
    places = jnp.arange(length).astype(F32)
    frequency = 10000.0 ** (-(jnp.arange(half).astype(F32) * 2.0 / HEAD_DIM))
    angles = places[:, None] * frequency[None, :]
    return jnp.cos(angles)[:, None, :], jnp.sin(angles)[:, None, :]


def rotate(values, cosine, sine):
    half = values.shape[-1] // 2
    first, second = values[..., :half], values[..., half:]
    return jnp.concatenate(
        [first * cosine - second * sine, second * cosine + first * sine], -1
    )


def gelu_tanh(values):
    return jax.nn.gelu(values, approximate=True)


def nn(left, right):
    return jnp.dot(left, right, preferred_element_type=F32)


def nt(left, right):
    return lax.dot_general(left, right, (((1,), (1,)), ((), ())), preferred_element_type=F32)


def tn(left, right):
    return lax.dot_general(left, right, (((0,), (0,)), ((), ())), preferred_element_type=F32)


def swap(value, axis, bit, size):
    return lax.ppermute(value, axis, [(i, i ^ bit) for i in range(size)])


def core_swap(value):
    return swap(value, "tensor", 1, 4)


def x_swap(value):
    return swap(value, "tensor", 2, 4)


def gather_blocks(block):
    far = x_swap(block)
    return [block, core_swap(block), far, core_swap(far)]


def scatter_sum(blocks):
    send = jnp.concatenate([blocks[1], blocks[3]], 0)
    got = core_swap(send)
    rows = blocks[0].shape[0]
    far = (blocks[2].astype(F32) + got[rows:].astype(F32)).astype(BF)
    far = x_swap(far)
    return blocks[0].astype(F32) + got[:rows].astype(F32) + far.astype(F32)


def reduce_dp(pack, size):
    place = lax.axis_index("dp")
    bits = []
    bit = 1
    while bit < size:
        bits.append(bit)
        bit *= 2
    for bit in bits:
        half = pack.shape[0] // 2
        mine = (place // bit) % 2
        send = lax.dynamic_slice_in_dim(pack, (1 - mine) * half, half, 0)
        keep = lax.dynamic_slice_in_dim(pack, mine * half, half, 0)
        got = swap(send, "dp", bit, size)
        pack = (keep.astype(F32) + got.astype(F32)).astype(BF)
    for bit in reversed(bits):
        mine = (place // bit) % 2
        got = swap(pack, "dp", bit, size)
        pack = jnp.where(
            mine == 0, jnp.concatenate([pack, got], 0), jnp.concatenate([got, pack], 0)
        )
    return pack


def make_local(dp_size):
    def local(
        tokens,
        out_grad,
        segments,
        neighbours,
        norm_gains,
        norm_biases,
        self_qkv,
        self_out,
        cross_q,
        cross_kv,
        cross_out,
        mlp_in,
        mlp_in_bias,
        mlp_out,
        mlp_out_bias,
    ):
        t = lax.axis_index("tensor")
        rows, width = tokens.shape
        seq_len = 4 * rows
        local_width = self_out.shape[0]
        heads = local_width // HEAD_DIM
        gains = norm_gains.astype(F32)
        biases = norm_biases.astype(F32)
        segment = segments[0]

        def to_absolute(blocks):
            pairs = jnp.where(
                t % 2 == 0,
                jnp.concatenate([jnp.stack(blocks[:2]), jnp.stack(blocks[2:])], 0),
                jnp.concatenate([jnp.stack(blocks[1::-1]), jnp.stack(blocks[3:1:-1])], 0),
            )
            turned = jnp.where(t // 2 == 0, pairs, jnp.concatenate([pairs[2:], pairs[:2]], 0))
            return turned.reshape((-1,) + turned.shape[2:])

        def block_of(whole, j):
            return lax.dynamic_slice_in_dim(whole, (t ^ j) * rows, rows, 0)

        token_blocks = gather_blocks(tokens)
        kv_pack = jnp.concatenate([cross_kv[0].T, cross_kv[1].T], 0)
        kv_full = jnp.stack(gather_blocks(kv_pack)).reshape(4, 2, heads, HEAD_DIM, width)
        rest_pack = jnp.concatenate([self_out, cross_q.T, cross_out], 0)
        rest_full = jnp.stack(gather_blocks(rest_pack)).reshape(4, 3, local_width, width)
        so_full = rest_full[:, 0].reshape(width, width)
        cq_full = rest_full[:, 1].reshape(width, width)
        co_full = rest_full[:, 2].reshape(width, width)
        grads_whole = jnp.concatenate(gather_blocks(out_grad), 0)

        whole_tokens = to_absolute(token_blocks)
        normed_one, _ = norm_rows(whole_tokens.astype(F32))
        input_one = (normed_one * gains[0] + biases[0]).astype(BF)
        projected = jnp.einsum("sd,kde->kse", input_one, self_qkv, preferred_element_type=F32)
        cosine, sine = rope_tables(seq_len)
        shape = (seq_len, heads, HEAD_DIM)
        queries = rotate(projected[0].reshape(shape), cosine, sine).astype(BF)
        keys = rotate(projected[1].reshape(shape), cosine, sine).astype(BF)
        values = projected[2].reshape(shape).astype(BF)
        places = jnp.arange(seq_len)
        allowed = (places[:, None] >= places[None, :]) & (segment[:, None] == segment[None, :])

        def self_scores():
            scores = jnp.einsum("qhe,khe->hqk", queries, keys, preferred_element_type=F32) * 0.125
            return jnp.where(allowed[None], scores, MASKED)

        scores = self_scores()
        row_max = jnp.max(scores, -1, keepdims=True)
        expo = jnp.exp(scores - row_max)
        row_sum = jnp.sum(expo, -1, keepdims=True)
        self_lse = row_max + jnp.log(row_sum)
        attended_heads = jnp.einsum(
            "hqk,khe->qhe", (expo / row_sum).astype(BF), values, preferred_element_type=F32
        ).astype(BF).reshape(seq_len, local_width)
        attended = jnp.concatenate(
            [block_of(attended_heads, 0)]
            + [swap(block_of(attended_heads, j), "tensor", j, 4) for j in (1, 2, 3)],
            1,
        )

        resid_one = tokens.astype(F32) + nn(attended, so_full)
        normed_two, inverse_two = norm_rows(resid_one)
        input_two = (normed_two * gains[1] + biases[1]).astype(BF)
        cross_queries = nt(input_two, cq_full).astype(BF)
        sets = neighbours.shape[0] // 4
        nb_tokens = neighbours.shape[1]
        before = lax.dynamic_slice_in_dim(neighbours, jnp.maximum(sets * t - 1, 0), 1, 0)
        own_sets = jnp.concatenate(
            [before, lax.dynamic_slice_in_dim(neighbours, sets * t, sets, 0)], 0
        )
        groups = sets + 1
        pool = jnp.einsum(
            "pnd,jkhed->kpnjhe", own_sets, kv_full, preferred_element_type=F32
        ).astype(BF).reshape(2, groups, nb_tokens, 4 * heads, HEAD_DIM)
        tail = SPAN * groups - rows - 1
        span_rows = (jnp.arange(groups * SPAN) >= jnp.where(t == 0, SPAN, 1)) & (
            jnp.arange(groups * SPAN) < rows + 1
        )

        def to_spans(array):
            padded = jnp.pad(array, ((1, tail), (0, 0)))
            padded = jnp.where(span_rows[:, None], padded, jnp.zeros((), array.dtype))
            return padded.reshape(groups, SPAN, 4 * heads, HEAD_DIM)

        def from_spans(array):
            flat = array.reshape(groups * SPAN, width)
            return jnp.where(span_rows[:, None], flat, jnp.zeros((), flat.dtype))[1 : rows + 1]

        shifted = to_spans(cross_queries)
        cross_scores = (
            jnp.einsum("cqhe,cnhe->chqn", shifted, pool[0], preferred_element_type=F32) * 0.125
        )
        cross_max = jnp.max(cross_scores, -1, keepdims=True)
        cross_expo = jnp.exp(cross_scores - cross_max)
        cross_probs = cross_expo / jnp.sum(cross_expo, -1, keepdims=True)
        cross_low = cross_probs.astype(BF)
        cross_mixed = jnp.einsum(
            "chqn,cnhe->cqhe", cross_low, pool[1], preferred_element_type=F32
        ).astype(BF)
        cross_mixed = from_spans(cross_mixed)
        resid_two = resid_one + nn(cross_mixed, co_full)
        normed_three, inverse_three = norm_rows(resid_two)
        input_three = (normed_three * gains[2] + biases[2]).astype(BF)

        mlp_rows = jnp.concatenate(gather_blocks(input_three), 0)
        pre_act = nn(mlp_rows, mlp_in) + mlp_in_bias.astype(F32)
        hidden, gelu_pull = jax.vjp(gelu_tanh, pre_act)
        hidden = hidden.astype(BF)
        grad_hidden = nt(grads_whole, mlp_out)
        grad_pre = gelu_pull(grad_hidden)[0].astype(BF)
        part_three = nt(grad_pre, mlp_in).astype(BF).reshape(4, rows, width)
        grad_norm_three = scatter_sum(part_three)
        branch_three = nn(hidden, mlp_out).astype(BF).reshape(4, rows, width)
        branch_three = scatter_sum(branch_three)
        output = (resid_two + branch_three + mlp_out_bias.astype(F32)).astype(BF)
        grad_mlp_out = reduce_dp(tn(hidden, grads_whole).astype(BF), dp_size)
        grad_mlp_in = reduce_dp(tn(mlp_rows, grad_pre).astype(BF), dp_size)
        bias_in_part = jnp.sum(grad_pre, 0, dtype=F32)
        bias_out_part = jnp.sum(out_grad, 0, dtype=F32)

        grads_two = out_grad.astype(F32) + norm_back(
            grad_norm_three, normed_three, inverse_three, gains[2]
        )
        grads_two_low = grads_two.astype(BF)
        co_part = tn(cross_mixed, grads_two_low)
        grad_mixed = to_spans(nt(grads_two_low, co_full).astype(BF))
        grad_probs = jnp.einsum(
            "cqhe,cnhe->chqn", grad_mixed, pool[1], preferred_element_type=F32
        )
        inner = jnp.sum(cross_probs * grad_probs, -1, keepdims=True)
        grad_scores = (cross_probs * (grad_probs - inner)).astype(BF)
        grad_queries = (
            jnp.einsum("chqn,cnhe->cqhe", grad_scores, pool[0], preferred_element_type=F32) * 0.125
        )
        grad_queries = from_spans(grad_queries.astype(BF))
        grad_norm_two = nn(grad_queries, cq_full)
        grads_one = grads_two + norm_back(grad_norm_two, normed_two, inverse_two, gains[1])
        grads_one_low = grads_one.astype(BF)
        grad_attended = nt(grads_one_low, so_full).astype(BF).reshape(rows, 4, local_width)

        upstream = to_absolute(
            [grad_attended[:, 0]]
            + [swap(grad_attended[:, j], "tensor", j, 4) for j in (1, 2, 3)]
        ).reshape(shape)
        probs = jnp.exp(self_scores() - self_lse)
        grad_self_probs = jnp.einsum("qhe,khe->hqk", upstream, values, preferred_element_type=F32)
        self_inner = jnp.sum(probs * grad_self_probs, -1, keepdims=True)
        grad_self_scores = (probs * (grad_self_probs - self_inner)).astype(BF)
        query_grads = (
            jnp.einsum("hqk,khe->qhe", grad_self_scores, keys, preferred_element_type=F32) * 0.125
        )
        key_grads = (
            jnp.einsum("hqk,qhe->khe", grad_self_scores, queries, preferred_element_type=F32)
            * 0.125
        )
        value_grads = jnp.einsum(
            "hqk,qhe->khe", probs.astype(BF), upstream, preferred_element_type=F32
        )
        grad_projected = jnp.stack(
            [
                rotate(query_grads, cosine, -sine).astype(BF),
                rotate(key_grads, cosine, -sine).astype(BF),
                value_grads.astype(BF),
            ]
        ).reshape(3, seq_len, local_width)
        qkv_part = jnp.einsum("sd,kse->ked", input_one, grad_projected, preferred_element_type=F32)
        grad_qkv = reduce_dp(qkv_part.astype(BF).reshape(3 * local_width, width), dp_size)
        grad_self_qkv = grad_qkv.reshape(3, local_width, width).transpose(0, 2, 1).astype(F32)
        part_one = jnp.einsum(
            "kse,kde->sd", grad_projected, self_qkv, preferred_element_type=F32
        ).astype(BF)
        grad_norm_one = scatter_sum([block_of(part_one, j) for j in range(4)])
        own_normed, own_inverse = norm_rows(tokens.astype(F32))
        tokens_grad = (
            grads_one + norm_back(grad_norm_one, own_normed, own_inverse, gains[0])
        ).astype(BF)

        grad_keys = (
            jnp.einsum("chqn,cqhe->cnhe", grad_scores, shifted, preferred_element_type=F32) * 0.125
        )
        grad_values = jnp.einsum(
            "chqn,cqhe->cnhe", cross_low, grad_mixed, preferred_element_type=F32
        )
        grad_pool = (
            jnp.stack([grad_keys, grad_values])
            .astype(BF)
            .reshape(2, groups, nb_tokens, 4, heads, HEAD_DIM)
        )
        kv_part = jnp.einsum(
            "pnd,kpnjhe->jkhed", own_sets, grad_pool, preferred_element_type=F32
        ).reshape(4, 2 * local_width, width)
        nb_part = jnp.einsum("kpnjhe,jkhed->pnd", grad_pool, kv_full, preferred_element_type=F32)
        back = lax.ppermute(nb_part[0].astype(BF), "tensor", [(i + 1, i) for i in range(3)])
        last = nb_part[sets] + back.astype(F32)
        neighbours_grad = jnp.concatenate([nb_part[1:sets], last[None]], 0).astype(BF)
        cq_part = tn(grad_queries, input_two).reshape(4, local_width, width)
        so_part = tn(attended, grads_one_low).reshape(4, local_width, width)
        co_part = co_part.reshape(4, local_width, width)
        parts = jnp.concatenate([so_part, co_part, cq_part, kv_part], 1).astype(BF)
        own_part = reduce_dp(scatter_sum(parts).astype(BF), dp_size).astype(F32)
        own_part = own_part.reshape(5, local_width, width)
        grad_self_out = own_part[0]
        grad_cross_out = own_part[1]
        grad_cross_q = own_part[2].T
        grad_cross_kv = own_part[3:].transpose(0, 2, 1)

        small = jnp.stack(
            [
                jnp.sum(grad_norm_one * own_normed, 0),
                jnp.sum(grad_norm_two * normed_two, 0),
                jnp.sum(grad_norm_three * normed_three, 0),
                jnp.sum(grad_norm_one, 0),
                jnp.sum(grad_norm_two, 0),
                jnp.sum(grad_norm_three, 0),
                bias_out_part,
            ]
        )
        small = small + core_swap(small)
        small = small + x_swap(small)
        small = jnp.concatenate([small, bias_in_part[None]], 0)
        bit = 1
        while bit < dp_size:
            small = small + swap(small, "dp", bit, dp_size)
            bit *= 2
        return (
            output,
            tokens_grad,
            neighbours_grad,
            small[:3],
            small[3:6],
            grad_self_qkv,
            grad_self_out,
            grad_cross_q,
            grad_cross_kv,
            grad_cross_out,
            grad_mlp_in.astype(F32),
            small[7],
            grad_mlp_out.astype(F32),
            small[6],
        )

    return local


def solution(mesh):
    rows = P(("dp", "tensor"), None)
    in_specs = (
        rows,
        rows,
        P("dp", None),
        P("dp", None, None),
        P(),
        P(),
        P(None, None, "tensor"),
        P("tensor", None),
        P(None, "tensor"),
        P(None, None, "tensor"),
        P("tensor", None),
        P(None, "tensor"),
        P("tensor"),
        P("tensor", None),
        P(),
    )
    out_specs = (
        rows,
        rows,
        P(("dp", "tensor"), None, None),
        P(),
        P(),
        P(None, None, "tensor"),
        P("tensor", None),
        P(None, "tensor"),
        P(None, None, "tensor"),
        P("tensor", None),
        P(None, "tensor"),
        P("tensor"),
        P("tensor", None),
        P(),
    )
    return jax.shard_map(
        make_local(mesh.shape["dp"]),
        mesh=mesh,
        in_specs=in_specs,
        out_specs=out_specs,
        check_vma=False,
    )
```

```python
import functools

import jax
import jax.numpy as jnp
from jax import lax
from jax.experimental import pallas as pl
from jax.experimental.pallas import tpu as pltpu
from jax.sharding import PartitionSpec as P

HEAD_DIM = 64
SPAN = 64
EPS = 1e-05
MASKED = -1e30
LANES = 256
QUAD = LANES // HEAD_DIM
COST = {
    "self_forward": 24.09,
    "pool": 19.8,
    "cross_forward": 14.52,
    "mlp_half": 10.23,
    "mlp_out_grads": 7.92,
    "mlp_in_grads": 6.6,
    "mlp_branch": 6.27,
    "cross_backward": 25.41,
    "cross_grads": 5.61,
    "pool_grads": 16.5,
    "self_backward": 31.02,
    "norm_one": 6.93,
    "sets_grads": 12.21,
}
BF = jnp.bfloat16
F32 = jnp.float32


def nn(left, right):
    return jnp.dot(left, right, preferred_element_type=F32)


def nt(left, right):
    return lax.dot_general(left, right, (((1,), (1,)), ((), ())), preferred_element_type=F32)


def tn(left, right):
    return lax.dot_general(left, right, (((0,), (0,)), ((), ())), preferred_element_type=F32)


def norm_rows(values):
    center = values - jnp.mean(values, -1, keepdims=True)
    inverse = lax.rsqrt(jnp.mean(center * center, -1, keepdims=True) + EPS)
    return center * inverse, inverse


def norm_back(upstream, normed, inverse, gain):
    scaled = upstream * gain
    return inverse * (
        scaled
        - jnp.mean(scaled, -1, keepdims=True)
        - normed * jnp.mean(scaled * normed, -1, keepdims=True)
    )


def lane_head(shape):
    return lax.broadcasted_iota(jnp.int32, shape, len(shape) - 1) // HEAD_DIM


def half_swap(values):
    half = HEAD_DIM // 2
    width = values.shape[1]
    lane = lax.broadcasted_iota(jnp.int32, values.shape, 1)
    return jnp.where(
        lane % HEAD_DIM < half,
        pltpu.roll(values, width - half, 1),
        pltpu.roll(values, half, 1),
    )


def staged(name, body, words, arrays, near, far, scratch=(), raw=(), limit=16):
    n, r, p, f = len(arrays), len(raw), len(near), len(far)

    def kernel(word, *refs):
        cuts = [n, n + r, n + r + p, n + r + p + f]
        body(word, *[refs[a:b] for a, b in zip([0] + cuts, cuts + [len(refs)])])

    hbm, vmem = pl.BlockSpec(memory_space=pltpu.HBM), pl.BlockSpec(memory_space=pltpu.VMEM)
    return pl.pallas_call(
        kernel,
        out_shape=list(near) + list(far),
        in_specs=[pl.BlockSpec(memory_space=pltpu.SMEM)] + [vmem] * n + [hbm] * r,
        out_specs=[vmem] * (p + f),
        scratch_shapes=list(scratch),
        compiler_params=pltpu.CompilerParams(vmem_limit_bytes=limit * 2**20),
        cost_estimate=pl.CostEstimate(flops=int(COST.get(name, 0.8) * 10**9), bytes_accessed=10**4, transcendentals=0),
        name=name,
    )(words, *arrays, *raw)


def joined(words, parts):
    def body(word, ins, raws, sends, outs, scratch):
        for i, part in enumerate(ins):
            sends[0][i] = part[...]

    return staged("joined", body, words, parts, [low_shape(len(parts), *parts[0].shape)], [], limit=4)[0]


def plus(words, left, right):
    rows, width = left.shape[0], left.shape[1]
    half = min(rows, right.shape[0] // 2)

    def body(word, ins, raws, sends, outs, scratch):
        a, b = ins
        sends[0][...] = (a[rows - half :, :].astype(F32) + b[half:, :].astype(F32)).astype(BF)

    return staged("plus", body, words, [left, right], [low_shape(half, width)], [], limit=6)[0]


def low_shape(*shape):
    return jax.ShapeDtypeStruct(shape, BF)


def wide_shape(*shape):
    return jax.ShapeDtypeStruct(shape, F32)


def block_mask(start_ref, i, rows):
    keys = (i + 1) * rows
    row = lax.broadcasted_iota(jnp.int32, (keys, rows), 0)
    place = lax.broadcasted_iota(jnp.int32, (keys, rows), 1) + i * rows
    start = start_ref[0:1, i * rows : (i + 1) * rows]
    return jnp.where((row >= start) & (row <= place), 0.0, MASKED)


def tables(cos_ref, sin_ref, part):
    return jnp.concatenate([cos_ref[part, :]] * 2, 1), jnp.concatenate([sin_ref[part, :]] * 2, 1)


def self_forward(words, toks, gains, biases, weights, cosine, sine, start, heads):
    rows, width = toks[0].shape
    total = 4 * rows
    local = heads * HEAD_DIM

    def body(word, ins, raws, sends, outs, scratch):
        tok0, gain_ref, bias_ref, w_ref, tok1, tok2, tok3, cos_ref, sin_ref, start_ref = ins
        x_ref, q_ref, k_ref, v_ref, lse_ref, o_ref = outs
        mask_ref, pad_ref = scratch
        t = word[0]
        for c in range(3):
            pad_ref[c, 0:local, :] = w_ref[c]
            pad_ref[c, local:, :] = jnp.zeros((LANES - local, width), BF)
        for j, tok in enumerate((tok0, tok1, tok2, tok3)):
            normed, _ = norm_rows(tok[...].astype(F32))
            x_ref[pl.ds(pl.multiple_of((t ^ j) * rows, rows), rows), :] = (
                normed * gain_ref[0:1, :] + bias_ref[0:1, :]
            ).astype(BF)
        for i in range(4):
            part = pl.ds(i * rows, rows)
            x = x_ref[part, :]
            cosines, sines = tables(cos_ref, sin_ref, part)
            q = nt(x, pad_ref[0])
            q_ref[part, :] = ((q * cosines + half_swap(q) * sines) * 0.125).astype(BF)
            k = nt(x, pad_ref[1])
            k_ref[part, :] = (k * cosines + half_swap(k) * sines).astype(BF)
            v_ref[part, :] = nt(x, pad_ref[2]).astype(BF)
        lane = lane_head((1, LANES))
        lse_ref[...] = jnp.zeros(lse_ref.shape, F32)
        for i in range(4):
            part = pl.ds(i * rows, rows)
            keys = (i + 1) * rows
            mask_ref[0:keys, :] = block_mask(start_ref, i, rows)
            out = jnp.zeros((rows, LANES), F32)
            for h in range(heads):
                qh = jnp.where(lane == h, q_ref[part, :], jnp.zeros((), BF))
                s = nt(k_ref[0:keys, :], qh) + mask_ref[0:keys, :]
                top = jnp.max(s, 0, keepdims=True)
                p = jnp.exp(s - top)
                norm = jnp.sum(p, 0, keepdims=True)
                lse_ref[h : h + 1, i * rows : (i + 1) * rows] = top + jnp.log(norm)
                low = (p * (1.0 / norm)).astype(BF)
                out = jnp.where(lane == h, tn(low, v_ref[0:keys, :]), out)
            o_ref[part, :] = out.astype(BF)
        for j, a in enumerate(sends):
            a[...] = o_ref[pl.ds(pl.multiple_of((t ^ j) * rows, rows), rows), 0:local]

    out = staged(
        "self_forward",
        body,
        words,
        [toks[0], gains, biases, weights, toks[1], toks[2], toks[3], cosine, sine, start],
        [low_shape(rows, local)] * 4,
        [low_shape(total, width)] + [low_shape(total, LANES)] * 3 + [wide_shape(8, total), low_shape(total, LANES)],
        [pltpu.VMEM((total, rows), F32), pltpu.VMEM((3, LANES, width), BF)],
    )
    return out[:4], out[4:]


def self_backward(words, ups, saved, cosine, sine, start, heads):
    total, width = saved[0].shape
    rows = total // 4
    local = heads * HEAD_DIM

    def body(word, ins, raws, sends, outs, scratch):
        d0, d1, d2, d3, o_ref, q_ref, k_ref, start_ref, v_ref, lse_ref, cos_ref, sin_ref, x_ref = ins
        (pack_ref,) = sends
        (grad_ref,) = outs
        d_ref, mask_ref, dk_ref, dv_ref, delta_ref = scratch
        t = word[0]
        d_ref[...] = jnp.zeros_like(d_ref)
        for j, d in enumerate((d0, d1, d2, d3)):
            d_ref[pl.ds(pl.multiple_of((t ^ j) * rows, rows), rows), 0:local] = d[...]
        pick = (lax.broadcasted_iota(jnp.int32, (8, LANES), 0) == lane_head((8, LANES))).astype(F32)
        delta_ref[...] = lax.dot_general(
            pick,
            d_ref[...].astype(F32) * o_ref[...].astype(F32),
            (((1,), (1,)), ((), ())),
            precision=lax.Precision.HIGHEST,
            preferred_element_type=F32,
        )
        dk_ref[...] = jnp.zeros_like(dk_ref)
        dv_ref[...] = jnp.zeros_like(dv_ref)
        lane = lane_head((1, LANES))
        zero = jnp.zeros((), BF)
        for i in range(4):
            part = pl.ds(i * rows, rows)
            keys = (i + 1) * rows
            mask_ref[0:keys, :] = block_mask(start_ref, i, rows)
            dq = jnp.zeros((rows, LANES), F32)
            for h in range(heads):
                qh = jnp.where(lane == h, q_ref[part, :], zero)
                dh = jnp.where(lane == h, d_ref[part, :], zero)
                lse = lse_ref[h : h + 1, i * rows : (i + 1) * rows]
                delta = delta_ref[h : h + 1, i * rows : (i + 1) * rows]
                s = nt(k_ref[0:keys, :], qh) + mask_ref[0:keys, :]
                p = jnp.exp(s - lse)
                dp = nt(v_ref[0:keys, :], dh)
                ds = (p * (dp - delta)).astype(BF)
                dv_ref[0:keys, :] += nn(p.astype(BF), dh)
                dk_ref[0:keys, :] += nn(ds, qh)
                dq = jnp.where(lane == h, tn(ds, k_ref[0:keys, :]), dq)
            cosines, sines = tables(cos_ref, sin_ref, part)
            dq = dq * 0.125
            grad_ref[part, 0:LANES] = (dq * cosines - half_swap(dq) * sines).astype(BF)
        for i in range(4):
            part = pl.ds(i * rows, rows)
            cosines, sines = tables(cos_ref, sin_ref, part)
            dk = dk_ref[part, :]
            grad_ref[part, LANES : 2 * LANES] = (dk * cosines - half_swap(dk) * sines).astype(BF)
            grad_ref[part, 2 * LANES : 3 * LANES] = dv_ref[part, :].astype(BF)
        for c in range(3):
            product = tn(grad_ref[:, c * LANES : (c + 1) * LANES], x_ref[...])
            pack_ref[c * local : (c + 1) * local, :] = product[0:local].astype(BF)

    x, q, k, v, lse, o = saved
    return staged(
        "self_backward",
        body,
        words,
        [*ups, o, q, k, start, v, lse, cosine, sine, x],
        [low_shape(3 * local, width)],
        [low_shape(total, 3 * LANES)],
        [
            pltpu.VMEM((total, LANES), BF),
            pltpu.VMEM((total, rows), F32),
            pltpu.VMEM((total, LANES), F32),
            pltpu.VMEM((total, LANES), F32),
            pltpu.VMEM((8, total), F32),
        ],
    )


def norm_one(words, grad, weights):
    rows, local, width = grad.shape[0] // 4, weights.shape[1], weights.shape[2]

    def body(word, ins, raws, sends, outs, scratch):
        grad_ref, w_ref = ins
        for p, j in enumerate((3, 1, 2, 0)):
            at = pl.ds(pl.multiple_of((word[0] ^ j) * rows, rows), rows)
            total = jnp.zeros((rows, width), F32)
            for c in range(3):
                total = total + nn(grad_ref[at, c * LANES : c * LANES + local], w_ref[c])
            target = sends[0] if j % 2 == 0 else sends[1]
            at = (j // 2) * rows
            target[at : at + rows, :] = total.astype(BF)

    return staged("norm_one", body, words, [grad, weights], [low_shape(2 * rows, width)] * 2, [])


def spread(values, t, block):
    shape = (LANES, LANES)
    tiled = jnp.concatenate([values] * QUAD, 0)
    row = lax.broadcasted_iota(jnp.int32, shape, 0)
    keep = (row // SPAN) == lane_head(shape)
    if block == 0:
        keep = keep & (row % SPAN > 0) & (t > 0)
    if block == 4:
        keep = keep & (row % SPAN == 0)
    return jnp.where(keep, tiled, jnp.zeros((), values.dtype))


def collect(values, t, block):
    shape = (SPAN, LANES)
    head = lane_head(shape)
    out = jnp.zeros(shape, values.dtype)
    for h in range(QUAD):
        out = jnp.where(head == h, values[h * SPAN : (h + 1) * SPAN], out)
    row = lax.broadcasted_iota(jnp.int32, shape, 0)
    if block == 0:
        out = jnp.where((row > 0) & (t > 0), out, 0.0)
    if block == 4:
        out = jnp.where(row == 0, out, 0.0)
    return out


def unroll_rows(parts):
    return pltpu.roll(jnp.concatenate([parts[0] + parts[4]] + parts[1:4], 0), 4 * SPAN - 1, 0)


def fetch_sets(t, nb_ref, buffer_ref, sem_ref):
    copies = []
    for b in range(5):
        at = jnp.maximum(4 * t - 1 + b, 0)
        copies.append(pltpu.make_async_copy(nb_ref.at[at], buffer_ref.at[b], sem_ref.at[b]))
        copies[-1].start()
    return copies


def pool(words, neighbours, own, core, far, both):
    tokens, width = neighbours.shape[1:]
    local = own.shape[1]

    def body(word, ins, raws, sends, outs, scratch):
        own_ref, core_ref, far_ref, both_ref = ins
        pk_ref, pv_ref, k_ref, v_ref = outs
        copies = fetch_sets(word[0], raws[0], *scratch)
        for i, target in enumerate((k_ref, v_ref)):
            other = i ^ word[1]
            for p, source in enumerate((own_ref[i], far_ref[other], core_ref[i], both_ref[other])):
                target[p * local : (p + 1) * local, :] = source
        for b in range(5):
            copies[b].wait()
            pk_ref[b] = nt(scratch[0][b], k_ref[...]).astype(BF)
            pv_ref[b] = nt(scratch[0][b], v_ref[...]).astype(BF)

    return staged(
        "pool",
        body,
        words,
        [own, core, far, both],
        [],
        [low_shape(5, tokens, width)] * 2 + [low_shape(width, width)] * 2,
        [pltpu.VMEM((5, tokens, width), BF), pltpu.SemaphoreType.DMA((5,))],
        raw=[neighbours],
    )


def cross_forward(words, tokens, a, rest, pool_keys, pool_values, gains, biases):
    rows, width = tokens.shape
    local = a[0].shape[1]
    quads = width // LANES

    def body(word, ins, raws, sends, outs, scratch):
        own_ref, core_ref, far_ref, both_ref, tok_ref, a0, a1, a2, a3, gain_ref, bias_ref, pk_ref, pv_ref = ins
        (in_three_ref,) = sends
        so_ref, cq_ref, co_ref, one_ref, two_ref, in_two_ref, q_ref, o_ref, lse_ref = outs
        t = word[0]
        half = local // 2
        for i, target in enumerate((so_ref, cq_ref, co_ref)):
            target[0:local, :] = own_ref[i]
            target[2 * local : 3 * local, :] = core_ref[i]
            for h in range(2):
                at = local + h * half
                target[at : at + half, :] = far_ref[h ^ word[1], i]
                at = 3 * local + h * half
                target[at : at + half, :] = both_ref[h ^ word[1], i]
        resid = tok_ref[...].astype(F32)
        for p, ap in enumerate((a0, a1, a2, a3)):
            resid = resid + nn(ap[...], so_ref[p * local : (p + 1) * local, :])
        one_ref[...] = resid
        normed, _ = norm_rows(resid)
        low = (normed * gain_ref[1:2, :] + bias_ref[1:2, :]).astype(BF)
        in_two_ref[...] = low
        q = nt(low, cq_ref[...]).astype(BF).astype(F32) * 0.125
        q_ref[...] = pltpu.roll(q, 1, 0).astype(BF)
        lse_ref[...] = jnp.zeros(lse_ref.shape, F32)
        for g in range(quads):
            cols = slice(g * LANES, (g + 1) * LANES)
            parts = []
            for b in range(5):
                at = (b % 4) * SPAN
                s = nt(pk_ref[b, :, cols], spread(q_ref[at : at + SPAN, cols], t, b))
                top = jnp.max(s, 0, keepdims=True)
                p = jnp.exp(s - top)
                norm = jnp.sum(p, 0, keepdims=True)
                lse_ref[g * 8 + b : g * 8 + b + 1, :] = top + jnp.log(norm)
                low = (p * (1.0 / norm)).astype(BF)
                parts.append(collect(tn(low, pv_ref[b, :, cols]), t, b))
            o_ref[:, cols] = unroll_rows(parts).astype(BF)
        resid = resid + nn(o_ref[...], co_ref[...])
        two_ref[...] = resid
        normed, _ = norm_rows(resid)
        in_three_ref[...] = (normed * gain_ref[2:3, :] + bias_ref[2:3, :]).astype(BF)

    return staged(
        "cross_forward",
        body,
        words,
        [*rest, tokens, *a, gains, biases, pool_keys, pool_values],
        [low_shape(rows, width)],
        [low_shape(width, width)] * 3
        + [wide_shape(rows, width)] * 2
        + [low_shape(rows, width)] * 3
        + [wide_shape(8 * quads, LANES)],
    )


def cross_backward(words, up, pieces, forward, pool_keys, pool_values, gains):
    rows, width = up.shape
    local = width // 4
    quads = width // LANES
    so, cq, co, one, two, _, q, o, lse = forward

    def body(word, ins, raws, sends, outs, scratch):
        up_ref, s0, s1, two_ref, gain_ref, s2, co_ref, q_ref, lse_ref, pk_ref, pv_ref, cq_ref, one_ref, so_ref = ins
        ga = sends
        one_grad_ref, g1_ref, g2_ref, dq_ref, dk_ref, dv_ref, small_ref = outs
        (d_ref,) = scratch
        t = word[0]
        up = s0[...].astype(F32) + s1[...].astype(F32) + s2[...].astype(F32)
        normed, inverse = norm_rows(two_ref[...])
        out_grad = up_ref[...].astype(F32)
        grads = out_grad + norm_back(up, normed, inverse, gain_ref[2:3, :])
        small_ref[...] = jnp.zeros(small_ref.shape, F32)
        small_ref[2:3, :] = jnp.sum(up * normed, 0, keepdims=True)
        small_ref[5:6, :] = jnp.sum(up, 0, keepdims=True)
        small_ref[6:7, :] = jnp.sum(out_grad, 0, keepdims=True)
        low = grads.astype(BF)
        g2_ref[...] = low
        d = nt(low, co_ref[...]).astype(BF).astype(F32)
        d_ref[...] = pltpu.roll(d, 1, 0).astype(BF)
        for g in range(quads):
            cols = slice(g * LANES, (g + 1) * LANES)
            parts = []
            for b in range(5):
                at = (b % 4) * SPAN
                bd = spread(q_ref[at : at + SPAN, cols], t, b)
                db = spread(d_ref[at : at + SPAN, cols], t, b)
                s = nt(pk_ref[b, :, cols], bd)
                p = jnp.exp(s - lse_ref[g * 8 + b : g * 8 + b + 1, :])
                dp = nt(pv_ref[b, :, cols], db)
                delta = jnp.sum(p * dp, 0, keepdims=True)
                ds = (p * (dp - delta)).astype(BF)
                dv_ref[b, :, cols] = nn(p.astype(BF), db).astype(BF)
                dk_ref[b, :, cols] = nn(ds, bd).astype(BF)
                parts.append(collect(tn(ds, pk_ref[b, :, cols]), t, b))
            dq_ref[:, cols] = (unroll_rows(parts) * 0.125).astype(BF)
        up = nn(dq_ref[...], cq_ref[...])
        normed, inverse = norm_rows(one_ref[...])
        small_ref[1:2, :] = jnp.sum(up * normed, 0, keepdims=True)
        small_ref[4:5, :] = jnp.sum(up, 0, keepdims=True)
        grads = grads + norm_back(up, normed, inverse, gain_ref[1:2, :])
        one_grad_ref[...] = grads
        low = grads.astype(BF)
        g1_ref[...] = low
        for p in range(4):
            ga[p][...] = nt(low, so_ref[p * local : (p + 1) * local, :]).astype(BF)

    out = staged(
        "cross_backward",
        body,
        words,
        [up, pieces[0], pieces[1], two, gains, pieces[2], co, q, lse, pool_keys, pool_values, cq, one, so],
        [low_shape(rows, local)] * 4,
        [wide_shape(rows, width)]
        + [low_shape(rows, width)] * 3
        + [jax.ShapeDtypeStruct(pool_keys.shape, BF)] * 2
        + [wide_shape(8, width)],
        [pltpu.VMEM((rows, width), BF)],
    )
    return out[:4], out[4:]


def cross_grads(words, a, o, dq, in_two, g1, g2):
    width, local = o.shape[1], a[0].shape[1]

    def body(word, ins, raws, sends, outs, scratch):
        a0, a1, a2, a3, g1_ref, o_ref, g2_ref, dq_ref, in_two_ref = ins
        for p, ap in enumerate((a0, a1, a2, a3)):
            at = (p % 2) * 3 * local
            sends[p // 2][at : at + local, :] = tn(ap[...], g1_ref[...]).astype(BF)
        for i, (left, right) in enumerate(((o_ref, g2_ref), (dq_ref, in_two_ref))):
            product = tn(left[...], right[...]).astype(BF)
            for p in range(4):
                at = ((p % 2) * 3 + 1 + i) * local
                sends[p // 2][at : at + local, :] = product[p * local : (p + 1) * local]

    return staged(
        "cross_grads", body, words, [*a, g1, o, g2, dq, in_two], [low_shape(6 * local, width)] * 2, []
    )


def pool_grads(words, neighbours, dk, dv):
    tokens, width = neighbours.shape[1:]
    local = width // 4

    def body(word, ins, raws, sends, outs, scratch):
        copies = fetch_sets(word[0], raws[0], *scratch)
        for copy in copies:
            copy.wait()
        for i, source in enumerate(ins):
            product = jnp.zeros((width, width), F32)
            for b in range(5):
                product = product + tn(source[b], scratch[0][b])
            product = product.astype(BF)
            for p in range(4):
                at = ((p % 2) * 2 + i) * local
                sends[p // 2][at : at + local, :] = product[p * local : (p + 1) * local]

    return staged(
        "pool_grads",
        body,
        words,
        [dk, dv],
        [low_shape(width, width)] * 2,
        [],
        [pltpu.VMEM((5, tokens, width), BF), pltpu.SemaphoreType.DMA((5,))],
        raw=[neighbours],
    )


def sets_grads(words, dk, dv, k, v):
    tokens, width = dk.shape[1:]

    def body(word, ins, raws, sends, outs, scratch):
        dk_ref, dv_ref, k_ref, v_ref = ins
        for b in range(5):
            product = (nn(dk_ref[b], k_ref[...]) + nn(dv_ref[b], v_ref[...])).astype(BF)
            if b == 0:
                sends[0][...] = product
            else:
                sends[1][b - 1] = product

    return staged(
        "sets_grads", body, words, [dk, dv, k, v], [low_shape(tokens, width), low_shape(4, tokens, width)], []
    )


def halved(words, bit, terms):
    rows, width = terms[0].shape
    half = rows // 2
    if half % 8:
        place = words[2] // bit % 2
        return [
            sum(lax.dynamic_slice_in_dim(term, which * half, half, 0).astype(F32) for term in terms).astype(BF)
            for which in (1 - place, place)
        ]

    def body(word, ins, raws, sends, outs, scratch):
        place = (word[2] // bit) % 2
        for which, target in zip((1 - place, place), sends):
            at = pl.ds(pl.multiple_of(which * half, half), half)
            total = ins[0][at, :].astype(F32)
            for term in ins[1:]:
                total = total + term[at, :].astype(F32)
            target[...] = total.astype(BF)

    return staged("halved", body, words, terms, [low_shape(half, width)] * 2, [], limit=8)


def doubled(words, bit, mine, other, cuts=None):
    half, width = mine.shape
    if half % 8:
        both = jnp.where(
            words[2] // bit % 2 == 0, jnp.concatenate([mine, other], 0), jnp.concatenate([other, mine], 0)
        )
        if cuts is None:
            return [both]
        return jnp.split(both.astype(F32), [sum(cuts[:i]) for i in range(1, len(cuts))], 0)

    def body(word, ins, raws, sends, outs, scratch):
        place = (word[2] // bit) % 2
        target = sends[0] if cuts is None else scratch[0]
        target[pl.ds(pl.multiple_of(place * half, half), half), :] = ins[0][...]
        target[pl.ds(pl.multiple_of((1 - place) * half, half), half), :] = ins[1][...]
        if cuts is not None:
            at = 0
            for result, count in zip(sends, cuts):
                result[...] = target[at : at + count, :].astype(F32)
                at += count

    shapes = [low_shape(2 * half, width)] if cuts is None else [wide_shape(count, width) for count in cuts]
    scratch = [] if cuts is None else [pltpu.VMEM((2 * half, width), BF)]
    return staged("doubled", body, words, [mine, other], shapes, [], scratch, limit=8)


def total(words, left, right):
    def body(word, ins, raws, sends, outs, scratch):
        sends[0][...] = (ins[0][...].astype(F32) + ins[1][...].astype(F32)).astype(BF)

    return staged("total", body, words, [left, right], [low_shape(*left.shape)], [], limit=4)[0]


def mlp_half(words, x0, x1, g0, g1, w_in, bias, w_out):
    rows, width = x0.shape
    units = w_in.shape[1]
    scale = 0.7978845608028654

    def body(word, ins, raws, sends, outs, scratch):
        x0, x1, w_in_ref, bias_ref, g0, g1, w_out_ref = ins
        keep_ref, send_ref = sends
        hidden_ref, pre_ref, sum_ref = outs
        sum_ref[...] = jnp.zeros(sum_ref.shape, F32)
        for i, (x, g, part) in enumerate(((x1, g1, send_ref), (x0, g0, keep_ref))):
            at = (1 - i) * rows
            v = nn(x[...], w_in_ref[...]) + bias_ref[0:1, :]
            square = v * v
            th = jnp.tanh(scale * v * (1.0 + 0.044715 * square))
            hidden_ref[at : at + rows, :] = (0.5 * v * (1.0 + th)).astype(BF)
            slope = 0.5 * (1.0 + th) + 0.5 * scale * v * (1.0 - th * th) * (1.0 + 3 * 0.044715 * square)
            pre = (nt(g[...], w_out_ref[...]) * slope).astype(BF)
            pre_ref[at : at + rows, :] = pre
            sum_ref[0:1, :] += jnp.sum(pre.astype(F32), 0, keepdims=True)
            part[...] = nt(pre, w_in_ref[...]).astype(BF)

    return staged(
        "mlp_half",
        body,
        words,
        [x0, x1, w_in, bias, g0, g1, w_out],
        [low_shape(rows, width)] * 2,
        [low_shape(2 * rows, units)] * 2 + [wide_shape(8, units)],
    )


def mlp_out_grads(words, hidden, gs):
    rows, width = gs[0].shape
    units = hidden[0].shape[1]

    def body(word, ins, raws, sends, outs, scratch):
        h_near, h_far, g0, g1, g2, g3 = ins
        product = jnp.zeros((units, width), F32)
        for h, g, i in ((h_near, g0, 0), (h_near, g1, 1), (h_far, g2, 0), (h_far, g3, 1)):
            product = product + tn(h[i * rows : (i + 1) * rows, :], g[...])
        sends[0][...] = product.astype(BF)

    return staged("mlp_out_grads", body, words, [*hidden, *gs], [low_shape(units, width)], [])[0]


def mlp_in_grads(words, pre, xs):
    rows, width = xs[0].shape
    units = pre[0].shape[1]

    def body(word, ins, raws, sends, outs, scratch):
        p_near, p_far, x0, x1, x2, x3 = ins
        product = jnp.zeros((width, units), F32)
        for p, x, i in ((p_near, x0, 0), (p_near, x1, 1), (p_far, x2, 0), (p_far, x3, 1)):
            product = product + tn(x[...], p[i * rows : (i + 1) * rows, :])
        sends[0][...] = product.astype(BF)

    return staged("mlp_in_grads", body, words, [*pre, *xs], [low_shape(width, units)], [])[0]


def mlp_branch(words, hidden, w_out):
    rows, width = hidden[0].shape[0] // 2, w_out.shape[1]

    def body(word, ins, raws, sends, outs, scratch):
        w_out_ref, h_near, h_far = ins
        for p, (h, i) in enumerate(((h_near, 0), (h_near, 1), (h_far, 0), (h_far, 1))):
            sends[p][...] = nn(h[i * rows : (i + 1) * rows, :], w_out_ref[...]).astype(BF)

    return staged("mlp_branch", body, words, [w_out, *hidden], [low_shape(rows, width)] * 4, [])


def swap(value, axis, bit, size):
    return lax.ppermute(value, axis, [(i, i ^ bit) for i in range(size)])


def core_swap(value):
    return swap(value, "tensor", 1, 4)


def x_swap(value):
    return swap(value, "tensor", 2, 4)


def after(value, *others):
    return lax.optimization_barrier((value, *others))[0]


def add(*terms):
    return sum(term.astype(F32) for term in terms)


class Order:
    def __init__(self, last):
        self.last = last

    def tie(self, value):
        return after(value, self.last)

    def sent(self, value):
        self.last = value
        return value


def halving(order, words, terms, bits, size, cuts):
    for bit in bits:
        send, keep = halved(words, bit, terms[:-1] + [order.tie(terms[-1])])
        terms = [keep, swap(order.sent(send), "dp", bit, size)]
        yield None
    pack = total(words, terms[0], order.tie(terms[1]))
    for bit in reversed(bits):
        got = swap(order.sent(pack), "dp", bit, size)
        yield None
        results = doubled(words, bit, pack, order.tie(got), cuts if bit == bits[0] else None)
        pack = results[0]
    order.sent(pack)
    yield results


def summing(order, value, bits, size):
    rows = value[:-1]
    for bit in (1, 2):
        got = swap(order.sent(order.tie(rows)), "tensor", bit, 4)
        yield None
        rows = rows + got
    value = jnp.concatenate([rows, value[-1:]], 0)
    for bit in bits:
        got = swap(order.sent(order.tie(value)), "dp", bit, size)
        yield None
        value = value + got
    yield value


def rope_tables(length):
    half = HEAD_DIM // 2
    places = jnp.arange(length).astype(F32)
    frequency = 10000.0 ** (-(jnp.arange(half).astype(F32) * 2.0 / HEAD_DIM))
    angles = places[:, None] * frequency[None, :]
    cosine, sine = jnp.cos(angles), jnp.sin(angles)
    return jnp.concatenate([cosine] * 4, 1), jnp.concatenate([-sine, sine] * 2, 1)


def spans(count, size):
    shares = [size / 2**i for i in range(1, count + 1)]
    return [4.0 + share for share in shares] + [4.0 + share for share in reversed(shares)]


def make_local(dp_size):
    bits = []
    bit = 1
    while bit < dp_size:
        bits.append(bit)
        bit *= 2
    turned = bits[1:2] + bits[0:1] + bits[2:]

    def local(
        tokens,
        out_grad,
        segments,
        neighbours,
        norm_gains,
        norm_biases,
        self_qkv,
        self_out,
        cross_q,
        cross_kv,
        cross_out,
        mlp_in,
        mlp_in_bias,
        mlp_out,
        mlp_out_bias,
    ):
        place = lax.axis_index("dp")
        words = jnp.stack([lax.axis_index("tensor"), place % 2, place]).astype(jnp.int32)
        parity = place % 2
        rows, width = tokens.shape
        seq_len = 4 * rows
        local_width = self_out.shape[0]
        heads = local_width // HEAD_DIM
        gains = norm_gains.astype(F32)
        biases = norm_biases.astype(F32)
        segment = segments[0]
        qkv_rows = self_qkv.transpose(0, 2, 1)
        kv_own = cross_kv.transpose(0, 2, 1)

        tok_far = x_swap(tokens)
        tok_near = core_swap(tokens)
        rest_own = jnp.stack([self_out, cross_q.T, cross_out])
        kv_send = lax.dynamic_slice_in_dim(kv_own, parity, 1, 0)
        rest_send = lax.dynamic_slice_in_dim(rest_own, parity * (local_width // 2), local_width // 2, 1)
        cosine, sine = rope_tables(seq_len)
        start = jnp.sum((segment[:, None] < segment[None, :]).astype(jnp.int32), 0)
        start = jnp.broadcast_to(start[None], (8, seq_len))
        bias_row = jnp.broadcast_to(mlp_in_bias.astype(F32)[None], (8, mlp_in_bias.shape[0]))
        tok_far, kv_send, rest_send, cosine, sine, start, gains, biases, bias_row, words, tok_near = (
            lax.optimization_barrier(
                (tok_far, kv_send, rest_send, cosine, sine, start, gains, biases, bias_row, words, tok_near)
            )
        )
        kv_x = x_swap(kv_send)
        rest_x = x_swap(rest_send)
        tok_both = core_swap(tok_far)
        kv_core = core_swap(after(kv_own, tok_far))
        rest_core = core_swap(after(rest_own, tok_far))
        up_near = core_swap(after(out_grad, tok_far))

        sends, saved = self_forward(
            words, (tokens, tok_near, tok_far, tok_both), gains, biases, qkv_rows, cosine, sine, start, heads
        )
        attended = [sends[0]] + [swap(sends[j], "tensor", j, 4) for j in (2, 1, 3)]
        kv_x, kv_core, rest_core, up_near, rest_x = (
            after(item, sends[0]) for item in (kv_x, kv_core, rest_core, up_near, rest_x)
        )
        kv_y = swap(kv_x, "dp", 1, dp_size)
        rest_x = after(rest_x, kv_x)
        rest_y = swap(rest_x, "dp", 1, dp_size)
        up_far = x_swap(after(out_grad, rest_x))
        attended[1:] = [after(item, rest_x) for item in attended[1:]]
        kv_far = joined(words, [kv_x[0], after(kv_y, rest_x, *attended[1:])[0]])
        kv_both = core_swap(kv_far)
        pool_keys, pool_values, k_full, v_full = pool(words, neighbours, kv_own, kv_core, kv_far, kv_both)
        rest_far = joined(words, [rest_x, after(rest_y, pool_keys)])
        rest_both = core_swap(rest_far)
        up_far = after(up_far, rest_far)
        up_both = core_swap(up_far)

        in_three, *forward = cross_forward(
            words, tokens, attended, (rest_own, rest_core, rest_far, rest_both), pool_keys, pool_values, gains, biases
        )
        x_far = x_swap(in_three)
        x_near = core_swap(in_three)
        up_both = after(up_both, in_three)
        keep_near, send_near, h_near, p_near, sum_near = mlp_half(
            words, in_three, x_near, out_grad, up_near, mlp_in, bias_row, mlp_out
        )
        got_near = core_swap(send_near)
        x_far = after(x_far, send_near)
        x_both = core_swap(x_far)
        keep_far, send_far, h_far, p_far, sum_far = mlp_half(
            words, x_far, x_both, up_far, up_both, mlp_in, bias_row, mlp_out
        )
        far = total(words, keep_far, core_swap(send_far))
        h_near = after(h_near, far)
        far = x_swap(far)
        grad_mlp_out = mlp_out_grads(words, (h_near, h_far), (out_grad, up_near, up_far, up_both))
        order = Order(grad_mlp_out)
        chain_m_out = halving(order, words, [grad_mlp_out], bits, dp_size, [grad_mlp_out.shape[0]])
        next(chain_m_out)
        grad_mlp_in = mlp_in_grads(words, (order.tie(p_near), p_far), (in_three, x_near, x_far, x_both))
        chain_m_in = halving(order, words, [grad_mlp_in], turned, dp_size, [grad_mlp_in.shape[0]])
        next(chain_m_in)
        branch = mlp_branch(words, (order.tie(h_near), h_far), mlp_out)
        far = after(far, branch[0])

        ga, backs = cross_backward(
            words, out_grad, (keep_near, got_near, far), forward, pool_keys, pool_values, gains
        )
        in_two, o_two, two = forward[5], forward[7], forward[4]
        one_grad, g1, g2, dq_two, dk_two, dv_two, small = backs
        ups = [ga[0]] + [swap(ga[p], "tensor", j, 4) for p, j in ((2, 1), (1, 2), (3, 3))]
        keep_one, send_one = cross_grads(words, attended, o_two, dq_two, in_two, g1, g2)
        got_one = core_swap(send_one)
        order.sent(send_one)
        next(chain_m_out)
        next(chain_m_in)
        keep_two, send_two = pool_grads(words, neighbours, order.tie(dk_two), dv_two)
        got_two = core_swap(send_two)
        one_rows, two_rows = 3 * local_width, 2 * local_width
        far_one = plus(words, keep_one, after(got_one, send_two))
        ups[1:] = [after(item, far_one) for item in ups[1:]]
        far_one = x_swap(far_one)
        pack_qkv, grad_one = self_backward(words, ups, saved, cosine, sine, start, heads)
        order.sent(pack_qkv)

        results = {}

        def chain_two():
            far = x_swap(order.sent(plus(words, keep_two, order.tie(got_two))))
            yield None
            yield from halving(
                order, words, [keep_two[:two_rows], got_two[:two_rows], far], bits, dp_size, [local_width] * 2
            )

        def chain_rows():
            keep, send = norm_one(words, order.tie(grad_one), qkv_rows)
            got = core_swap(order.sent(send))
            yield None
            far = x_swap(order.sent(plus(words, keep, order.tie(got))))
            yield None
            grad = add(keep[:rows], got[:rows], order.tie(far))
            normed, inverse = norm_rows(tokens.astype(F32))
            results["tokens_grad"] = (one_grad + norm_back(grad, normed, inverse, gains[0])).astype(BF)
            own = jnp.stack([jnp.sum(grad * normed, 0), jnp.sum(grad, 0)])
            bias_in_part = sum_near[0] + sum_far[0]
            value = jnp.concatenate([own[:1], small[1:3], own[1:], small[4:7], bias_in_part[None]], 0)
            yield from summing(order, value, bits, dp_size)

        def chain_sets():
            before, mine = sets_grads(words, order.tie(dk_two), dv_two, k_full, v_full)
            back = lax.ppermute(order.sent(before), "tensor", [(i + 1, i) for i in range(3)])
            yield None
            last = add(mine[3], order.tie(back)).astype(BF)
            yield jnp.concatenate([mine[:3], last[None]], 0)

        def chain_output():
            near = core_swap(order.sent(order.tie(branch[1])))
            got = core_swap(order.sent(order.tie(branch[3])))
            yield None
            far = x_swap(order.sent(total(words, branch[2], order.tie(got))))
            yield None
            yield (two + add(branch[0], near, order.tie(far)) + mlp_out_bias.astype(F32)).astype(BF)

        count = len(bits)
        chain_qkv = halving(order, words, [pack_qkv], bits, dp_size, [local_width] * 3)
        chain_one = halving(
            order, words, [keep_one[:one_rows], got_one[:one_rows], far_one], turned, dp_size, [local_width] * 3
        )
        plans = {
            "qkv": (chain_qkv, 0.0, spans(count, 20.0)),
            "m_out": (chain_m_out, 1.0, spans(count, 27.0)[2:]),
            "m_in": (chain_m_in, 1.1, spans(count, 27.0)[2:]),
            "rows": (chain_rows(), 4.0, [4.0, 24.0] + [5.0] * (2 + count)),
            "one": (chain_one, 10.0, spans(count, 20.0)),
            "two": (chain_two(), 9.0, [23.0] + spans(count, 13.0)),
            "sets": (chain_sets(), 12.0, [20.0]),
            "output": (chain_output(), 34.0, [6.0, 11.0]),
        }
        events = []
        for name, (_, moment, lengths) in plans.items():
            events.append((moment, name))
            for length in lengths:
                moment += length
                events.append((moment, name))
        for _, name in sorted(events):
            results[name] = next(plans[name][0])

        sum_one = results["one"]
        sums = results["rows"]
        return (
            results["output"],
            results["tokens_grad"],
            results["sets"],
            sums[:3],
            sums[3:6],
            jnp.stack(results["qkv"]).transpose(0, 2, 1),
            sum_one[0],
            sum_one[2].T,
            jnp.stack(results["two"]).transpose(0, 2, 1),
            sum_one[1],
            results["m_in"][0],
            sums[7],
            results["m_out"][0],
            sums[6],
        )

    return local


def solution(mesh):
    rows = P(("dp", "tensor"), None)
    in_specs = (
        rows,
        rows,
        P("dp", None),
        P("dp", None, None),
        P(),
        P(),
        P(None, None, "tensor"),
        P("tensor", None),
        P(None, "tensor"),
        P(None, None, "tensor"),
        P("tensor", None),
        P(None, "tensor"),
        P("tensor"),
        P("tensor", None),
        P(),
    )
    out_specs = (
        rows,
        rows,
        P(("dp", "tensor"), None, None),
        P(),
        P(),
        P(None, None, "tensor"),
        P("tensor", None),
        P(None, "tensor"),
        P(None, None, "tensor"),
        P("tensor", None),
        P(None, "tensor"),
        P("tensor"),
        P("tensor", None),
        P(),
    )
    return jax.shard_map(
        make_local(mesh.shape["dp"]),
        mesh=mesh,
        in_specs=in_specs,
        out_specs=out_specs,
        check_vma=False,
    )
```

```python
import functools

import jax
import jax.numpy as jnp
from jax import lax
from jax.experimental import pallas as pl
from jax.experimental.pallas import tpu as pltpu
from jax.sharding import PartitionSpec as P

HEAD_DIM = 64
SPAN = 64
EPS = 1e-05
MASKED = -1e30
LANES = 256
QUAD = LANES // HEAD_DIM
COST = {
    "self_forward": 80,
    "pool": 66,
    "cross_forward": 40,
    "mlp_half": 34,
    "mlp_out_grads": 26,
    "mlp_in_grads": 22,
    "mlp_branch": 21,
    "cross_backward": 85,
    "cross_grads": 18,
    "pool_grads": 0.8,
    "self_backward": 103,
    "norm_one": 0.8,
    "sets_grads": 0.8,
    "slot": 60,
}
BF = jnp.bfloat16
F32 = jnp.float32


def nn(left, right):
    return jnp.dot(left, right, preferred_element_type=F32)


def nt(left, right):
    return lax.dot_general(left, right, (((1,), (1,)), ((), ())), preferred_element_type=F32)


def tn(left, right):
    return lax.dot_general(left, right, (((0,), (0,)), ((), ())), preferred_element_type=F32)


def norm_rows(values):
    center = values - jnp.mean(values, -1, keepdims=True)
    inverse = lax.rsqrt(jnp.mean(center * center, -1, keepdims=True) + EPS)
    return center * inverse, inverse


def norm_back(upstream, normed, inverse, gain):
    scaled = upstream * gain
    return inverse * (
        scaled
        - jnp.mean(scaled, -1, keepdims=True)
        - normed * jnp.mean(scaled * normed, -1, keepdims=True)
    )


def lane_head(shape):
    return lax.broadcasted_iota(jnp.int32, shape, len(shape) - 1) // HEAD_DIM


def half_swap(values):
    half = HEAD_DIM // 2
    width = values.shape[1]
    lane = lax.broadcasted_iota(jnp.int32, values.shape, 1)
    return jnp.where(
        lane % HEAD_DIM < half,
        pltpu.roll(values, width - half, 1),
        pltpu.roll(values, half, 1),
    )


def staged(name, body, words, arrays, near, far, scratch=(), raw=(), limit=16, cost=None):
    n, r, p, f = len(arrays), len(raw), len(near), len(far)

    def kernel(word, *refs):
        cuts = [n, n + r, n + r + p, n + r + p + f]
        body(word, *[refs[a:b] for a, b in zip([0] + cuts, cuts + [len(refs)])])

    hbm, vmem = pl.BlockSpec(memory_space=pltpu.HBM), pl.BlockSpec(memory_space=pltpu.VMEM)
    return pl.pallas_call(
        kernel,
        out_shape=list(near) + list(far),
        in_specs=[pl.BlockSpec(memory_space=pltpu.SMEM)] + [vmem] * n + [hbm] * r,
        out_specs=[vmem] * (p + f),
        scratch_shapes=list(scratch),
        compiler_params=pltpu.CompilerParams(vmem_limit_bytes=limit * 2**20),
        cost_estimate=pl.CostEstimate(flops=int(COST.get(cost or name, 0.8) * 10**9), bytes_accessed=10**4, transcendentals=0),
        name=name,
    )(words, *arrays, *raw)


def plus(words, left, rights):
    rows, width = left.shape
    half = rows // 2

    def body(word, ins, raws, sends, outs, scratch):
        at = -half
        for right in ins[1:]:
            count = right.shape[0]
            begin = max(-at, 0)
            if begin < count:
                to = slice(at + begin, at + count)
                share = ins[0][half + at + begin : half + at + count, :].astype(F32) + right[begin:count, :].astype(F32)
                sends[0][to, :] = share.astype(BF)
            at += count

    return staged("plus", body, words, [left, *rights], [low_shape(half, width)], [], limit=6)[0]


def low_shape(*shape):
    return jax.ShapeDtypeStruct(shape, BF)


def wide_shape(*shape):
    return jax.ShapeDtypeStruct(shape, F32)


def block_mask(start_ref, i, rows):
    keys = (i + 1) * rows
    row = lax.broadcasted_iota(jnp.int32, (keys, rows), 0)
    place = lax.broadcasted_iota(jnp.int32, (keys, rows), 1) + i * rows
    start = start_ref[0:1, i * rows : (i + 1) * rows]
    return jnp.where((row >= start) & (row <= place), 0.0, MASKED)


def tables(cos_ref, sin_ref, part):
    return jnp.concatenate([cos_ref[part, :]] * 2, 1), jnp.concatenate([sin_ref[part, :]] * 2, 1)


def self_forward(words, toks, gains, biases, weights, cosine, sine, start, heads):
    rows, width = toks[0].shape
    total = 4 * rows
    local = heads * HEAD_DIM

    def body(word, ins, raws, sends, outs, scratch):
        tok0, gain_ref, bias_ref, w_ref, tok1, tok2, tok3, cos_ref, sin_ref, start_ref = ins
        x_ref, q_ref, k_ref, v_ref, lse_ref, o_ref = outs
        mask_ref, pad_ref = scratch
        t = word[0]
        for c in range(3):
            pad_ref[c, 0:local, :] = w_ref[c]
            pad_ref[c, local:, :] = jnp.zeros((LANES - local, width), BF)
        for j, tok in enumerate((tok0, tok1, tok2, tok3)):
            normed, _ = norm_rows(tok[...].astype(F32))
            x_ref[pl.ds(pl.multiple_of((t ^ j) * rows, rows), rows), :] = (
                normed * gain_ref[0:1, :] + bias_ref[0:1, :]
            ).astype(BF)
        for i in range(4):
            part = pl.ds(i * rows, rows)
            x = x_ref[part, :]
            cosines, sines = tables(cos_ref, sin_ref, part)
            q = nt(x, pad_ref[0])
            q_ref[part, :] = ((q * cosines + half_swap(q) * sines) * 0.125).astype(BF)
            k = nt(x, pad_ref[1])
            k_ref[part, :] = (k * cosines + half_swap(k) * sines).astype(BF)
            v_ref[part, :] = nt(x, pad_ref[2]).astype(BF)
        lane = lane_head((1, LANES))
        lse_ref[...] = jnp.zeros(lse_ref.shape, F32)
        for i in range(4):
            part = pl.ds(i * rows, rows)
            keys = (i + 1) * rows
            mask_ref[0:keys, :] = block_mask(start_ref, i, rows)
            out = jnp.zeros((rows, LANES), F32)
            for h in range(heads):
                qh = jnp.where(lane == h, q_ref[part, :], jnp.zeros((), BF))
                s = nt(k_ref[0:keys, :], qh) + mask_ref[0:keys, :]
                top = jnp.max(s, 0, keepdims=True)
                p = jnp.exp(s - top)
                norm = jnp.sum(p, 0, keepdims=True)
                lse_ref[h : h + 1, i * rows : (i + 1) * rows] = top + jnp.log(norm)
                low = (p * (1.0 / norm)).astype(BF)
                out = jnp.where(lane == h, tn(low, v_ref[0:keys, :]), out)
            o_ref[part, :] = out.astype(BF)
        for j, a in enumerate(sends):
            a[...] = o_ref[pl.ds(pl.multiple_of((t ^ j) * rows, rows), rows), 0:local]

    out = staged(
        "self_forward",
        body,
        words,
        [toks[0], gains, biases, weights, toks[1], toks[2], toks[3], cosine, sine, start],
        [low_shape(rows, local)] * 4,
        [low_shape(total, width)] + [low_shape(total, LANES)] * 3 + [wide_shape(8, total), low_shape(total, LANES)],
        [pltpu.VMEM((total, rows), F32), pltpu.VMEM((3, LANES, width), BF)],
    )
    return out[:4], out[4:]


def self_backward(words, ups, saved, cosine, sine, start, heads):
    total, width = saved[0].shape
    rows = total // 4
    local = heads * HEAD_DIM

    def body(word, ins, raws, sends, outs, scratch):
        d0, d1, d2, d3, o_ref, q_ref, k_ref, start_ref, v_ref, lse_ref, cos_ref, sin_ref, x_ref = ins
        (pack_ref,) = sends
        (grad_ref,) = outs
        d_ref, mask_ref, dk_ref, dv_ref, delta_ref = scratch
        t = word[0]
        d_ref[...] = jnp.zeros_like(d_ref)
        for j, d in enumerate((d0, d1, d2, d3)):
            d_ref[pl.ds(pl.multiple_of((t ^ j) * rows, rows), rows), 0:local] = d[...]
        pick = (lax.broadcasted_iota(jnp.int32, (8, LANES), 0) == lane_head((8, LANES))).astype(F32)
        delta_ref[...] = lax.dot_general(
            pick,
            d_ref[...].astype(F32) * o_ref[...].astype(F32),
            (((1,), (1,)), ((), ())),
            precision=lax.Precision.HIGHEST,
            preferred_element_type=F32,
        )
        dk_ref[...] = jnp.zeros_like(dk_ref)
        dv_ref[...] = jnp.zeros_like(dv_ref)
        lane = lane_head((1, LANES))
        zero = jnp.zeros((), BF)
        for i in range(4):
            part = pl.ds(i * rows, rows)
            keys = (i + 1) * rows
            mask_ref[0:keys, :] = block_mask(start_ref, i, rows)
            dq = jnp.zeros((rows, LANES), F32)
            for h in range(heads):
                qh = jnp.where(lane == h, q_ref[part, :], zero)
                dh = jnp.where(lane == h, d_ref[part, :], zero)
                lse = lse_ref[h : h + 1, i * rows : (i + 1) * rows]
                delta = delta_ref[h : h + 1, i * rows : (i + 1) * rows]
                s = nt(k_ref[0:keys, :], qh) + mask_ref[0:keys, :]
                p = jnp.exp(s - lse)
                dp = nt(v_ref[0:keys, :], dh)
                ds = (p * (dp - delta)).astype(BF)
                dv_ref[0:keys, :] += nn(p.astype(BF), dh)
                dk_ref[0:keys, :] += nn(ds, qh)
                dq = jnp.where(lane == h, tn(ds, k_ref[0:keys, :]), dq)
            cosines, sines = tables(cos_ref, sin_ref, part)
            dq = dq * 0.125
            grad_ref[part, 0:LANES] = (dq * cosines - half_swap(dq) * sines).astype(BF)
        for i in range(4):
            part = pl.ds(i * rows, rows)
            cosines, sines = tables(cos_ref, sin_ref, part)
            dk = dk_ref[part, :]
            grad_ref[part, LANES : 2 * LANES] = (dk * cosines - half_swap(dk) * sines).astype(BF)
            grad_ref[part, 2 * LANES : 3 * LANES] = dv_ref[part, :].astype(BF)
        for c in range(3):
            product = tn(grad_ref[:, c * LANES : (c + 1) * LANES], x_ref[...])
            pack_ref[c * local : (c + 1) * local, :] = product[0:local].astype(BF)

    x, q, k, v, lse, o = saved
    return staged(
        "self_backward",
        body,
        words,
        [*ups, o, q, k, start, v, lse, cosine, sine, x],
        [low_shape(3 * local, width)],
        [low_shape(total, 3 * LANES)],
        [
            pltpu.VMEM((total, LANES), BF),
            pltpu.VMEM((total, rows), F32),
            pltpu.VMEM((total, LANES), F32),
            pltpu.VMEM((total, LANES), F32),
            pltpu.VMEM((8, total), F32),
        ],
    )


def norm_one(words, grad, weights, toks, small, sums, branch):
    rows, local, width = grad.shape[0] // 4, weights.shape[1], weights.shape[2]

    def body(word, ins, raws, sends, outs, scratch):
        grad_ref, w_ref, small_ref, near_ref, far_ref = ins[:5]
        gain = jnp.zeros((1, width), F32)
        bias = jnp.zeros((1, width), F32)
        for j in range(4):
            at = pl.ds(pl.multiple_of((word[0] ^ j) * rows, rows), rows)
            share = jnp.zeros((rows, width), F32)
            for c in range(3):
                share = share + nn(grad_ref[at, c * LANES : c * LANES + local], w_ref[c])
            normed, _ = norm_rows(ins[5 + j][...].astype(F32))
            gain = gain + jnp.sum(share * normed, 0, keepdims=True)
            bias = bias + jnp.sum(share, 0, keepdims=True)
            target = sends[j % 2]
            at = (j // 2) * 2 * rows
            target[at : at + rows, :] = share.astype(BF)
            target[at + rows : at + 2 * rows, :] = ins[9 + (0, 1, 2, 3)[j]][...]
        sends[2][...] = small_ref[...]
        sends[2][0:1, :] = gain
        sends[2][3:4, :] = bias
        sends[2][7:8, :] = near_ref[0:1, :] + far_ref[0:1, :]

    return staged(
        "norm_one",
        body,
        words,
        [grad, weights, small, *sums, *toks, *branch],
        [low_shape(4 * rows, width)] * 2 + [wide_shape(8, width)],
        [],
    )


def small_total(words, left, right):
    def body(word, ins, raws, sends, outs, scratch):
        row = lax.broadcasted_iota(jnp.int32, left.shape, 0)
        sends[0][...] = ins[0][...] + jnp.where(row < 7, ins[1][...], 0.0)

    return staged("small_total", body, words, [left, right], [wide_shape(*left.shape)], [], limit=4)[0]


def merged(words, keep, gots, far, small):
    rows, width = far.shape

    def body(word, ins, raws, sends, outs, scratch):
        keep_ref, far_ref, small_ref = ins[:3]
        at = 0
        for got in ins[3:]:
            part = slice(at, at + got.shape[0])
            share = keep_ref[part, :].astype(F32) + got[...].astype(F32) + far_ref[part, :].astype(F32)
            sends[0][part, :] = share.astype(BF)
            at += got.shape[0]
        sends[0][rows:, :] = jnp.zeros((64, width), BF)
        sends[0][rows : rows + 8, :] = small_ref[...].astype(BF)

    return staged("merged", body, words, [keep, far, small, *gots], [low_shape(rows + 64, width)], [], limit=8)[0]


def spread(values, t, block):
    shape = (LANES, LANES)
    tiled = jnp.concatenate([values] * QUAD, 0)
    row = lax.broadcasted_iota(jnp.int32, shape, 0)
    keep = (row // SPAN) == lane_head(shape)
    if block == 0:
        keep = keep & (row % SPAN > 0) & (t > 0)
    if block == 4:
        keep = keep & (row % SPAN == 0)
    return jnp.where(keep, tiled, jnp.zeros((), values.dtype))


def collect(values, t, block):
    shape = (SPAN, LANES)
    head = lane_head(shape)
    out = jnp.zeros(shape, values.dtype)
    for h in range(QUAD):
        out = jnp.where(head == h, values[h * SPAN : (h + 1) * SPAN], out)
    row = lax.broadcasted_iota(jnp.int32, shape, 0)
    if block == 0:
        out = jnp.where((row > 0) & (t > 0), out, 0.0)
    if block == 4:
        out = jnp.where(row == 0, out, 0.0)
    return out


def unroll_rows(parts):
    return pltpu.roll(jnp.concatenate([parts[0] + parts[4]] + parts[1:4], 0), 4 * SPAN - 1, 0)


def fetch_sets(t, nb_ref, buffer_ref, sem_ref):
    copies = []
    for b in range(5):
        at = jnp.maximum(4 * t - 1 + b, 0)
        copies.append(pltpu.make_async_copy(nb_ref.at[at], buffer_ref.at[b], sem_ref.at[b]))
        copies[-1].start()
    return copies


def pool(words, neighbours, own, core, far, both):
    tokens, width = neighbours.shape[1:]
    local = own.shape[1]

    def body(word, ins, raws, sends, outs, scratch):
        own_ref, core_ref, far_x, far_y, both_x, both_y = ins
        pk_ref, pv_ref, k_ref, v_ref = outs
        copies = fetch_sets(word[0], raws[0], *scratch)
        for i, target in enumerate((k_ref, v_ref)):
            direct = word[1] == i
            target[0:local, :] = own_ref[i]
            target[local : 2 * local, :] = jnp.where(direct, far_x[0], far_y[0])
            target[2 * local : 3 * local, :] = core_ref[i]
            target[3 * local : 4 * local, :] = jnp.where(direct, both_x[0], both_y[0])
        for b in range(5):
            copies[b].wait()
            pk_ref[b] = nt(scratch[0][b], k_ref[...]).astype(BF)
            pv_ref[b] = nt(scratch[0][b], v_ref[...]).astype(BF)

    return staged(
        "pool",
        body,
        words,
        [own, core, *far, *both],
        [],
        [low_shape(5, tokens, width)] * 2 + [low_shape(width, width)] * 2,
        [pltpu.VMEM((5, tokens, width), BF), pltpu.SemaphoreType.DMA((5,))],
        raw=[neighbours],
    )


def cross_forward(words, tokens, a, rest, pool_keys, pool_values, gains, biases):
    rows, width = tokens.shape
    local = a[0].shape[1]
    quads = width // LANES

    def body(word, ins, raws, sends, outs, scratch):
        own_ref, core_ref, far_x, far_y, both_x, both_y, tok_ref, a0, a1, a2, a3, gain_ref, bias_ref, pk_ref, pv_ref = ins
        (in_three_ref,) = sends
        so_ref, cq_ref, co_ref, one_ref, two_ref, in_two_ref, q_ref, o_ref, lse_ref = outs
        t = word[0]
        half = local // 2
        for i, target in enumerate((so_ref, cq_ref, co_ref)):
            target[0:local, :] = own_ref[i]
            target[2 * local : 3 * local, :] = core_ref[i]
            for h in range(2):
                direct = word[1] == h
                at = local + h * half
                target[at : at + half, :] = jnp.where(direct, far_x[i], far_y[i])
                at = 3 * local + h * half
                target[at : at + half, :] = jnp.where(direct, both_x[i], both_y[i])
        resid = tok_ref[...].astype(F32)
        for p, ap in enumerate((a0, a1, a2, a3)):
            resid = resid + nn(ap[...], so_ref[p * local : (p + 1) * local, :])
        one_ref[...] = resid
        normed, _ = norm_rows(resid)
        low = (normed * gain_ref[1:2, :] + bias_ref[1:2, :]).astype(BF)
        in_two_ref[...] = low
        q = nt(low, cq_ref[...]).astype(BF).astype(F32) * 0.125
        q_ref[...] = pltpu.roll(q, 1, 0).astype(BF)
        lse_ref[...] = jnp.zeros(lse_ref.shape, F32)
        for g in range(quads):
            cols = slice(g * LANES, (g + 1) * LANES)
            parts = []
            for b in range(5):
                at = (b % 4) * SPAN
                s = nt(pk_ref[b, :, cols], spread(q_ref[at : at + SPAN, cols], t, b))
                top = jnp.max(s, 0, keepdims=True)
                p = jnp.exp(s - top)
                norm = jnp.sum(p, 0, keepdims=True)
                lse_ref[g * 8 + b : g * 8 + b + 1, :] = top + jnp.log(norm)
                low = (p * (1.0 / norm)).astype(BF)
                parts.append(collect(tn(low, pv_ref[b, :, cols]), t, b))
            o_ref[:, cols] = unroll_rows(parts).astype(BF)
        resid = resid + nn(o_ref[...], co_ref[...])
        two_ref[...] = resid
        normed, _ = norm_rows(resid)
        in_three_ref[...] = (normed * gain_ref[2:3, :] + bias_ref[2:3, :]).astype(BF)

    return staged(
        "cross_forward",
        body,
        words,
        [*rest, tokens, *a, gains, biases, pool_keys, pool_values],
        [low_shape(rows, width)],
        [low_shape(width, width)] * 3
        + [wide_shape(rows, width)] * 2
        + [low_shape(rows, width)] * 3
        + [wide_shape(8 * quads, LANES)],
    )


def cross_backward(words, up, pieces, forward, pool_keys, pool_values, gains):
    rows, width = up.shape
    local = width // 4
    quads = width // LANES
    so, cq, co, one, two, _, q, o, lse = forward

    def body(word, ins, raws, sends, outs, scratch):
        up_ref, s0, s1, two_ref, gain_ref, s2, co_ref, q_ref, lse_ref, pk_ref, pv_ref, cq_ref, one_ref, so_ref = ins
        ga = sends
        one_grad_ref, g1_ref, g2_ref, dq_ref, dk_ref, dv_ref, small_ref = outs
        (d_ref,) = scratch
        t = word[0]
        up = s0[...].astype(F32) + s1[...].astype(F32) + s2[...].astype(F32)
        normed, inverse = norm_rows(two_ref[...])
        out_grad = up_ref[...].astype(F32)
        grads = out_grad + norm_back(up, normed, inverse, gain_ref[2:3, :])
        small_ref[...] = jnp.zeros(small_ref.shape, F32)
        small_ref[2:3, :] = jnp.sum(up * normed, 0, keepdims=True)
        small_ref[5:6, :] = jnp.sum(up, 0, keepdims=True)
        small_ref[6:7, :] = jnp.sum(out_grad, 0, keepdims=True)
        low = grads.astype(BF)
        g2_ref[...] = low
        d = nt(low, co_ref[...]).astype(BF).astype(F32)
        d_ref[...] = pltpu.roll(d, 1, 0).astype(BF)
        for g in range(quads):
            cols = slice(g * LANES, (g + 1) * LANES)
            parts = []
            for b in range(5):
                at = (b % 4) * SPAN
                bd = spread(q_ref[at : at + SPAN, cols], t, b)
                db = spread(d_ref[at : at + SPAN, cols], t, b)
                s = nt(pk_ref[b, :, cols], bd)
                p = jnp.exp(s - lse_ref[g * 8 + b : g * 8 + b + 1, :])
                dp = nt(pv_ref[b, :, cols], db)
                delta = jnp.sum(p * dp, 0, keepdims=True)
                ds = (p * (dp - delta)).astype(BF)
                dv_ref[b, :, cols] = nn(p.astype(BF), db).astype(BF)
                dk_ref[b, :, cols] = nn(ds, bd).astype(BF)
                parts.append(collect(tn(ds, pk_ref[b, :, cols]), t, b))
            dq_ref[:, cols] = (unroll_rows(parts) * 0.125).astype(BF)
        up = nn(dq_ref[...], cq_ref[...])
        normed, inverse = norm_rows(one_ref[...])
        small_ref[1:2, :] = jnp.sum(up * normed, 0, keepdims=True)
        small_ref[4:5, :] = jnp.sum(up, 0, keepdims=True)
        grads = grads + norm_back(up, normed, inverse, gain_ref[1:2, :])
        one_grad_ref[...] = grads
        low = grads.astype(BF)
        g1_ref[...] = low
        for p in range(4):
            ga[p][...] = nt(low, so_ref[p * local : (p + 1) * local, :]).astype(BF)

    out = staged(
        "cross_backward",
        body,
        words,
        [up, pieces[0], pieces[1], two, gains, pieces[2], co, q, lse, pool_keys, pool_values, cq, one, so],
        [low_shape(rows, local)] * 4,
        [wide_shape(rows, width)]
        + [low_shape(rows, width)] * 3
        + [jax.ShapeDtypeStruct(pool_keys.shape, BF)] * 2
        + [wide_shape(8, width)],
        [pltpu.VMEM((rows, width), BF)],
    )
    return out[:4], out[4:]


def cross_grads(words, a, o, dq, in_two, g1, g2):
    width, local = o.shape[1], a[0].shape[1]

    def body(word, ins, raws, sends, outs, scratch):
        a0, a1, a2, a3, g1_ref, o_ref, g2_ref, dq_ref, in_two_ref = ins
        for p, ap in enumerate((a0, a1, a2, a3)):
            at = (p % 2) * 3 * local
            sends[p // 2][at : at + local, :] = tn(ap[...], g1_ref[...]).astype(BF)
        for i, (left, right) in enumerate(((o_ref, g2_ref), (dq_ref, in_two_ref))):
            product = tn(left[...], right[...]).astype(BF)
            for p in range(4):
                at = ((p % 2) * 3 + 1 + i) * local
                sends[p // 2][at : at + local, :] = product[p * local : (p + 1) * local]

    return staged(
        "cross_grads", body, words, [*a, g1, o, g2, dq, in_two], [low_shape(6 * local, width)] * 2, []
    )


def pool_grads(words, neighbours, dk, dv):
    tokens, width = neighbours.shape[1:]
    local = width // 4

    def body(word, ins, raws, sends, outs, scratch):
        copies = fetch_sets(word[0], raws[0], *scratch)
        for copy in copies:
            copy.wait()
        for i, source in enumerate(ins):
            product = jnp.zeros((width, width), F32)
            for b in range(5):
                product = product + tn(source[b], scratch[0][b])
            product = product.astype(BF)
            for p in range(2):
                at = (2 * p + i) * local
                sends[0][at : at + local, :] = product[p * local : (p + 1) * local]
                sends[1 + 2 * p + i][...] = product[(2 + p) * local : (3 + p) * local]

    return staged(
        "pool_grads",
        body,
        words,
        [dk, dv],
        [low_shape(width, width)] + [low_shape(local, width)] * 4,
        [],
        [pltpu.VMEM((5, tokens, width), BF), pltpu.SemaphoreType.DMA((5,))],
        raw=[neighbours],
    )


def sets_grads(words, dk, dv, k, v):
    tokens, width = dk.shape[1:]

    def body(word, ins, raws, sends, outs, scratch):
        dk_ref, dv_ref, k_ref, v_ref = ins
        for b in range(5):
            product = (nn(dk_ref[b], k_ref[...]) + nn(dv_ref[b], v_ref[...])).astype(BF)
            if b == 0:
                sends[0][...] = product
            else:
                sends[1][b - 1] = product

    return staged(
        "sets_grads", body, words, [dk, dv, k, v], [low_shape(tokens, width), low_shape(4, tokens, width)], []
    )


def halved(words, bit, terms, cost=None):
    rows, width = min(term.shape[0] for term in terms), terms[0].shape[1]
    half = rows // 2
    if half % 8:
        place = words[2] // bit % 2
        return [
            sum(lax.dynamic_slice_in_dim(term, which * half, half, 0).astype(F32) for term in terms).astype(BF)
            for which in (1 - place, place)
        ]

    def body(word, ins, raws, sends, outs, scratch):
        place = (word[2] // bit) % 2
        for which, target in zip((1 - place, place), sends):
            at = pl.ds(pl.multiple_of(which * half, half), half)
            total = ins[0][at, :].astype(F32)
            for term in ins[1:]:
                total = total + term[at, :].astype(F32)
            target[...] = total.astype(BF)

    return staged("halved", body, words, terms, [low_shape(half, width)] * 2, [], limit=8, cost=cost)


def doubled(words, bit, mine, other, cuts=None):
    half, width = mine.shape
    if half % 8:
        both = jnp.where(
            words[2] // bit % 2 == 0, jnp.concatenate([mine, other], 0), jnp.concatenate([other, mine], 0)
        )
        if cuts is None:
            return [both]
        return jnp.split(both.astype(F32), [sum(cuts[:i]) for i in range(1, len(cuts))], 0)

    def body(word, ins, raws, sends, outs, scratch):
        place = (word[2] // bit) % 2
        target = sends[0] if cuts is None else scratch[0]
        target[pl.ds(pl.multiple_of(place * half, half), half), :] = ins[0][...]
        target[pl.ds(pl.multiple_of((1 - place) * half, half), half), :] = ins[1][...]
        if cuts is not None:
            at = 0
            for result, count in zip(sends, cuts):
                result[...] = target[at : at + count, :].astype(F32)
                at += count

    shapes = [low_shape(2 * half, width)] if cuts is None else [wide_shape(count, width) for count in cuts]
    scratch = [] if cuts is None else [pltpu.VMEM((2 * half, width), BF)]
    return staged("doubled", body, words, [mine, other], shapes, [], scratch, limit=8)


def total(words, left, right):
    def body(word, ins, raws, sends, outs, scratch):
        sends[0][...] = (ins[0][...].astype(F32) + ins[1][...].astype(F32)).astype(BF)

    return staged("total", body, words, [left, right], [low_shape(*left.shape)], [], limit=4)[0]


def mlp_half(words, x0, x1, g0, g1, w_in, bias, w_out):
    rows, width = x0.shape
    units = w_in.shape[1]
    scale = 0.7978845608028654

    def body(word, ins, raws, sends, outs, scratch):
        x0, x1, w_in_ref, bias_ref, g0, g1, w_out_ref = ins
        keep_ref, send_ref = sends
        hidden_ref, pre_ref, sum_ref = outs
        sum_ref[...] = jnp.zeros(sum_ref.shape, F32)
        for i, (x, g, part) in enumerate(((x1, g1, send_ref), (x0, g0, keep_ref))):
            at = (1 - i) * rows
            v = nn(x[...], w_in_ref[...]) + bias_ref[0:1, :]
            square = v * v
            th = jnp.tanh(scale * v * (1.0 + 0.044715 * square))
            hidden_ref[at : at + rows, :] = (0.5 * v * (1.0 + th)).astype(BF)
            slope = 0.5 * (1.0 + th) + 0.5 * scale * v * (1.0 - th * th) * (1.0 + 3 * 0.044715 * square)
            pre = (nt(g[...], w_out_ref[...]) * slope).astype(BF)
            pre_ref[at : at + rows, :] = pre
            sum_ref[0:1, :] += jnp.sum(pre.astype(F32), 0, keepdims=True)
            part[...] = nt(pre, w_in_ref[...]).astype(BF)

    return staged(
        "mlp_half",
        body,
        words,
        [x0, x1, w_in, bias, g0, g1, w_out],
        [low_shape(rows, width)] * 2,
        [low_shape(2 * rows, units)] * 2 + [wide_shape(8, units)],
    )


def mlp_out_grads(words, hidden, gs):
    rows, width = gs[0].shape
    units = hidden[0].shape[1]

    def body(word, ins, raws, sends, outs, scratch):
        h_near, h_far, g0, g1, g2, g3 = ins
        product = jnp.zeros((units, width), F32)
        for h, g, i in ((h_near, g0, 0), (h_near, g1, 1), (h_far, g2, 0), (h_far, g3, 1)):
            product = product + tn(h[i * rows : (i + 1) * rows, :], g[...])
        sends[0][...] = product.astype(BF)

    return staged("mlp_out_grads", body, words, [*hidden, *gs], [low_shape(units, width)], [])[0]


def mlp_in_grads(words, pre, xs):
    rows, width = xs[0].shape
    units = pre[0].shape[1]

    def body(word, ins, raws, sends, outs, scratch):
        p_near, p_far, x0, x1, x2, x3 = ins
        product = jnp.zeros((width, units), F32)
        for p, x, i in ((p_near, x0, 0), (p_near, x1, 1), (p_far, x2, 0), (p_far, x3, 1)):
            product = product + tn(x[...], p[i * rows : (i + 1) * rows, :])
        sends[0][...] = product.astype(BF)

    return staged("mlp_in_grads", body, words, [*pre, *xs], [low_shape(width, units)], [])[0]


def mlp_branch(words, hidden, w_out):
    rows, width = hidden[0].shape[0] // 2, w_out.shape[1]

    def body(word, ins, raws, sends, outs, scratch):
        w_out_ref, h_near, h_far = ins
        for p, (h, i) in enumerate(((h_near, 0), (h_near, 1), (h_far, 0), (h_far, 1))):
            sends[p][...] = nn(h[i * rows : (i + 1) * rows, :], w_out_ref[...]).astype(BF)

    return staged("mlp_branch", body, words, [w_out, *hidden], [low_shape(rows, width)] * 4, [])


def swap(value, axis, bit, size):
    return lax.ppermute(value, axis, [(i, i ^ bit) for i in range(size)])


def core_swap(value):
    return swap(value, "tensor", 1, 4)


def x_swap(value):
    return swap(value, "tensor", 2, 4)


def after(value, *others):
    return lax.optimization_barrier((value, *others))[0]


def add(*terms):
    return sum(term.astype(F32) for term in terms)


class Order:
    def __init__(self, last):
        self.last = last

    def tie(self, value):
        return after(value, self.last)

    def sent(self, value):
        self.last = value
        return value


def halving(order, words, terms, bits, size, cuts, cost=None):
    for bit in bits[:-1]:
        send, keep = halved(words, bit, terms[:-1] + [order.tie(terms[-1])], cost)
        terms = [keep, swap(order.sent(send), "dp", bit, size)]
        yield None
    pack = total(words, terms[0], order.tie(terms[1]))
    got = swap(order.sent(pack), "dp", bits[-1], size)
    yield None
    pack = total(words, pack, order.tie(got))
    for bit in reversed(bits[:-1]):
        got = swap(order.sent(pack), "dp", bit, size)
        yield None
        results = doubled(words, bit, pack, order.tie(got), cuts if bit == bits[0] else None)
        pack = results[0]
    order.sent(pack)
    yield results


def rope_tables(length):
    half = HEAD_DIM // 2
    places = jnp.arange(length).astype(F32)
    frequency = 10000.0 ** (-(jnp.arange(half).astype(F32) * 2.0 / HEAD_DIM))
    angles = places[:, None] * frequency[None, :]
    cosine, sine = jnp.cos(angles), jnp.sin(angles)
    return jnp.concatenate([cosine] * 4, 1), jnp.concatenate([-sine, sine] * 2, 1)


def spans(rows, bits):
    lengths = []
    for bit in bits[:-1]:
        rows /= 2
        lengths.append(5.0 + 0.045 * rows)
    return lengths + [5.0 + 0.09 * rows] + lengths[::-1]


def make_local(dp_size):
    bits = []
    bit = 1
    while bit < dp_size:
        bits.append(bit)
        bit *= 2
    turned = bits[1:2] + bits[0:1] + bits[2:]

    def local(
        tokens,
        out_grad,
        segments,
        neighbours,
        norm_gains,
        norm_biases,
        self_qkv,
        self_out,
        cross_q,
        cross_kv,
        cross_out,
        mlp_in,
        mlp_in_bias,
        mlp_out,
        mlp_out_bias,
    ):
        place = lax.axis_index("dp")
        words = jnp.stack([lax.axis_index("tensor"), place % 2, place]).astype(jnp.int32)
        parity = place % 2
        rows, width = tokens.shape
        seq_len = 4 * rows
        local_width = self_out.shape[0]
        heads = local_width // HEAD_DIM
        gains = norm_gains.astype(F32)
        biases = norm_biases.astype(F32)
        segment = segments[0]
        qkv_rows = self_qkv.transpose(0, 2, 1)
        kv_own = cross_kv.transpose(0, 2, 1)

        kv_send = lax.dynamic_slice_in_dim(kv_own, parity, 1, 0)
        kv_x = x_swap(kv_send)
        tok_far = x_swap(tokens)
        tok_near = core_swap(tokens)
        rest_own = jnp.stack([self_out, cross_q.T, cross_out])
        rest_send = lax.dynamic_slice_in_dim(rest_own, parity * (local_width // 2), local_width // 2, 1)
        cosine, sine = rope_tables(seq_len)
        start = jnp.sum((segment[:, None] < segment[None, :]).astype(jnp.int32), 0)
        start = jnp.broadcast_to(start[None], (8, seq_len))
        bias_row = jnp.broadcast_to(mlp_in_bias.astype(F32)[None], (8, mlp_in_bias.shape[0]))
        tok_far, kv_x, rest_send, cosine, sine, start, gains, biases, bias_row, words, tok_near = (
            lax.optimization_barrier(
                (tok_far, kv_x, rest_send, cosine, sine, start, gains, biases, bias_row, words, tok_near)
            )
        )
        rest_x = x_swap(rest_send)
        tok_both = core_swap(tok_far)
        kv_y = swap(kv_x, "dp", 1, dp_size)
        kv_both_x = core_swap(kv_x)
        kv_core = core_swap(after(kv_own, tok_far))
        rest_core = core_swap(after(rest_own, tok_far))
        up_near = core_swap(after(out_grad, tok_far))

        sends, saved = self_forward(
            words, (tokens, tok_near, tok_far, tok_both), gains, biases, qkv_rows, cosine, sine, start, heads
        )
        attended = [sends[0]] + [swap(sends[j], "tensor", j, 4) for j in (2, 1, 3)]
        kv_y, kv_core, rest_core, up_near, rest_x, kv_both_x = (
            after(item, sends[0]) for item in (kv_y, kv_core, rest_core, up_near, rest_x, kv_both_x)
        )
        kv_both_y = core_swap(kv_y)
        rest_x = after(rest_x, kv_y)
        rest_y = swap(rest_x, "dp", 1, dp_size)
        rest_both_x = core_swap(rest_x)
        up_far = x_swap(after(out_grad, rest_x))
        pool_keys, pool_values, k_full, v_full = pool(
            words, neighbours, kv_own, kv_core, (kv_x, after(kv_y, rest_x)), (kv_both_x, kv_both_y)
        )
        rest_y = after(rest_y, pool_keys, up_far, *attended[1:])
        rest_both_y = core_swap(rest_y)

        in_three, *forward = cross_forward(
            words, tokens, attended, (rest_own, rest_core, rest_x, rest_y, rest_both_x, rest_both_y), pool_keys, pool_values, gains, biases
        )
        x_far = x_swap(in_three)
        x_near = core_swap(in_three)
        up_both = core_swap(after(up_far, in_three))
        keep_near, send_near, h_near, p_near, sum_near = mlp_half(
            words, in_three, x_near, out_grad, up_near, mlp_in, bias_row, mlp_out
        )
        got_near = core_swap(send_near)
        x_far = after(x_far, send_near)
        x_both = core_swap(x_far)
        keep_far, send_far, h_far, p_far, sum_far = mlp_half(
            words, x_far, x_both, up_far, up_both, mlp_in, bias_row, mlp_out
        )
        far = total(words, keep_far, core_swap(send_far))
        h_near = after(h_near, far)
        far = x_swap(far)
        grad_mlp_out = mlp_out_grads(words, (h_near, h_far), (out_grad, up_near, up_far, up_both))
        order = Order(grad_mlp_out)
        chain_m_out = halving(order, words, [grad_mlp_out], bits, dp_size, [width], "slot")
        next(chain_m_out)
        grad_mlp_in = mlp_in_grads(words, (order.tie(p_near), p_far), (in_three, x_near, x_far, x_both))
        chain_m_in = halving(order, words, [grad_mlp_in], turned, dp_size, [width], "slot")
        next(chain_m_in)
        branch = mlp_branch(words, (order.tie(h_near), h_far), mlp_out)
        far = after(far, branch[0])

        ga, backs = cross_backward(
            words, out_grad, (keep_near, got_near, far), forward, pool_keys, pool_values, gains
        )
        in_two, o_two, two = forward[5], forward[7], forward[4]
        one_grad, g1, g2, dq_two, dk_two, dv_two, small = backs
        ups = [ga[0]] + [swap(ga[p], "tensor", j, 4) for p, j in ((2, 1), (1, 2), (3, 3))]
        keep_one, send_one = cross_grads(words, attended, o_two, dq_two, in_two, g1, g2)
        got_one = core_swap(send_one)
        order.sent(send_one)
        next(chain_m_out)
        next(chain_m_in)
        far_one = plus(words, keep_one, [order.tie(got_one)])
        ups[1:] = [after(item, far_one) for item in ups[1:]]
        far_one = x_swap(far_one)
        pack_qkv, grad_one = self_backward(words, ups, saved, cosine, sine, start, heads)
        order.sent(pack_qkv)

        results = {}

        def chain_two():
            keep, *send = pool_grads(words, neighbours, order.tie(dk_two), dv_two)
            got = [core_swap(part) for part in send]
            order.sent(keep)
            yield None
            got[2:] = [order.tie(part) for part in got[2:]]
            far = x_swap(order.sent(plus(words, keep, got)))
            yield None
            pack = merged(words, keep, got[:2], order.tie(far), results["small"])
            yield from halving(order, words, [order.sent(pack)], bits, dp_size, [local_width, local_width, 64])

        def chain_rows():
            keep, send, small_sums = norm_one(
                words, order.tie(grad_one), qkv_rows, (tokens, tok_near, tok_far, tok_both), small, (sum_near, sum_far), branch
            )
            results["small"] = small_sums
            got = core_swap(order.sent(send))
            yield None
            far = x_swap(order.sent(plus(words, keep, [order.tie(got)])))
            yield None
            far = order.tie(far)
            grad = add(keep[:rows], got[:rows], far[:rows])
            normed, inverse = norm_rows(tokens.astype(F32))
            results["tokens_grad"] = (one_grad + norm_back(grad, normed, inverse, gains[0])).astype(BF)
            branch_sum = add(keep[rows : 2 * rows], got[rows : 2 * rows], far[rows:])
            yield (two + branch_sum + mlp_out_bias.astype(F32)).astype(BF)

        def chain_small():
            for bit in (1, 2):
                got = swap(order.sent(order.tie(results["small"])), "tensor", bit, 4)
                yield None
                results["small"] = small_total(words, results["small"], order.tie(got))
            yield results["small"]

        def chain_sets():
            before, mine = sets_grads(words, order.tie(dk_two), dv_two, k_full, v_full)
            back = lax.ppermute(order.sent(before), "tensor", [(i + 1, i) for i in range(3)])
            yield None
            last = add(mine[3], order.tie(back)).astype(BF)
            yield jnp.concatenate([mine[:3], last[None]], 0)

        chain_qkv = halving(order, words, [pack_qkv], bits, dp_size, [local_width] * 3)
        chain_one = halving(order, words, [keep_one, got_one, far_one], turned, dp_size, [local_width] * 3)
        plans = {
            "q": (chain_qkv, 0.1, spans(3 * local_width, bits)),
            "o": (chain_m_out, 0.2, spans(width, bits)[2:]),
            "i": (chain_m_in, 0.3, spans(width, turned)[2:]),
            "t": (chain_two(), 0.4, [9.0, 20.0] + spans(2 * local_width + 64, bits)),
            "r": (chain_rows(), 0.0, [26.0, 24.0]),
            "s": (chain_small(), 0.5, [4.0, 6.0]),
            "1": (chain_one, 8.0, spans(3 * local_width, turned)),
            "b": (chain_sets(), 14.0, [20.0]),
        }
        steps = []
        for name, (_, moment, lengths) in plans.items():
            steps.append((moment, name))
            for length in lengths:
                moment += length
                steps.append((moment, name))
        steps = [name for _, name in sorted(steps)]
        if len(bits) == 3:
            steps = "qoitrss1tsbqoi1tqbirro1qtt1oiq1tqt1t"
        for name in steps:
            results[name] = next(plans[name][0])

        sum_one = results["1"]
        sum_two = results["t"]
        sums = sum_two[2]
        return (
            results["r"],
            results["tokens_grad"],
            results["b"],
            sums[:3],
            sums[3:6],
            jnp.stack(results["q"]).transpose(0, 2, 1),
            sum_one[0],
            sum_one[2].T,
            jnp.stack(sum_two[:2]).transpose(0, 2, 1),
            sum_one[1],
            results["i"][0],
            sums[7],
            results["o"][0],
            sums[6],
        )

    return local


def solution(mesh):
    rows = P(("dp", "tensor"), None)
    in_specs = (
        rows,
        rows,
        P("dp", None),
        P("dp", None, None),
        P(),
        P(),
        P(None, None, "tensor"),
        P("tensor", None),
        P(None, "tensor"),
        P(None, None, "tensor"),
        P("tensor", None),
        P(None, "tensor"),
        P("tensor"),
        P("tensor", None),
        P(),
    )
    out_specs = (
        rows,
        rows,
        P(("dp", "tensor"), None, None),
        P(),
        P(),
        P(None, None, "tensor"),
        P("tensor", None),
        P(None, "tensor"),
        P(None, None, "tensor"),
        P("tensor", None),
        P(None, "tensor"),
        P("tensor"),
        P("tensor", None),
        P(),
    )
    return jax.shard_map(
        make_local(mesh.shape["dp"]),
        mesh=mesh,
        in_specs=in_specs,
        out_specs=out_specs,
        check_vma=False,
    )
```

```python
import functools

import jax
import jax.numpy as jnp
from jax import lax
from jax.experimental import pallas as pl
from jax.experimental.pallas import tpu as pltpu
from jax.sharding import PartitionSpec as P

HEAD_DIM = 64
SPAN = 64
EPS = 1e-05
MASKED = -1e30
LANES = 256
QUAD = LANES // HEAD_DIM
COST = {
    "self_forward": 80,
    "pool": 66,
    "cross_forward": 40,
    "mlp_half": 34,
    "mlp_out_grads": 26,
    "mlp_in_grads": 22,
    "mlp_branch": 21,
    "cross_backward": 85,
    "cross_grads": 18,
    "pool_grads": 0.8,
    "self_backward": 103,
    "norm_one": 0.8,
    "sets_grads": 0.8,
    "slot": 60,
}
BF = jnp.bfloat16
F32 = jnp.float32


def nn(left, right):
    return jnp.dot(left, right, preferred_element_type=F32)


def nt(left, right):
    return lax.dot_general(left, right, (((1,), (1,)), ((), ())), preferred_element_type=F32)


def tn(left, right):
    return lax.dot_general(left, right, (((0,), (0,)), ((), ())), preferred_element_type=F32)


def norm_rows(values):
    center = values - jnp.mean(values, -1, keepdims=True)
    inverse = lax.rsqrt(jnp.mean(center * center, -1, keepdims=True) + EPS)
    return center * inverse, inverse


def norm_back(upstream, normed, inverse, gain):
    scaled = upstream * gain
    return inverse * (
        scaled
        - jnp.mean(scaled, -1, keepdims=True)
        - normed * jnp.mean(scaled * normed, -1, keepdims=True)
    )


def lane_head(shape):
    return lax.broadcasted_iota(jnp.int32, shape, len(shape) - 1) // HEAD_DIM


def half_swap(values):
    half = HEAD_DIM // 2
    width = values.shape[1]
    lane = lax.broadcasted_iota(jnp.int32, values.shape, 1)
    return jnp.where(
        lane % HEAD_DIM < half,
        pltpu.roll(values, width - half, 1),
        pltpu.roll(values, half, 1),
    )


def staged(name, body, words, arrays, near, far, scratch=(), raw=(), limit=16, cost=None):
    n, r, p, f = len(arrays), len(raw), len(near), len(far)

    def kernel(word, *refs):
        cuts = [n, n + r, n + r + p, n + r + p + f]
        body(word, *[refs[a:b] for a, b in zip([0] + cuts, cuts + [len(refs)])])

    hbm, vmem = pl.BlockSpec(memory_space=pltpu.HBM), pl.BlockSpec(memory_space=pltpu.VMEM)
    return pl.pallas_call(
        kernel,
        out_shape=list(near) + list(far),
        in_specs=[pl.BlockSpec(memory_space=pltpu.SMEM)] + [vmem] * n + [hbm] * r,
        out_specs=[vmem] * (p + f),
        scratch_shapes=list(scratch),
        compiler_params=pltpu.CompilerParams(vmem_limit_bytes=limit * 2**20),
        cost_estimate=pl.CostEstimate(flops=int(COST.get(cost or name, 0.8) * 10**9), bytes_accessed=10**4, transcendentals=0),
        name=name,
    )(words, *arrays, *raw)


def plus(words, left, rights):
    rows, width = left.shape
    half = rows // 2

    def body(word, ins, raws, sends, outs, scratch):
        at = -half
        for right in ins[1:]:
            count = right.shape[0]
            begin = max(-at, 0)
            if begin < count:
                to = slice(at + begin, at + count)
                share = ins[0][half + at + begin : half + at + count, :].astype(F32) + right[begin:count, :].astype(F32)
                sends[0][to, :] = share.astype(BF)
            at += count

    return staged("plus", body, words, [left, *rights], [low_shape(half, width)], [], limit=6)[0]


def low_shape(*shape):
    return jax.ShapeDtypeStruct(shape, BF)


def wide_shape(*shape):
    return jax.ShapeDtypeStruct(shape, F32)


def block_mask(start_ref, i, rows):
    keys = (i + 1) * rows
    row = lax.broadcasted_iota(jnp.int32, (keys, rows), 0)
    place = lax.broadcasted_iota(jnp.int32, (keys, rows), 1) + i * rows
    start = start_ref[0:1, i * rows : (i + 1) * rows]
    return jnp.where((row >= start) & (row <= place), 0.0, MASKED)


def tables(cos_ref, sin_ref, part):
    return jnp.concatenate([cos_ref[part, :]] * 2, 1), jnp.concatenate([sin_ref[part, :]] * 2, 1)


def self_forward(words, toks, gains, biases, weights, cosine, sine, start, heads):
    rows, width = toks[0].shape
    total = 4 * rows
    local = heads * HEAD_DIM

    def body(word, ins, raws, sends, outs, scratch):
        tok0, gain_ref, bias_ref, w_ref, tok1, tok2, tok3, cos_ref, sin_ref, start_ref = ins
        x_ref, q_ref, k_ref, v_ref, lse_ref, o_ref = outs
        mask_ref, pad_ref = scratch
        t = word[0]
        for c in range(3):
            pad_ref[c, 0:local, :] = w_ref[c]
            pad_ref[c, local:, :] = jnp.zeros((LANES - local, width), BF)
        for j, tok in enumerate((tok0, tok1, tok2, tok3)):
            normed, _ = norm_rows(tok[...].astype(F32))
            x_ref[pl.ds(pl.multiple_of((t ^ j) * rows, rows), rows), :] = (
                normed * gain_ref[0:1, :] + bias_ref[0:1, :]
            ).astype(BF)
        for i in range(4):
            part = pl.ds(i * rows, rows)
            x = x_ref[part, :]
            cosines, sines = tables(cos_ref, sin_ref, part)
            q = nt(x, pad_ref[0])
            q_ref[part, :] = ((q * cosines + half_swap(q) * sines) * 0.125).astype(BF)
            k = nt(x, pad_ref[1])
            k_ref[part, :] = (k * cosines + half_swap(k) * sines).astype(BF)
            v_ref[part, :] = nt(x, pad_ref[2]).astype(BF)
        lane = lane_head((1, LANES))
        lse_ref[...] = jnp.zeros(lse_ref.shape, F32)
        for i in range(4):
            part = pl.ds(i * rows, rows)
            keys = (i + 1) * rows
            mask_ref[0:keys, :] = block_mask(start_ref, i, rows)
            out = jnp.zeros((rows, LANES), F32)
            for h in range(heads):
                qh = jnp.where(lane == h, q_ref[part, :], jnp.zeros((), BF))
                s = nt(k_ref[0:keys, :], qh) + mask_ref[0:keys, :]
                top = jnp.max(s, 0, keepdims=True)
                p = jnp.exp(s - top)
                norm = jnp.sum(p, 0, keepdims=True)
                lse_ref[h : h + 1, i * rows : (i + 1) * rows] = top + jnp.log(norm)
                low = (p * (1.0 / norm)).astype(BF)
                out = jnp.where(lane == h, tn(low, v_ref[0:keys, :]), out)
            o_ref[part, :] = out.astype(BF)
        for j, a in enumerate(sends):
            a[...] = o_ref[pl.ds(pl.multiple_of((t ^ j) * rows, rows), rows), 0:local]

    out = staged(
        "self_forward",
        body,
        words,
        [toks[0], gains, biases, weights, toks[1], toks[2], toks[3], cosine, sine, start],
        [low_shape(rows, local)] * 4,
        [low_shape(total, width)] + [low_shape(total, LANES)] * 3 + [wide_shape(8, total), low_shape(total, LANES)],
        [pltpu.VMEM((total, rows), F32), pltpu.VMEM((3, LANES, width), BF)],
    )
    return out[:4], out[4:]


def self_backward(words, ups, saved, cosine, sine, start, heads):
    total, width = saved[0].shape
    rows = total // 4
    local = heads * HEAD_DIM

    def body(word, ins, raws, sends, outs, scratch):
        d0, d1, d2, d3, o_ref, q_ref, k_ref, start_ref, v_ref, lse_ref, cos_ref, sin_ref, x_ref = ins
        (pack_ref,) = sends
        (grad_ref,) = outs
        d_ref, mask_ref, dk_ref, dv_ref, delta_ref = scratch
        t = word[0]
        d_ref[...] = jnp.zeros_like(d_ref)
        for j, d in enumerate((d0, d1, d2, d3)):
            d_ref[pl.ds(pl.multiple_of((t ^ j) * rows, rows), rows), 0:local] = d[...]
        pick = (lax.broadcasted_iota(jnp.int32, (8, LANES), 0) == lane_head((8, LANES))).astype(F32)
        delta_ref[...] = lax.dot_general(
            pick,
            d_ref[...].astype(F32) * o_ref[...].astype(F32),
            (((1,), (1,)), ((), ())),
            precision=lax.Precision.HIGHEST,
            preferred_element_type=F32,
        )
        dk_ref[...] = jnp.zeros_like(dk_ref)
        dv_ref[...] = jnp.zeros_like(dv_ref)
        lane = lane_head((1, LANES))
        zero = jnp.zeros((), BF)
        for i in range(4):
            part = pl.ds(i * rows, rows)
            keys = (i + 1) * rows
            mask_ref[0:keys, :] = block_mask(start_ref, i, rows)
            dq = jnp.zeros((rows, LANES), F32)
            for h in range(heads):
                qh = jnp.where(lane == h, q_ref[part, :], zero)
                dh = jnp.where(lane == h, d_ref[part, :], zero)
                lse = lse_ref[h : h + 1, i * rows : (i + 1) * rows]
                delta = delta_ref[h : h + 1, i * rows : (i + 1) * rows]
                s = nt(k_ref[0:keys, :], qh) + mask_ref[0:keys, :]
                p = jnp.exp(s - lse)
                dp = nt(v_ref[0:keys, :], dh)
                ds = (p * (dp - delta)).astype(BF)
                dv_ref[0:keys, :] += nn(p.astype(BF), dh)
                dk_ref[0:keys, :] += nn(ds, qh)
                dq = jnp.where(lane == h, tn(ds, k_ref[0:keys, :]), dq)
            cosines, sines = tables(cos_ref, sin_ref, part)
            dq = dq * 0.125
            grad_ref[part, 0:LANES] = (dq * cosines - half_swap(dq) * sines).astype(BF)
        for i in range(4):
            part = pl.ds(i * rows, rows)
            cosines, sines = tables(cos_ref, sin_ref, part)
            dk = dk_ref[part, :]
            grad_ref[part, LANES : 2 * LANES] = (dk * cosines - half_swap(dk) * sines).astype(BF)
            grad_ref[part, 2 * LANES : 3 * LANES] = dv_ref[part, :].astype(BF)
        for c in range(3):
            product = tn(grad_ref[:, c * LANES : (c + 1) * LANES], x_ref[...])
            pack_ref[c * local : (c + 1) * local, :] = product[0:local].astype(BF)

    x, q, k, v, lse, o = saved
    return staged(
        "self_backward",
        body,
        words,
        [*ups, o, q, k, start, v, lse, cosine, sine, x],
        [low_shape(3 * local, width)],
        [low_shape(total, 3 * LANES)],
        [
            pltpu.VMEM((total, LANES), BF),
            pltpu.VMEM((total, rows), F32),
            pltpu.VMEM((total, LANES), F32),
            pltpu.VMEM((total, LANES), F32),
            pltpu.VMEM((8, total), F32),
        ],
    )


def norm_one(words, grad, weights, toks, small, sums, branch):
    rows, local, width = grad.shape[0] // 4, weights.shape[1], weights.shape[2]

    def body(word, ins, raws, sends, outs, scratch):
        grad_ref, w_ref, small_ref, near_ref, far_ref = ins[:5]
        gain = jnp.zeros((1, width), F32)
        bias = jnp.zeros((1, width), F32)
        for j in range(4):
            at = pl.ds(pl.multiple_of((word[0] ^ j) * rows, rows), rows)
            share = jnp.zeros((rows, width), F32)
            for c in range(3):
                share = share + nn(grad_ref[at, c * LANES : c * LANES + local], w_ref[c])
            normed, _ = norm_rows(ins[5 + j][...].astype(F32))
            gain = gain + jnp.sum(share * normed, 0, keepdims=True)
            bias = bias + jnp.sum(share, 0, keepdims=True)
            target = sends[j % 2]
            at = (j // 2) * 2 * rows
            target[at : at + rows, :] = share.astype(BF)
            target[at + rows : at + 2 * rows, :] = ins[9 + (0, 1, 2, 3)[j]][...]
        sends[2][...] = small_ref[...]
        sends[2][0:1, :] = gain
        sends[2][3:4, :] = bias
        sends[2][7:8, :] = near_ref[0:1, :] + far_ref[0:1, :]

    return staged(
        "norm_one",
        body,
        words,
        [grad, weights, small, *sums, *toks, *branch],
        [low_shape(4 * rows, width)] * 2 + [wide_shape(8, width)],
        [],
    )


def shared(rows):
    row = lax.broadcasted_iota(jnp.int32, rows.shape, 0)
    return jnp.where(row < 7, rows.astype(F32), 0.0)


def plus_small(words, keep, gots, small):
    local, width = gots[0].shape

    def body(word, ins, raws, sends, outs, scratch):
        keep_ref, got_ref, last_ref, small_ref = ins
        sends[0][0:local, :] = (keep_ref[2 * local : 3 * local, :].astype(F32) + got_ref[...].astype(F32)).astype(BF)
        share = keep_ref[3 * local : 4 * local, :].astype(F32) + last_ref[0:local, :].astype(F32)
        sends[0][local : 2 * local, :] = share.astype(BF)
        both = (small_ref[...].astype(BF).astype(F32) + shared(last_ref[local : local + 8, :])).astype(BF)
        sends[0][2 * local :, :] = jnp.zeros((16, width), BF)
        sends[0][2 * local : 2 * local + 8, :] = both
        sends[1][...] = both.astype(F32)

    return staged(
        "plus_small",
        body,
        words,
        [keep, *gots, small],
        [low_shape(2 * local + 16, width), wide_shape(8, width)],
        [],
        limit=8,
    )


def merged(words, keep, gots, far, small):
    local, width = gots[0].shape
    rows = 2 * local

    def body(word, ins, raws, sends, outs, scratch):
        keep_ref, far_ref, small_ref = ins[:3]
        for p, got in enumerate(ins[3:]):
            part = slice(p * local, (p + 1) * local)
            share = keep_ref[part, :].astype(F32) + got[...].astype(F32) + far_ref[part, :].astype(F32)
            sends[0][part, :] = share.astype(BF)
        sends[0][rows:, :] = jnp.zeros((64, width), BF)
        sends[0][rows : rows + 8, :] = (small_ref[...] + shared(far_ref[rows : rows + 8, :])).astype(BF)

    return staged("merged", body, words, [keep, far, small, *gots], [low_shape(rows + 64, width)], [], limit=8)[0]


def spread(values, t, block):
    shape = (LANES, LANES)
    tiled = jnp.concatenate([values] * QUAD, 0)
    row = lax.broadcasted_iota(jnp.int32, shape, 0)
    keep = (row // SPAN) == lane_head(shape)
    if block == 0:
        keep = keep & (row % SPAN > 0) & (t > 0)
    if block == 4:
        keep = keep & (row % SPAN == 0)
    return jnp.where(keep, tiled, jnp.zeros((), values.dtype))


def collect(values, t, block):
    shape = (SPAN, LANES)
    head = lane_head(shape)
    out = jnp.zeros(shape, values.dtype)
    for h in range(QUAD):
        out = jnp.where(head == h, values[h * SPAN : (h + 1) * SPAN], out)
    row = lax.broadcasted_iota(jnp.int32, shape, 0)
    if block == 0:
        out = jnp.where((row > 0) & (t > 0), out, 0.0)
    if block == 4:
        out = jnp.where(row == 0, out, 0.0)
    return out


def unroll_rows(parts):
    return pltpu.roll(jnp.concatenate([parts[0] + parts[4]] + parts[1:4], 0), 4 * SPAN - 1, 0)


def fetch_sets(t, nb_ref, buffer_ref, sem_ref):
    copies = []
    for b in range(5):
        at = jnp.maximum(4 * t - 1 + b, 0)
        copies.append(pltpu.make_async_copy(nb_ref.at[at], buffer_ref.at[b], sem_ref.at[b]))
        copies[-1].start()
    return copies


def pool(words, neighbours, own, core, far, both):
    tokens, width = neighbours.shape[1:]
    local = own.shape[1]

    def body(word, ins, raws, sends, outs, scratch):
        own_ref, core_ref, far_x, far_y, both_x, both_y = ins
        pk_ref, pv_ref, k_ref, v_ref = outs
        copies = fetch_sets(word[0], raws[0], *scratch)
        for i, target in enumerate((k_ref, v_ref)):
            direct = word[1] == i
            target[0:local, :] = own_ref[i]
            target[local : 2 * local, :] = jnp.where(direct, far_x[0], far_y[0])
            target[2 * local : 3 * local, :] = core_ref[i]
            target[3 * local : 4 * local, :] = jnp.where(direct, both_x[0], both_y[0])
        for b in range(5):
            copies[b].wait()
            pk_ref[b] = nt(scratch[0][b], k_ref[...]).astype(BF)
            pv_ref[b] = nt(scratch[0][b], v_ref[...]).astype(BF)

    return staged(
        "pool",
        body,
        words,
        [own, core, *far, *both],
        [],
        [low_shape(5, tokens, width)] * 2 + [low_shape(width, width)] * 2,
        [pltpu.VMEM((5, tokens, width), BF), pltpu.SemaphoreType.DMA((5,))],
        raw=[neighbours],
    )


def cross_forward(words, tokens, a, rest, pool_keys, pool_values, gains, biases):
    rows, width = tokens.shape
    local = a[0].shape[1]
    quads = width // LANES

    def body(word, ins, raws, sends, outs, scratch):
        own_ref, core_ref, far_x, far_y, both_x, both_y, tok_ref, a0, a1, a2, a3, gain_ref, bias_ref, pk_ref, pv_ref = ins
        (in_three_ref,) = sends
        so_ref, cq_ref, co_ref, one_ref, two_ref, in_two_ref, q_ref, o_ref, lse_ref = outs
        t = word[0]
        half = local // 2
        for i, target in enumerate((so_ref, cq_ref, co_ref)):
            target[0:local, :] = own_ref[i]
            target[2 * local : 3 * local, :] = core_ref[i]
            for h in range(2):
                direct = word[1] == h
                at = local + h * half
                target[at : at + half, :] = jnp.where(direct, far_x[i], far_y[i])
                at = 3 * local + h * half
                target[at : at + half, :] = jnp.where(direct, both_x[i], both_y[i])
        resid = tok_ref[...].astype(F32)
        for p, ap in enumerate((a0, a1, a2, a3)):
            resid = resid + nn(ap[...], so_ref[p * local : (p + 1) * local, :])
        one_ref[...] = resid
        normed, _ = norm_rows(resid)
        low = (normed * gain_ref[1:2, :] + bias_ref[1:2, :]).astype(BF)
        in_two_ref[...] = low
        q = nt(low, cq_ref[...]).astype(BF).astype(F32) * 0.125
        q_ref[...] = pltpu.roll(q, 1, 0).astype(BF)
        lse_ref[...] = jnp.zeros(lse_ref.shape, F32)
        for g in range(quads):
            cols = slice(g * LANES, (g + 1) * LANES)
            parts = []
            for b in range(5):
                at = (b % 4) * SPAN
                s = nt(pk_ref[b, :, cols], spread(q_ref[at : at + SPAN, cols], t, b))
                top = jnp.max(s, 0, keepdims=True)
                p = jnp.exp(s - top)
                norm = jnp.sum(p, 0, keepdims=True)
                lse_ref[g * 8 + b : g * 8 + b + 1, :] = top + jnp.log(norm)
                low = (p * (1.0 / norm)).astype(BF)
                parts.append(collect(tn(low, pv_ref[b, :, cols]), t, b))
            o_ref[:, cols] = unroll_rows(parts).astype(BF)
        resid = resid + nn(o_ref[...], co_ref[...])
        two_ref[...] = resid
        normed, _ = norm_rows(resid)
        in_three_ref[...] = (normed * gain_ref[2:3, :] + bias_ref[2:3, :]).astype(BF)

    return staged(
        "cross_forward",
        body,
        words,
        [*rest, tokens, *a, gains, biases, pool_keys, pool_values],
        [low_shape(rows, width)],
        [low_shape(width, width)] * 3
        + [wide_shape(rows, width)] * 2
        + [low_shape(rows, width)] * 3
        + [wide_shape(8 * quads, LANES)],
    )


def cross_backward(words, up, pieces, forward, pool_keys, pool_values, gains):
    rows, width = up.shape
    local = width // 4
    quads = width // LANES
    so, cq, co, one, two, _, q, o, lse = forward

    def body(word, ins, raws, sends, outs, scratch):
        up_ref, s0, s1, two_ref, gain_ref, s2, co_ref, q_ref, lse_ref, pk_ref, pv_ref, cq_ref, one_ref, so_ref = ins
        ga = sends
        one_grad_ref, g1_ref, g2_ref, dq_ref, dk_ref, dv_ref, small_ref = outs
        (d_ref,) = scratch
        t = word[0]
        up = s0[...].astype(F32) + s1[...].astype(F32) + s2[...].astype(F32)
        normed, inverse = norm_rows(two_ref[...])
        out_grad = up_ref[...].astype(F32)
        grads = out_grad + norm_back(up, normed, inverse, gain_ref[2:3, :])
        small_ref[...] = jnp.zeros(small_ref.shape, F32)
        small_ref[2:3, :] = jnp.sum(up * normed, 0, keepdims=True)
        small_ref[5:6, :] = jnp.sum(up, 0, keepdims=True)
        small_ref[6:7, :] = jnp.sum(out_grad, 0, keepdims=True)
        low = grads.astype(BF)
        g2_ref[...] = low
        d = nt(low, co_ref[...]).astype(BF).astype(F32)
        d_ref[...] = pltpu.roll(d, 1, 0).astype(BF)
        for g in range(quads):
            cols = slice(g * LANES, (g + 1) * LANES)
            parts = []
            for b in range(5):
                at = (b % 4) * SPAN
                bd = spread(q_ref[at : at + SPAN, cols], t, b)
                db = spread(d_ref[at : at + SPAN, cols], t, b)
                s = nt(pk_ref[b, :, cols], bd)
                p = jnp.exp(s - lse_ref[g * 8 + b : g * 8 + b + 1, :])
                dp = nt(pv_ref[b, :, cols], db)
                delta = jnp.sum(p * dp, 0, keepdims=True)
                ds = (p * (dp - delta)).astype(BF)
                dv_ref[b, :, cols] = nn(p.astype(BF), db).astype(BF)
                dk_ref[b, :, cols] = nn(ds, bd).astype(BF)
                parts.append(collect(tn(ds, pk_ref[b, :, cols]), t, b))
            dq_ref[:, cols] = (unroll_rows(parts) * 0.125).astype(BF)
        up = nn(dq_ref[...], cq_ref[...])
        normed, inverse = norm_rows(one_ref[...])
        small_ref[1:2, :] = jnp.sum(up * normed, 0, keepdims=True)
        small_ref[4:5, :] = jnp.sum(up, 0, keepdims=True)
        grads = grads + norm_back(up, normed, inverse, gain_ref[1:2, :])
        one_grad_ref[...] = grads
        low = grads.astype(BF)
        g1_ref[...] = low
        for p in range(4):
            ga[p][...] = nt(low, so_ref[p * local : (p + 1) * local, :]).astype(BF)

    out = staged(
        "cross_backward",
        body,
        words,
        [up, pieces[0], pieces[1], two, gains, pieces[2], co, q, lse, pool_keys, pool_values, cq, one, so],
        [low_shape(rows, local)] * 4,
        [wide_shape(rows, width)]
        + [low_shape(rows, width)] * 3
        + [jax.ShapeDtypeStruct(pool_keys.shape, BF)] * 2
        + [wide_shape(8, width)],
        [pltpu.VMEM((rows, width), BF)],
    )
    return out[:4], out[4:]


def cross_grads(words, a, o, dq, in_two, g1, g2):
    width, local = o.shape[1], a[0].shape[1]

    def body(word, ins, raws, sends, outs, scratch):
        a0, a1, a2, a3, g1_ref, o_ref, g2_ref, dq_ref, in_two_ref = ins
        for p, ap in enumerate((a0, a1, a2, a3)):
            at = (p % 2) * 3 * local
            sends[p // 2][at : at + local, :] = tn(ap[...], g1_ref[...]).astype(BF)
        for i, (left, right) in enumerate(((o_ref, g2_ref), (dq_ref, in_two_ref))):
            product = tn(left[...], right[...]).astype(BF)
            for p in range(4):
                at = ((p % 2) * 3 + 1 + i) * local
                sends[p // 2][at : at + local, :] = product[p * local : (p + 1) * local]

    return staged(
        "cross_grads", body, words, [*a, g1, o, g2, dq, in_two], [low_shape(6 * local, width)] * 2, []
    )


def pool_grads(words, neighbours, dk, dv, small):
    tokens, width = neighbours.shape[1:]
    local = width // 4

    def body(word, ins, raws, sends, outs, scratch):
        copies = fetch_sets(word[0], raws[0], *scratch)
        for copy in copies:
            copy.wait()
        sends[4][local:, :] = jnp.zeros((16, width), BF)
        sends[4][local : local + 8, :] = ins[2][...].astype(BF)
        for i, source in enumerate(ins[:2]):
            product = jnp.zeros((width, width), F32)
            for b in range(5):
                product = product + tn(source[b], scratch[0][b])
            product = product.astype(BF)
            for p in range(2):
                at = (2 * p + i) * local
                sends[0][at : at + local, :] = product[p * local : (p + 1) * local]
                sends[1 + 2 * p + i][0:local, :] = product[(2 + p) * local : (3 + p) * local]

    return staged(
        "pool_grads",
        body,
        words,
        [dk, dv, small],
        [low_shape(width, width)] + [low_shape(local, width)] * 3 + [low_shape(local + 16, width)],
        [],
        [pltpu.VMEM((5, tokens, width), BF), pltpu.SemaphoreType.DMA((5,))],
        raw=[neighbours],
    )


def sets_grads(words, dk, dv, k, v):
    tokens, width = dk.shape[1:]

    def body(word, ins, raws, sends, outs, scratch):
        dk_ref, dv_ref, k_ref, v_ref = ins
        for b in range(5):
            product = (nn(dk_ref[b], k_ref[...]) + nn(dv_ref[b], v_ref[...])).astype(BF)
            if b == 0:
                sends[0][...] = product
            else:
                sends[1][b - 1] = product

    return staged(
        "sets_grads", body, words, [dk, dv, k, v], [low_shape(tokens, width), low_shape(4, tokens, width)], []
    )


def halved(words, bit, terms, cost=None):
    rows, width = min(term.shape[0] for term in terms), terms[0].shape[1]
    half = rows // 2
    if half % 8:
        place = words[2] // bit % 2
        return [
            sum(lax.dynamic_slice_in_dim(term, which * half, half, 0).astype(F32) for term in terms).astype(BF)
            for which in (1 - place, place)
        ]

    def body(word, ins, raws, sends, outs, scratch):
        place = (word[2] // bit) % 2
        for which, target in zip((1 - place, place), sends):
            at = pl.ds(pl.multiple_of(which * half, half), half)
            total = ins[0][at, :].astype(F32)
            for term in ins[1:]:
                total = total + term[at, :].astype(F32)
            target[...] = total.astype(BF)

    return staged("halved", body, words, terms, [low_shape(half, width)] * 2, [], limit=8, cost=cost)


def doubled(words, bit, mine, other, cuts=None):
    half, width = mine.shape
    if half % 8:
        both = jnp.where(
            words[2] // bit % 2 == 0, jnp.concatenate([mine, other], 0), jnp.concatenate([other, mine], 0)
        )
        if cuts is None:
            return [both]
        return jnp.split(both.astype(F32), [sum(cuts[:i]) for i in range(1, len(cuts))], 0)

    def body(word, ins, raws, sends, outs, scratch):
        place = (word[2] // bit) % 2
        target = sends[0] if cuts is None else scratch[0]
        target[pl.ds(pl.multiple_of(place * half, half), half), :] = ins[0][...]
        target[pl.ds(pl.multiple_of((1 - place) * half, half), half), :] = ins[1][...]
        if cuts is not None:
            at = 0
            for result, count in zip(sends, cuts):
                result[...] = target[at : at + count, :].astype(F32)
                at += count

    shapes = [low_shape(2 * half, width)] if cuts is None else [wide_shape(count, width) for count in cuts]
    scratch = [] if cuts is None else [pltpu.VMEM((2 * half, width), BF)]
    return staged("doubled", body, words, [mine, other], shapes, [], scratch, limit=8)


def total(words, left, right):
    def body(word, ins, raws, sends, outs, scratch):
        sends[0][...] = (ins[0][...].astype(F32) + ins[1][...].astype(F32)).astype(BF)

    return staged("total", body, words, [left, right], [low_shape(*left.shape)], [], limit=4)[0]


def mlp_half(words, x0, x1, g0, g1, w_in, bias, w_out):
    rows, width = x0.shape
    units = w_in.shape[1]
    scale = 0.7978845608028654

    def body(word, ins, raws, sends, outs, scratch):
        x0, x1, w_in_ref, bias_ref, g0, g1, w_out_ref = ins
        keep_ref, send_ref = sends
        hidden_ref, pre_ref, sum_ref = outs
        sum_ref[...] = jnp.zeros(sum_ref.shape, F32)
        for i, (x, g, part) in enumerate(((x1, g1, send_ref), (x0, g0, keep_ref))):
            at = (1 - i) * rows
            v = nn(x[...], w_in_ref[...]) + bias_ref[0:1, :]
            square = v * v
            th = jnp.tanh(scale * v * (1.0 + 0.044715 * square))
            hidden_ref[at : at + rows, :] = (0.5 * v * (1.0 + th)).astype(BF)
            slope = 0.5 * (1.0 + th) + 0.5 * scale * v * (1.0 - th * th) * (1.0 + 3 * 0.044715 * square)
            pre = (nt(g[...], w_out_ref[...]) * slope).astype(BF)
            pre_ref[at : at + rows, :] = pre
            sum_ref[0:1, :] += jnp.sum(pre.astype(F32), 0, keepdims=True)
            part[...] = nt(pre, w_in_ref[...]).astype(BF)

    return staged(
        "mlp_half",
        body,
        words,
        [x0, x1, w_in, bias, g0, g1, w_out],
        [low_shape(rows, width)] * 2,
        [low_shape(2 * rows, units)] * 2 + [wide_shape(8, units)],
    )


def mlp_out_grads(words, hidden, gs):
    rows, width = gs[0].shape
    units = hidden[0].shape[1]

    def body(word, ins, raws, sends, outs, scratch):
        h_near, h_far, g0, g1, g2, g3 = ins
        product = jnp.zeros((units, width), F32)
        for h, g, i in ((h_near, g0, 0), (h_near, g1, 1), (h_far, g2, 0), (h_far, g3, 1)):
            product = product + tn(h[i * rows : (i + 1) * rows, :], g[...])
        sends[0][...] = product.astype(BF)

    return staged("mlp_out_grads", body, words, [*hidden, *gs], [low_shape(units, width)], [])[0]


def mlp_in_grads(words, pre, xs):
    rows, width = xs[0].shape
    units = pre[0].shape[1]

    def body(word, ins, raws, sends, outs, scratch):
        p_near, p_far, x0, x1, x2, x3 = ins
        product = jnp.zeros((width, units), F32)
        for p, x, i in ((p_near, x0, 0), (p_near, x1, 1), (p_far, x2, 0), (p_far, x3, 1)):
            product = product + tn(x[...], p[i * rows : (i + 1) * rows, :])
        sends[0][...] = product.astype(BF)

    return staged("mlp_in_grads", body, words, [*pre, *xs], [low_shape(width, units)], [])[0]


def mlp_branch(words, hidden, w_out):
    rows, width = hidden[0].shape[0] // 2, w_out.shape[1]

    def body(word, ins, raws, sends, outs, scratch):
        w_out_ref, h_near, h_far = ins
        for p, (h, i) in enumerate(((h_near, 0), (h_near, 1), (h_far, 0), (h_far, 1))):
            sends[p][...] = nn(h[i * rows : (i + 1) * rows, :], w_out_ref[...]).astype(BF)

    return staged("mlp_branch", body, words, [w_out, *hidden], [low_shape(rows, width)] * 4, [])


def swap(value, axis, bit, size):
    return lax.ppermute(value, axis, [(i, i ^ bit) for i in range(size)])


def core_swap(value):
    return swap(value, "tensor", 1, 4)


def x_swap(value):
    return swap(value, "tensor", 2, 4)


def after(value, *others):
    return lax.optimization_barrier((value, *others))[0]


def add(*terms):
    return sum(term.astype(F32) for term in terms)


class Order:
    def __init__(self, last):
        self.last = last

    def tie(self, value):
        return after(value, self.last)

    def sent(self, value):
        self.last = value
        return value


def halving(order, words, terms, bits, size, cuts, cost=None):
    for bit in bits[:-1]:
        send, keep = halved(words, bit, terms[:-1] + [order.tie(terms[-1])], cost)
        terms = [keep, swap(order.sent(send), "dp", bit, size)]
        yield None
    pack = total(words, terms[0], order.tie(terms[1]))
    got = swap(order.sent(pack), "dp", bits[-1], size)
    yield None
    pack = total(words, pack, order.tie(got))
    for bit in reversed(bits[:-1]):
        got = swap(order.sent(pack), "dp", bit, size)
        yield None
        results = doubled(words, bit, pack, order.tie(got), cuts if bit == bits[0] else None)
        pack = results[0]
    order.sent(pack)
    yield results


def rope_tables(length):
    half = HEAD_DIM // 2
    places = jnp.arange(length).astype(F32)
    frequency = 10000.0 ** (-(jnp.arange(half).astype(F32) * 2.0 / HEAD_DIM))
    angles = places[:, None] * frequency[None, :]
    cosine, sine = jnp.cos(angles), jnp.sin(angles)
    return jnp.concatenate([cosine] * 4, 1), jnp.concatenate([-sine, sine] * 2, 1)


def spans(rows, bits):
    lengths = []
    for bit in bits[:-1]:
        rows /= 2
        lengths.append(5.0 + 0.045 * rows)
    return lengths + [5.0 + 0.09 * rows] + lengths[::-1]


def make_local(dp_size):
    bits = []
    bit = 1
    while bit < dp_size:
        bits.append(bit)
        bit *= 2
    turned = bits[1:2] + bits[0:1] + bits[2:]

    def local(
        tokens,
        out_grad,
        segments,
        neighbours,
        norm_gains,
        norm_biases,
        self_qkv,
        self_out,
        cross_q,
        cross_kv,
        cross_out,
        mlp_in,
        mlp_in_bias,
        mlp_out,
        mlp_out_bias,
    ):
        place = lax.axis_index("dp")
        words = jnp.stack([lax.axis_index("tensor"), place % 2, place]).astype(jnp.int32)
        parity = place % 2
        rows, width = tokens.shape
        seq_len = 4 * rows
        local_width = self_out.shape[0]
        heads = local_width // HEAD_DIM
        gains = norm_gains.astype(F32)
        biases = norm_biases.astype(F32)
        segment = segments[0]
        qkv_rows = self_qkv.transpose(0, 2, 1)
        kv_own = cross_kv.transpose(0, 2, 1)

        kv_send = lax.dynamic_slice_in_dim(kv_own, parity, 1, 0)
        kv_x = x_swap(kv_send)
        tok_far = x_swap(tokens)
        tok_near = core_swap(tokens)
        rest_own = jnp.stack([self_out, cross_q.T, cross_out])
        rest_send = lax.dynamic_slice_in_dim(rest_own, parity * (local_width // 2), local_width // 2, 1)
        cosine, sine = rope_tables(seq_len)
        start = jnp.sum((segment[:, None] < segment[None, :]).astype(jnp.int32), 0)
        start = jnp.broadcast_to(start[None], (8, seq_len))
        bias_row = jnp.broadcast_to(mlp_in_bias.astype(F32)[None], (8, mlp_in_bias.shape[0]))
        tok_far, kv_x, rest_send, cosine, sine, start, gains, biases, bias_row, words, tok_near = (
            lax.optimization_barrier(
                (tok_far, kv_x, rest_send, cosine, sine, start, gains, biases, bias_row, words, tok_near)
            )
        )
        rest_x = x_swap(rest_send)
        tok_both = core_swap(tok_far)
        kv_y = swap(kv_x, "dp", 1, dp_size)
        kv_both_x = core_swap(kv_x)
        kv_core = core_swap(after(kv_own, tok_far))
        rest_core = core_swap(after(rest_own, tok_far))
        up_near = core_swap(after(out_grad, tok_far))

        sends, saved = self_forward(
            words, (tokens, tok_near, tok_far, tok_both), gains, biases, qkv_rows, cosine, sine, start, heads
        )
        attended = [sends[0]] + [swap(sends[j], "tensor", j, 4) for j in (2, 1, 3)]
        kv_y, kv_core, rest_core, up_near, rest_x, kv_both_x = (
            after(item, sends[0]) for item in (kv_y, kv_core, rest_core, up_near, rest_x, kv_both_x)
        )
        kv_both_y = core_swap(kv_y)
        rest_x = after(rest_x, kv_y)
        rest_y = swap(rest_x, "dp", 1, dp_size)
        rest_both_x = core_swap(rest_x)
        up_far = x_swap(after(out_grad, rest_x))
        pool_keys, pool_values, k_full, v_full = pool(
            words, neighbours, kv_own, kv_core, (kv_x, after(kv_y, rest_x)), (kv_both_x, kv_both_y)
        )
        rest_y = after(rest_y, pool_keys, up_far, *attended[1:])
        rest_both_y = core_swap(rest_y)

        in_three, *forward = cross_forward(
            words, tokens, attended, (rest_own, rest_core, rest_x, rest_y, rest_both_x, rest_both_y), pool_keys, pool_values, gains, biases
        )
        x_far = x_swap(in_three)
        x_near = core_swap(in_three)
        up_both = core_swap(after(up_far, in_three))
        keep_near, send_near, h_near, p_near, sum_near = mlp_half(
            words, in_three, x_near, out_grad, up_near, mlp_in, bias_row, mlp_out
        )
        got_near = core_swap(send_near)
        x_far = after(x_far, send_near)
        x_both = core_swap(x_far)
        keep_far, send_far, h_far, p_far, sum_far = mlp_half(
            words, x_far, x_both, up_far, up_both, mlp_in, bias_row, mlp_out
        )
        far = total(words, keep_far, core_swap(send_far))
        h_near = after(h_near, far)
        far = x_swap(far)
        grad_mlp_out = mlp_out_grads(words, (h_near, h_far), (out_grad, up_near, up_far, up_both))
        order = Order(grad_mlp_out)
        chain_m_out = halving(order, words, [grad_mlp_out], bits, dp_size, [width], "slot")
        next(chain_m_out)
        grad_mlp_in = mlp_in_grads(words, (order.tie(p_near), p_far), (in_three, x_near, x_far, x_both))
        chain_m_in = halving(order, words, [grad_mlp_in], turned, dp_size, [width], "slot")
        next(chain_m_in)
        branch = mlp_branch(words, (order.tie(h_near), h_far), mlp_out)
        far = after(far, branch[0])

        ga, backs = cross_backward(
            words, out_grad, (keep_near, got_near, far), forward, pool_keys, pool_values, gains
        )
        in_two, o_two, two = forward[5], forward[7], forward[4]
        one_grad, g1, g2, dq_two, dk_two, dv_two, small = backs
        ups = [ga[0]] + [swap(ga[p], "tensor", j, 4) for p, j in ((2, 1), (1, 2), (3, 3))]
        keep_one, send_one = cross_grads(words, attended, o_two, dq_two, in_two, g1, g2)
        got_one = core_swap(send_one)
        order.sent(send_one)
        next(chain_m_out)
        next(chain_m_in)
        far_one = plus(words, keep_one, [order.tie(got_one)])
        ups[1:] = [after(item, far_one) for item in ups[1:]]
        far_one = x_swap(far_one)
        pack_qkv, grad_one = self_backward(words, ups, saved, cosine, sine, start, heads)
        order.sent(pack_qkv)

        results = {}

        def chain_two():
            own = results["small"]
            keep, *send = pool_grads(words, neighbours, order.tie(dk_two), dv_two, own)
            got = [core_swap(part) for part in send]
            order.sent(keep)
            yield None
            send, both = plus_small(words, keep, [order.tie(part) for part in got[2:]], own)
            far = x_swap(order.sent(send))
            yield None
            pack = merged(words, keep, got[:2], order.tie(far), both)
            yield from halving(order, words, [order.sent(pack)], bits, dp_size, [2 * local_width, 64])

        def chain_rows():
            keep, send, small_sums = norm_one(
                words, order.tie(grad_one), qkv_rows, (tokens, tok_near, tok_far, tok_both), small, (sum_near, sum_far), branch
            )
            results["small"] = small_sums
            got = core_swap(order.sent(send))
            yield None
            far = x_swap(order.sent(plus(words, keep, [order.tie(got)])))
            yield None
            far = order.tie(far)
            grad = add(keep[:rows], got[:rows], far[:rows])
            normed, inverse = norm_rows(tokens.astype(F32))
            results["tokens_grad"] = (one_grad + norm_back(grad, normed, inverse, gains[0])).astype(BF)
            branch_sum = add(keep[rows : 2 * rows], got[rows : 2 * rows], far[rows:])
            yield (two + branch_sum + mlp_out_bias.astype(F32)).astype(BF)

        def chain_sets():
            before, mine = sets_grads(words, order.tie(dk_two), dv_two, k_full, v_full)
            back = lax.ppermute(order.sent(before), "tensor", [(i + 1, i) for i in range(3)])
            yield None
            last = add(mine[3], order.tie(back)).astype(BF)
            yield jnp.concatenate([mine[:3], last[None]], 0)

        chain_qkv = halving(order, words, [pack_qkv], bits, dp_size, [3 * local_width])
        chain_one = halving(order, words, [keep_one, got_one, far_one], turned, dp_size, [local_width] * 3)
        plans = {
            "q": (chain_qkv, 0.0, spans(3 * local_width, bits)),
            "o": (chain_m_out, 0.2, spans(width, bits)[2:]),
            "i": (chain_m_in, 0.25, spans(width, turned)[2:]),
            "r": (chain_rows(), 0.3, [36.0, 20.0]),
            "t": (chain_two(), 0.4, [9.0, 20.0] + spans(2 * local_width + 64, bits)),
            "1": (chain_one, 8.0, spans(3 * local_width, turned)),
            "b": (chain_sets(), 14.0, [20.0]),
        }
        steps = []
        for name, (_, moment, lengths) in plans.items():
            steps.append((moment, name))
            for length in lengths:
                moment += length
                steps.append((moment, name))
        steps = [name for _, name in sorted(steps)]
        if len(bits) == 3:
            steps = "qoirt1tbqoi1tqbirro1qtt1oiq1tqt1t"
        for name in steps:
            results[name] = next(plans[name][0])

        sum_one = results["1"]
        sum_two = results["t"]
        sums = sum_two[1]
        return (
            results["r"],
            results["tokens_grad"],
            results["b"],
            sums[:3],
            sums[3:6],
            results["q"][0].reshape(3, local_width, width).transpose(0, 2, 1),
            sum_one[0],
            sum_one[2].T,
            sum_two[0].reshape(2, local_width, width).transpose(0, 2, 1),
            sum_one[1],
            results["i"][0],
            sums[7],
            results["o"][0],
            sums[6],
        )

    return local


def solution(mesh):
    rows = P(("dp", "tensor"), None)
    in_specs = (
        rows,
        rows,
        P("dp", None),
        P("dp", None, None),
        P(),
        P(),
        P(None, None, "tensor"),
        P("tensor", None),
        P(None, "tensor"),
        P(None, None, "tensor"),
        P("tensor", None),
        P(None, "tensor"),
        P("tensor"),
        P("tensor", None),
        P(),
    )
    out_specs = (
        rows,
        rows,
        P(("dp", "tensor"), None, None),
        P(),
        P(),
        P(None, None, "tensor"),
        P("tensor", None),
        P(None, "tensor"),
        P(None, None, "tensor"),
        P("tensor", None),
        P(None, "tensor"),
        P("tensor"),
        P("tensor", None),
        P(),
    )
    return jax.shard_map(
        make_local(mesh.shape["dp"]),
        mesh=mesh,
        in_specs=in_specs,
        out_specs=out_specs,
        check_vma=False,
    )
```

```python
import functools

import jax
import jax.numpy as jnp
from jax import lax
from jax.experimental import pallas as pl
from jax.experimental.pallas import tpu as pltpu
from jax.sharding import PartitionSpec as P

HEAD_DIM = 64
SPAN = 64
EPS = 1e-05
MASKED = -1e30
LANES = 256
QUAD = LANES // HEAD_DIM
COST = {
    "self_forward": 80,
    "pool": 66,
    "cross_forward": 2,
    "mlp_half": 34,
    "mlp_out_grads": 26,
    "mlp_in_grads": 22,
    "mlp_branch": 21,
    "cross_backward": 85,
    "cross_grads": 18,
    "pool_grads": 0.8,
    "self_backward": 103,
    "norm_one": 0.8,
    "sets_grads": 0.8,
    "slot": 60,
}
BF = jnp.bfloat16
F32 = jnp.float32


def nn(left, right):
    return jnp.dot(left, right, preferred_element_type=F32)


def nt(left, right):
    return lax.dot_general(left, right, (((1,), (1,)), ((), ())), preferred_element_type=F32)


def tn(left, right):
    return lax.dot_general(left, right, (((0,), (0,)), ((), ())), preferred_element_type=F32)


def norm_rows(values):
    center = values - jnp.mean(values, -1, keepdims=True)
    inverse = lax.rsqrt(jnp.mean(center * center, -1, keepdims=True) + EPS)
    return center * inverse, inverse


def norm_back(upstream, normed, inverse, gain):
    scaled = upstream * gain
    return inverse * (
        scaled
        - jnp.mean(scaled, -1, keepdims=True)
        - normed * jnp.mean(scaled * normed, -1, keepdims=True)
    )


def lane_head(shape):
    return lax.broadcasted_iota(jnp.int32, shape, len(shape) - 1) // HEAD_DIM


def half_swap(values):
    half = HEAD_DIM // 2
    width = values.shape[1]
    lane = lax.broadcasted_iota(jnp.int32, values.shape, 1)
    return jnp.where(
        lane % HEAD_DIM < half,
        pltpu.roll(values, width - half, 1),
        pltpu.roll(values, half, 1),
    )


def staged(name, body, words, arrays, near, far, scratch=(), raw=(), limit=16, cost=None):
    n, r, p, f = len(arrays), len(raw), len(near), len(far)

    def kernel(word, *refs):
        cuts = [n, n + r, n + r + p, n + r + p + f]
        body(word, *[refs[a:b] for a, b in zip([0] + cuts, cuts + [len(refs)])])

    hbm, vmem = pl.BlockSpec(memory_space=pltpu.HBM), pl.BlockSpec(memory_space=pltpu.VMEM)
    return pl.pallas_call(
        kernel,
        out_shape=list(near) + list(far),
        in_specs=[pl.BlockSpec(memory_space=pltpu.SMEM)] + [vmem] * n + [hbm] * r,
        out_specs=[vmem] * (p + f),
        scratch_shapes=list(scratch),
        compiler_params=pltpu.CompilerParams(vmem_limit_bytes=limit * 2**20),
        cost_estimate=pl.CostEstimate(flops=int(COST.get(cost or name, 0.8) * 10**9), bytes_accessed=10**4, transcendentals=0),
        name=name,
    )(words, *arrays, *raw)


def plus(words, left, rights):
    rows, width = left.shape
    half = rows // 2

    def body(word, ins, raws, sends, outs, scratch):
        at = -half
        for right in ins[1:]:
            count = right.shape[0]
            begin = max(-at, 0)
            if begin < count:
                to = slice(at + begin, at + count)
                share = ins[0][half + at + begin : half + at + count, :].astype(F32) + right[begin:count, :].astype(F32)
                sends[0][to, :] = share.astype(BF)
            at += count

    return staged("plus", body, words, [left, *rights], [low_shape(half, width)], [], limit=6)[0]


def low_shape(*shape):
    return jax.ShapeDtypeStruct(shape, BF)


def wide_shape(*shape):
    return jax.ShapeDtypeStruct(shape, F32)


def block_mask(start_ref, i, rows):
    keys = (i + 1) * rows
    row = lax.broadcasted_iota(jnp.int32, (keys, rows), 0)
    place = lax.broadcasted_iota(jnp.int32, (keys, rows), 1) + i * rows
    start = start_ref[0:1, i * rows : (i + 1) * rows]
    return jnp.where((row >= start) & (row <= place), 0.0, MASKED)


def tables(cos_ref, sin_ref, part):
    return jnp.concatenate([cos_ref[part, :]] * 2, 1), jnp.concatenate([sin_ref[part, :]] * 2, 1)


def self_forward(words, toks, gains, biases, weights, cosine, sine, start, heads):
    rows, width = toks[0].shape
    total = 4 * rows
    local = heads * HEAD_DIM

    def body(word, ins, raws, sends, outs, scratch):
        tok0, gain_ref, bias_ref, w_ref, tok1, tok2, tok3, cos_ref, sin_ref, start_ref = ins
        x_ref, q_ref, k_ref, v_ref, lse_ref, o_ref = outs
        mask_ref, pad_ref = scratch
        t = word[0]
        for c in range(3):
            pad_ref[c, 0:local, :] = w_ref[c]
            pad_ref[c, local:, :] = jnp.zeros((LANES - local, width), BF)
        for j, tok in enumerate((tok0, tok1, tok2, tok3)):
            normed, _ = norm_rows(tok[...].astype(F32))
            x_ref[pl.ds(pl.multiple_of((t ^ j) * rows, rows), rows), :] = (
                normed * gain_ref[0:1, :] + bias_ref[0:1, :]
            ).astype(BF)
        for i in range(4):
            part = pl.ds(i * rows, rows)
            x = x_ref[part, :]
            cosines, sines = tables(cos_ref, sin_ref, part)
            q = nt(x, pad_ref[0])
            q_ref[part, :] = ((q * cosines + half_swap(q) * sines) * 0.125).astype(BF)
            k = nt(x, pad_ref[1])
            k_ref[part, :] = (k * cosines + half_swap(k) * sines).astype(BF)
            v_ref[part, :] = nt(x, pad_ref[2]).astype(BF)
        lane = lane_head((1, LANES))
        lse_ref[...] = jnp.zeros(lse_ref.shape, F32)
        for i in range(4):
            part = pl.ds(i * rows, rows)
            keys = (i + 1) * rows
            mask_ref[0:keys, :] = block_mask(start_ref, i, rows)
            out = jnp.zeros((rows, LANES), F32)
            for h in range(heads):
                qh = jnp.where(lane == h, q_ref[part, :], jnp.zeros((), BF))
                s = nt(k_ref[0:keys, :], qh) + mask_ref[0:keys, :]
                top = jnp.max(s, 0, keepdims=True)
                p = jnp.exp(s - top)
                norm = jnp.sum(p, 0, keepdims=True)
                lse_ref[h : h + 1, i * rows : (i + 1) * rows] = top + jnp.log(norm)
                low = (p * (1.0 / norm)).astype(BF)
                out = jnp.where(lane == h, tn(low, v_ref[0:keys, :]), out)
            o_ref[part, :] = out.astype(BF)
        for j, a in enumerate(sends):
            a[...] = o_ref[pl.ds(pl.multiple_of((t ^ j) * rows, rows), rows), 0:local]

    out = staged(
        "self_forward",
        body,
        words,
        [toks[0], gains, biases, weights, toks[1], toks[2], toks[3], cosine, sine, start],
        [low_shape(rows, local)] * 4,
        [low_shape(total, width)] + [low_shape(total, LANES)] * 3 + [wide_shape(8, total), low_shape(total, LANES)],
        [pltpu.VMEM((total, rows), F32), pltpu.VMEM((3, LANES, width), BF)],
    )
    return out[:4], out[4:]


def self_backward(words, ups, saved, cosine, sine, start, heads):
    total, width = saved[0].shape
    rows = total // 4
    local = heads * HEAD_DIM

    def body(word, ins, raws, sends, outs, scratch):
        d0, d1, d2, d3, o_ref, q_ref, k_ref, start_ref, v_ref, lse_ref, cos_ref, sin_ref, x_ref = ins
        (pack_ref,) = sends
        (grad_ref,) = outs
        d_ref, mask_ref, dk_ref, dv_ref, delta_ref = scratch
        t = word[0]
        d_ref[...] = jnp.zeros_like(d_ref)
        for j, d in enumerate((d0, d1, d2, d3)):
            d_ref[pl.ds(pl.multiple_of((t ^ j) * rows, rows), rows), 0:local] = d[...]
        pick = (lax.broadcasted_iota(jnp.int32, (8, LANES), 0) == lane_head((8, LANES))).astype(F32)
        delta_ref[...] = lax.dot_general(
            pick,
            d_ref[...].astype(F32) * o_ref[...].astype(F32),
            (((1,), (1,)), ((), ())),
            precision=lax.Precision.HIGHEST,
            preferred_element_type=F32,
        )
        dk_ref[...] = jnp.zeros_like(dk_ref)
        dv_ref[...] = jnp.zeros_like(dv_ref)
        lane = lane_head((1, LANES))
        zero = jnp.zeros((), BF)
        for i in range(4):
            part = pl.ds(i * rows, rows)
            keys = (i + 1) * rows
            mask_ref[0:keys, :] = block_mask(start_ref, i, rows)
            dq = jnp.zeros((rows, LANES), F32)
            for h in range(heads):
                qh = jnp.where(lane == h, q_ref[part, :], zero)
                dh = jnp.where(lane == h, d_ref[part, :], zero)
                lse = lse_ref[h : h + 1, i * rows : (i + 1) * rows]
                delta = delta_ref[h : h + 1, i * rows : (i + 1) * rows]
                s = nt(k_ref[0:keys, :], qh) + mask_ref[0:keys, :]
                p = jnp.exp(s - lse)
                dp = nt(v_ref[0:keys, :], dh)
                ds = (p * (dp - delta)).astype(BF)
                dv_ref[0:keys, :] += nn(p.astype(BF), dh)
                dk_ref[0:keys, :] += nn(ds, qh)
                dq = jnp.where(lane == h, tn(ds, k_ref[0:keys, :]), dq)
            cosines, sines = tables(cos_ref, sin_ref, part)
            dq = dq * 0.125
            grad_ref[part, 0:LANES] = (dq * cosines - half_swap(dq) * sines).astype(BF)
        for i in range(4):
            part = pl.ds(i * rows, rows)
            cosines, sines = tables(cos_ref, sin_ref, part)
            dk = dk_ref[part, :]
            grad_ref[part, LANES : 2 * LANES] = (dk * cosines - half_swap(dk) * sines).astype(BF)
            grad_ref[part, 2 * LANES : 3 * LANES] = dv_ref[part, :].astype(BF)
        for c in range(3):
            product = tn(grad_ref[:, c * LANES : (c + 1) * LANES], x_ref[...])
            pack_ref[c * local : (c + 1) * local, :] = product[0:local].astype(BF)

    x, q, k, v, lse, o = saved
    return staged(
        "self_backward",
        body,
        words,
        [*ups, o, q, k, start, v, lse, cosine, sine, x],
        [low_shape(3 * local, width)],
        [low_shape(total, 3 * LANES)],
        [
            pltpu.VMEM((total, LANES), BF),
            pltpu.VMEM((total, rows), F32),
            pltpu.VMEM((total, LANES), F32),
            pltpu.VMEM((total, LANES), F32),
            pltpu.VMEM((8, total), F32),
        ],
    )


def norm_one(words, grad, weights, toks, small, sums, branch):
    rows, local, width = grad.shape[0] // 4, weights.shape[1], weights.shape[2]

    def body(word, ins, raws, sends, outs, scratch):
        grad_ref, w_ref, small_ref, near_ref, far_ref = ins[:5]
        gain = jnp.zeros((1, width), F32)
        bias = jnp.zeros((1, width), F32)
        for j in range(4):
            at = pl.ds(pl.multiple_of((word[0] ^ j) * rows, rows), rows)
            share = jnp.zeros((rows, width), F32)
            for c in range(3):
                share = share + nn(grad_ref[at, c * LANES : c * LANES + local], w_ref[c])
            normed, _ = norm_rows(ins[5 + j][...].astype(F32))
            gain = gain + jnp.sum(share * normed, 0, keepdims=True)
            bias = bias + jnp.sum(share, 0, keepdims=True)
            target = sends[j % 2]
            at = (j // 2) * 2 * rows
            target[at : at + rows, :] = share.astype(BF)
            target[at + rows : at + 2 * rows, :] = ins[9 + (0, 1, 2, 3)[j]][...]
        sends[2][...] = small_ref[...]
        sends[2][0:1, :] = gain
        sends[2][3:4, :] = bias
        sends[2][7:8, :] = near_ref[0:1, :] + far_ref[0:1, :]

    return staged(
        "norm_one",
        body,
        words,
        [grad, weights, small, *sums, *toks, *branch],
        [low_shape(4 * rows, width)] * 2 + [wide_shape(8, width)],
        [],
    )


def shared(rows):
    row = lax.broadcasted_iota(jnp.int32, rows.shape, 0)
    return jnp.where(row < 7, rows.astype(F32), 0.0)


def plus_small(words, keep, gots, small):
    local, width = gots[0].shape

    def body(word, ins, raws, sends, outs, scratch):
        keep_ref, got_ref, last_ref, small_ref = ins
        sends[0][0:local, :] = (keep_ref[2 * local : 3 * local, :].astype(F32) + got_ref[...].astype(F32)).astype(BF)
        share = keep_ref[3 * local : 4 * local, :].astype(F32) + last_ref[0:local, :].astype(F32)
        sends[0][local : 2 * local, :] = share.astype(BF)
        both = (small_ref[...].astype(BF).astype(F32) + shared(last_ref[local : local + 8, :])).astype(BF)
        sends[0][2 * local :, :] = jnp.zeros((16, width), BF)
        sends[0][2 * local : 2 * local + 8, :] = both
        sends[1][...] = both.astype(F32)

    return staged(
        "plus_small",
        body,
        words,
        [keep, *gots, small],
        [low_shape(2 * local + 16, width), wide_shape(8, width)],
        [],
        limit=8,
    )


def merged(words, keep, gots, far, small):
    local, width = gots[0].shape
    rows = 2 * local

    def body(word, ins, raws, sends, outs, scratch):
        keep_ref, far_ref, small_ref = ins[:3]
        for p, got in enumerate(ins[3:]):
            part = slice(p * local, (p + 1) * local)
            share = keep_ref[part, :].astype(F32) + got[...].astype(F32) + far_ref[part, :].astype(F32)
            sends[0][part, :] = share.astype(BF)
        sends[0][rows:, :] = jnp.zeros((64, width), BF)
        sends[0][rows : rows + 8, :] = (small_ref[...] + shared(far_ref[rows : rows + 8, :])).astype(BF)

    return staged("merged", body, words, [keep, far, small, *gots], [low_shape(rows + 64, width)], [], limit=8)[0]


def spread(values, t, block):
    shape = (LANES, LANES)
    tiled = jnp.concatenate([values] * QUAD, 0)
    row = lax.broadcasted_iota(jnp.int32, shape, 0)
    keep = (row // SPAN) == lane_head(shape)
    if block == 0:
        keep = keep & (row % SPAN > 0) & (t > 0)
    if block == 4:
        keep = keep & (row % SPAN == 0)
    return jnp.where(keep, tiled, jnp.zeros((), values.dtype))


def collect(values, t, block):
    shape = (SPAN, LANES)
    head = lane_head(shape)
    out = jnp.zeros(shape, values.dtype)
    for h in range(QUAD):
        out = jnp.where(head == h, values[h * SPAN : (h + 1) * SPAN], out)
    row = lax.broadcasted_iota(jnp.int32, shape, 0)
    if block == 0:
        out = jnp.where((row > 0) & (t > 0), out, 0.0)
    if block == 4:
        out = jnp.where(row == 0, out, 0.0)
    return out


def unroll_rows(parts):
    return pltpu.roll(jnp.concatenate([parts[0] + parts[4]] + parts[1:4], 0), 4 * SPAN - 1, 0)


def fetch_sets(t, nb_ref, buffer_ref, sem_ref):
    copies = []
    for b in range(5):
        at = jnp.maximum(4 * t - 1 + b, 0)
        copies.append(pltpu.make_async_copy(nb_ref.at[at], buffer_ref.at[b], sem_ref.at[b]))
        copies[-1].start()
    return copies


def pool(words, neighbours, own, core, far, both):
    tokens, width = neighbours.shape[1:]
    local = own.shape[1]

    def body(word, ins, raws, sends, outs, scratch):
        own_ref, core_ref, far_x, far_y, both_x, both_y = ins
        pk_ref, pv_ref, k_ref, v_ref = outs
        copies = fetch_sets(word[0], raws[0], *scratch)
        for i, target in enumerate((k_ref, v_ref)):
            direct = word[1] == i
            target[0:local, :] = own_ref[i]
            target[local : 2 * local, :] = jnp.where(direct, far_x[0], far_y[0])
            target[2 * local : 3 * local, :] = core_ref[i]
            target[3 * local : 4 * local, :] = jnp.where(direct, both_x[0], both_y[0])
        for b in range(5):
            copies[b].wait()
            pk_ref[b] = nt(scratch[0][b], k_ref[...]).astype(BF)
            pv_ref[b] = nt(scratch[0][b], v_ref[...]).astype(BF)

    return staged(
        "pool",
        body,
        words,
        [own, core, *far, *both],
        [],
        [low_shape(5, tokens, width)] * 2 + [low_shape(width, width)] * 2,
        [pltpu.VMEM((5, tokens, width), BF), pltpu.SemaphoreType.DMA((5,))],
        raw=[neighbours],
    )


def cross_forward(words, tokens, a, rest, pool_keys, pool_values, gains, biases):
    rows, width = tokens.shape
    local = a[0].shape[1]
    quads = width // LANES

    def body(word, ins, raws, sends, outs, scratch):
        own_ref, core_ref, far_x, far_y, both_x, both_y, tok_ref, a0, a1, a2, a3, gain_ref, bias_ref, pk_ref, pv_ref = ins
        (in_three_ref,) = sends
        so_ref, cq_ref, co_ref, one_ref, two_ref, in_two_ref, q_ref, o_ref, lse_ref = outs
        t = word[0]
        half = local // 2
        for i, target in enumerate((so_ref, cq_ref, co_ref)):
            target[0:local, :] = own_ref[i]
            target[2 * local : 3 * local, :] = core_ref[i]
            for h in range(2):
                direct = word[1] == h
                at = local + h * half
                target[at : at + half, :] = jnp.where(direct, far_x[i], far_y[i])
                at = 3 * local + h * half
                target[at : at + half, :] = jnp.where(direct, both_x[i], both_y[i])
        resid = tok_ref[...].astype(F32)
        for p, ap in enumerate((a0, a1, a2, a3)):
            resid = resid + nn(ap[...], so_ref[p * local : (p + 1) * local, :])
        one_ref[...] = resid
        normed, _ = norm_rows(resid)
        low = (normed * gain_ref[1:2, :] + bias_ref[1:2, :]).astype(BF)
        in_two_ref[...] = low
        q = nt(low, cq_ref[...]).astype(BF).astype(F32) * 0.125
        q_ref[...] = pltpu.roll(q, 1, 0).astype(BF)
        lse_ref[...] = jnp.zeros(lse_ref.shape, F32)
        for g in range(quads):
            cols = slice(g * LANES, (g + 1) * LANES)
            parts = []
            for b in range(5):
                at = (b % 4) * SPAN
                s = nt(pk_ref[b, :, cols], spread(q_ref[at : at + SPAN, cols], t, b))
                top = jnp.max(s, 0, keepdims=True)
                p = jnp.exp(s - top)
                norm = jnp.sum(p, 0, keepdims=True)
                lse_ref[g * 8 + b : g * 8 + b + 1, :] = top + jnp.log(norm)
                low = (p * (1.0 / norm)).astype(BF)
                parts.append(collect(tn(low, pv_ref[b, :, cols]), t, b))
            o_ref[:, cols] = unroll_rows(parts).astype(BF)
        resid = resid + nn(o_ref[...], co_ref[...])
        two_ref[...] = resid
        normed, _ = norm_rows(resid)
        in_three_ref[...] = (normed * gain_ref[2:3, :] + bias_ref[2:3, :]).astype(BF)

    return staged(
        "cross_forward",
        body,
        words,
        [*rest, tokens, *a, gains, biases, pool_keys, pool_values],
        [low_shape(rows, width)],
        [low_shape(width, width)] * 3
        + [wide_shape(rows, width)] * 2
        + [low_shape(rows, width)] * 3
        + [wide_shape(8 * quads, LANES)],
    )


def cross_backward(words, up, pieces, forward, pool_keys, pool_values, gains):
    rows, width = up.shape
    local = width // 4
    quads = width // LANES
    so, cq, co, one, two, _, q, o, lse = forward

    def body(word, ins, raws, sends, outs, scratch):
        up_ref, s0, s1, two_ref, gain_ref, s2, co_ref, q_ref, lse_ref, pk_ref, pv_ref, cq_ref, one_ref, so_ref = ins
        ga = sends
        one_grad_ref, g1_ref, g2_ref, dq_ref, dk_ref, dv_ref, small_ref = outs
        (d_ref,) = scratch
        t = word[0]
        up = s0[...].astype(F32) + s1[...].astype(F32) + s2[...].astype(F32)
        normed, inverse = norm_rows(two_ref[...])
        out_grad = up_ref[...].astype(F32)
        grads = out_grad + norm_back(up, normed, inverse, gain_ref[2:3, :])
        small_ref[...] = jnp.zeros(small_ref.shape, F32)
        small_ref[2:3, :] = jnp.sum(up * normed, 0, keepdims=True)
        small_ref[5:6, :] = jnp.sum(up, 0, keepdims=True)
        small_ref[6:7, :] = jnp.sum(out_grad, 0, keepdims=True)
        low = grads.astype(BF)
        g2_ref[...] = low
        d = nt(low, co_ref[...]).astype(BF).astype(F32)
        d_ref[...] = pltpu.roll(d, 1, 0).astype(BF)
        for g in range(quads):
            cols = slice(g * LANES, (g + 1) * LANES)
            parts = []
            for b in range(5):
                at = (b % 4) * SPAN
                bd = spread(q_ref[at : at + SPAN, cols], t, b)
                db = spread(d_ref[at : at + SPAN, cols], t, b)
                s = nt(pk_ref[b, :, cols], bd)
                p = jnp.exp(s - lse_ref[g * 8 + b : g * 8 + b + 1, :])
                dp = nt(pv_ref[b, :, cols], db)
                delta = jnp.sum(p * dp, 0, keepdims=True)
                ds = (p * (dp - delta)).astype(BF)
                dv_ref[b, :, cols] = nn(p.astype(BF), db).astype(BF)
                dk_ref[b, :, cols] = nn(ds, bd).astype(BF)
                parts.append(collect(tn(ds, pk_ref[b, :, cols]), t, b))
            dq_ref[:, cols] = (unroll_rows(parts) * 0.125).astype(BF)
        up = nn(dq_ref[...], cq_ref[...])
        normed, inverse = norm_rows(one_ref[...])
        small_ref[1:2, :] = jnp.sum(up * normed, 0, keepdims=True)
        small_ref[4:5, :] = jnp.sum(up, 0, keepdims=True)
        grads = grads + norm_back(up, normed, inverse, gain_ref[1:2, :])
        one_grad_ref[...] = grads
        low = grads.astype(BF)
        g1_ref[...] = low
        for p in range(4):
            ga[p][...] = nt(low, so_ref[p * local : (p + 1) * local, :]).astype(BF)

    out = staged(
        "cross_backward",
        body,
        words,
        [up, pieces[0], pieces[1], two, gains, pieces[2], co, q, lse, pool_keys, pool_values, cq, one, so],
        [low_shape(rows, local)] * 4,
        [wide_shape(rows, width)]
        + [low_shape(rows, width)] * 3
        + [jax.ShapeDtypeStruct(pool_keys.shape, BF)] * 2
        + [wide_shape(8, width)],
        [pltpu.VMEM((rows, width), BF)],
    )
    return out[:4], out[4:]


def cross_grads(words, a, o, dq, in_two, g1, g2):
    width, local = o.shape[1], a[0].shape[1]

    def body(word, ins, raws, sends, outs, scratch):
        a0, a1, a2, a3, g1_ref, o_ref, g2_ref, dq_ref, in_two_ref = ins
        for p, ap in enumerate((a0, a1, a2, a3)):
            at = (p % 2) * 3 * local
            sends[p // 2][at : at + local, :] = tn(ap[...], g1_ref[...]).astype(BF)
        for i, (left, right) in enumerate(((o_ref, g2_ref), (dq_ref, in_two_ref))):
            product = tn(left[...], right[...]).astype(BF)
            for p in range(4):
                at = ((p % 2) * 3 + 1 + i) * local
                sends[p // 2][at : at + local, :] = product[p * local : (p + 1) * local]

    return staged(
        "cross_grads", body, words, [*a, g1, o, g2, dq, in_two], [low_shape(6 * local, width)] * 2, []
    )


def pool_grads(words, neighbours, dk, dv, small):
    tokens, width = neighbours.shape[1:]
    local = width // 4

    def body(word, ins, raws, sends, outs, scratch):
        copies = fetch_sets(word[0], raws[0], *scratch)
        for copy in copies:
            copy.wait()
        sends[4][local:, :] = jnp.zeros((16, width), BF)
        sends[4][local : local + 8, :] = ins[2][...].astype(BF)
        for i, source in enumerate(ins[:2]):
            product = jnp.zeros((width, width), F32)
            for b in range(5):
                product = product + tn(source[b], scratch[0][b])
            product = product.astype(BF)
            for p in range(2):
                at = (2 * p + i) * local
                sends[0][at : at + local, :] = product[p * local : (p + 1) * local]
                sends[1 + 2 * p + i][0:local, :] = product[(2 + p) * local : (3 + p) * local]

    return staged(
        "pool_grads",
        body,
        words,
        [dk, dv, small],
        [low_shape(width, width)] + [low_shape(local, width)] * 3 + [low_shape(local + 16, width)],
        [],
        [pltpu.VMEM((5, tokens, width), BF), pltpu.SemaphoreType.DMA((5,))],
        raw=[neighbours],
    )


def sets_grads(words, dk, dv, k, v):
    tokens, width = dk.shape[1:]

    def body(word, ins, raws, sends, outs, scratch):
        dk_ref, dv_ref, k_ref, v_ref = ins
        for b in range(5):
            product = (nn(dk_ref[b], k_ref[...]) + nn(dv_ref[b], v_ref[...])).astype(BF)
            if b == 0:
                sends[0][...] = product
            else:
                sends[1][b - 1] = product

    return staged(
        "sets_grads", body, words, [dk, dv, k, v], [low_shape(tokens, width), low_shape(4, tokens, width)], []
    )


def halved(words, bit, terms, cost=None):
    rows, width = min(term.shape[0] for term in terms), terms[0].shape[1]
    half = rows // 2
    if half % 8:
        place = words[2] // bit % 2
        return [
            sum(lax.dynamic_slice_in_dim(term, which * half, half, 0).astype(F32) for term in terms).astype(BF)
            for which in (1 - place, place)
        ]

    def body(word, ins, raws, sends, outs, scratch):
        place = (word[2] // bit) % 2
        for which, target in zip((1 - place, place), sends):
            at = pl.ds(pl.multiple_of(which * half, half), half)
            total = ins[0][at, :].astype(F32)
            for term in ins[1:]:
                total = total + term[at, :].astype(F32)
            target[...] = total.astype(BF)

    return staged("halved", body, words, terms, [low_shape(half, width)] * 2, [], limit=8, cost=cost)


def doubled(words, bit, mine, other, cuts=None):
    half, width = mine.shape
    if half % 8:
        both = jnp.where(
            words[2] // bit % 2 == 0, jnp.concatenate([mine, other], 0), jnp.concatenate([other, mine], 0)
        )
        if cuts is None:
            return [both]
        return jnp.split(both.astype(F32), [sum(cuts[:i]) for i in range(1, len(cuts))], 0)

    def body(word, ins, raws, sends, outs, scratch):
        place = (word[2] // bit) % 2
        target = sends[0] if cuts is None else scratch[0]
        target[pl.ds(pl.multiple_of(place * half, half), half), :] = ins[0][...]
        target[pl.ds(pl.multiple_of((1 - place) * half, half), half), :] = ins[1][...]
        if cuts is not None:
            at = 0
            for result, count in zip(sends, cuts):
                result[...] = target[at : at + count, :].astype(F32)
                at += count

    shapes = [low_shape(2 * half, width)] if cuts is None else [wide_shape(count, width) for count in cuts]
    scratch = [] if cuts is None else [pltpu.VMEM((2 * half, width), BF)]
    return staged("doubled", body, words, [mine, other], shapes, [], scratch, limit=8)


def total(words, left, right):
    def body(word, ins, raws, sends, outs, scratch):
        sends[0][...] = (ins[0][...].astype(F32) + ins[1][...].astype(F32)).astype(BF)

    return staged("total", body, words, [left, right], [low_shape(*left.shape)], [], limit=4)[0]


def mlp_half(words, x0, x1, g0, g1, w_in, bias, w_out):
    rows, width = x0.shape
    units = w_in.shape[1]
    scale = 0.7978845608028654

    def body(word, ins, raws, sends, outs, scratch):
        x0, x1, w_in_ref, bias_ref, g0, g1, w_out_ref = ins
        keep_ref, send_ref = sends
        hidden_ref, pre_ref, sum_ref = outs
        sum_ref[...] = jnp.zeros(sum_ref.shape, F32)
        for i, (x, g, part) in enumerate(((x1, g1, send_ref), (x0, g0, keep_ref))):
            at = (1 - i) * rows
            v = nn(x[...], w_in_ref[...]) + bias_ref[0:1, :]
            square = v * v
            th = jnp.tanh(scale * v * (1.0 + 0.044715 * square))
            hidden_ref[at : at + rows, :] = (0.5 * v * (1.0 + th)).astype(BF)
            slope = 0.5 * (1.0 + th) + 0.5 * scale * v * (1.0 - th * th) * (1.0 + 3 * 0.044715 * square)
            pre = (nt(g[...], w_out_ref[...]) * slope).astype(BF)
            pre_ref[at : at + rows, :] = pre
            sum_ref[0:1, :] += jnp.sum(pre.astype(F32), 0, keepdims=True)
            part[...] = nt(pre, w_in_ref[...]).astype(BF)

    return staged(
        "mlp_half",
        body,
        words,
        [x0, x1, w_in, bias, g0, g1, w_out],
        [low_shape(rows, width)] * 2,
        [low_shape(2 * rows, units)] * 2 + [wide_shape(8, units)],
    )


def mlp_out_grads(words, hidden, gs):
    rows, width = gs[0].shape
    units = hidden[0].shape[1]

    def body(word, ins, raws, sends, outs, scratch):
        h_near, h_far, g0, g1, g2, g3 = ins
        product = jnp.zeros((units, width), F32)
        for h, g, i in ((h_near, g0, 0), (h_near, g1, 1), (h_far, g2, 0), (h_far, g3, 1)):
            product = product + tn(h[i * rows : (i + 1) * rows, :], g[...])
        sends[0][...] = product.astype(BF)

    return staged("mlp_out_grads", body, words, [*hidden, *gs], [low_shape(units, width)], [])[0]


def mlp_in_grads(words, pre, xs):
    rows, width = xs[0].shape
    units = pre[0].shape[1]

    def body(word, ins, raws, sends, outs, scratch):
        p_near, p_far, x0, x1, x2, x3 = ins
        product = jnp.zeros((width, units), F32)
        for p, x, i in ((p_near, x0, 0), (p_near, x1, 1), (p_far, x2, 0), (p_far, x3, 1)):
            product = product + tn(x[...], p[i * rows : (i + 1) * rows, :])
        sends[0][...] = product.astype(BF)

    return staged("mlp_in_grads", body, words, [*pre, *xs], [low_shape(width, units)], [])[0]


def mlp_branch(words, hidden, w_out):
    rows, width = hidden[0].shape[0] // 2, w_out.shape[1]

    def body(word, ins, raws, sends, outs, scratch):
        w_out_ref, h_near, h_far = ins
        for p, (h, i) in enumerate(((h_near, 0), (h_near, 1), (h_far, 0), (h_far, 1))):
            sends[p][...] = nn(h[i * rows : (i + 1) * rows, :], w_out_ref[...]).astype(BF)

    return staged("mlp_branch", body, words, [w_out, *hidden], [low_shape(rows, width)] * 4, [])


def swap(value, axis, bit, size):
    return lax.ppermute(value, axis, [(i, i ^ bit) for i in range(size)])


def core_swap(value):
    return swap(value, "tensor", 1, 4)


def x_swap(value):
    return swap(value, "tensor", 2, 4)


def after(value, *others):
    return lax.optimization_barrier((value, *others))[0]


def add(*terms):
    return sum(term.astype(F32) for term in terms)


class Order:
    def __init__(self, last):
        self.last = last

    def tie(self, value):
        return after(value, self.last)

    def sent(self, value):
        self.last = value
        return value


def halving(order, words, terms, bits, size, cuts, cost=None):
    for bit in bits[:-1]:
        send, keep = halved(words, bit, terms[:-1] + [order.tie(terms[-1])], cost)
        terms = [keep, swap(order.sent(send), "dp", bit, size)]
        yield None
    pack = total(words, terms[0], order.tie(terms[1]))
    got = swap(order.sent(pack), "dp", bits[-1], size)
    yield None
    pack = total(words, pack, order.tie(got))
    for bit in reversed(bits[:-1]):
        got = swap(order.sent(pack), "dp", bit, size)
        yield None
        results = doubled(words, bit, pack, order.tie(got), cuts if bit == bits[0] else None)
        pack = results[0]
    order.sent(pack)
    yield results


def rope_tables(length):
    half = HEAD_DIM // 2
    places = jnp.arange(length).astype(F32)
    frequency = 10000.0 ** (-(jnp.arange(half).astype(F32) * 2.0 / HEAD_DIM))
    angles = places[:, None] * frequency[None, :]
    cosine, sine = jnp.cos(angles), jnp.sin(angles)
    return jnp.concatenate([cosine] * 4, 1), jnp.concatenate([-sine, sine] * 2, 1)


def spans(rows, bits):
    lengths = []
    for bit in bits[:-1]:
        rows /= 2
        lengths.append(5.0 + 0.045 * rows)
    return lengths + [5.0 + 0.09 * rows] + lengths[::-1]


def make_local(dp_size):
    bits = []
    bit = 1
    while bit < dp_size:
        bits.append(bit)
        bit *= 2
    turned = bits[1:2] + bits[0:1] + bits[2:]

    def local(
        tokens,
        out_grad,
        segments,
        neighbours,
        norm_gains,
        norm_biases,
        self_qkv,
        self_out,
        cross_q,
        cross_kv,
        cross_out,
        mlp_in,
        mlp_in_bias,
        mlp_out,
        mlp_out_bias,
    ):
        place = lax.axis_index("dp")
        words = jnp.stack([lax.axis_index("tensor"), place % 2, place]).astype(jnp.int32)
        parity = place % 2
        rows, width = tokens.shape
        seq_len = 4 * rows
        local_width = self_out.shape[0]
        heads = local_width // HEAD_DIM
        gains = norm_gains.astype(F32)
        biases = norm_biases.astype(F32)
        segment = segments[0]
        qkv_rows = self_qkv.transpose(0, 2, 1)
        kv_own = cross_kv.transpose(0, 2, 1)

        kv_send = lax.dynamic_slice_in_dim(kv_own, parity, 1, 0)
        kv_x = x_swap(kv_send)
        tok_far = x_swap(tokens)
        tok_near = core_swap(tokens)
        rest_own = jnp.stack([self_out, cross_q.T, cross_out])
        rest_send = lax.dynamic_slice_in_dim(rest_own, parity * (local_width // 2), local_width // 2, 1)
        cosine, sine = rope_tables(seq_len)
        start = jnp.sum((segment[:, None] < segment[None, :]).astype(jnp.int32), 0)
        start = jnp.broadcast_to(start[None], (8, seq_len))
        bias_row = jnp.broadcast_to(mlp_in_bias.astype(F32)[None], (8, mlp_in_bias.shape[0]))
        tok_far, kv_x, rest_send, cosine, sine, start, gains, biases, bias_row, words, tok_near = (
            lax.optimization_barrier(
                (tok_far, kv_x, rest_send, cosine, sine, start, gains, biases, bias_row, words, tok_near)
            )
        )
        rest_x = x_swap(rest_send)
        tok_both = core_swap(tok_far)
        kv_y = swap(kv_x, "dp", 1, dp_size)
        kv_both_x = core_swap(kv_x)
        kv_core = core_swap(after(kv_own, tok_far))
        rest_core = core_swap(after(rest_own, tok_far))
        up_near = core_swap(after(out_grad, tok_far))

        sends, saved = self_forward(
            words, (tokens, tok_near, tok_far, tok_both), gains, biases, qkv_rows, cosine, sine, start, heads
        )
        attended = [sends[0]] + [swap(sends[j], "tensor", j, 4) for j in (2, 1, 3)]
        kv_y, kv_core, rest_core, up_near, rest_x, kv_both_x = (
            after(item, sends[0]) for item in (kv_y, kv_core, rest_core, up_near, rest_x, kv_both_x)
        )
        kv_both_y = core_swap(kv_y)
        rest_x = after(rest_x, kv_y)
        rest_y = swap(rest_x, "dp", 1, dp_size)
        rest_both_x = core_swap(rest_x)
        up_far = x_swap(after(out_grad, rest_x))
        pool_keys, pool_values, k_full, v_full = pool(
            words, neighbours, kv_own, kv_core, (kv_x, after(kv_y, rest_x)), (kv_both_x, kv_both_y)
        )
        rest_y = after(rest_y, pool_keys, *attended[1:])
        rest_both_y = core_swap(rest_y)

        in_three, *forward = cross_forward(
            words, tokens, attended, (rest_own, rest_core, rest_x, rest_y, rest_both_x, rest_both_y), pool_keys, pool_values, gains, biases
        )
        x_far = x_swap(in_three)
        x_near = core_swap(in_three)
        up_both = core_swap(after(up_far, in_three))
        keep_near, send_near, h_near, p_near, sum_near = mlp_half(
            words, in_three, x_near, out_grad, up_near, mlp_in, bias_row, mlp_out
        )
        got_near = core_swap(send_near)
        x_far = after(x_far, send_near)
        x_both = core_swap(x_far)
        keep_far, send_far, h_far, p_far, sum_far = mlp_half(
            words, x_far, x_both, up_far, up_both, mlp_in, bias_row, mlp_out
        )
        far = total(words, keep_far, core_swap(send_far))
        h_near = after(h_near, far)
        far = x_swap(far)
        grad_mlp_out = mlp_out_grads(words, (h_near, h_far), (out_grad, up_near, up_far, up_both))
        order = Order(grad_mlp_out)
        chain_m_out = halving(order, words, [grad_mlp_out], bits, dp_size, [width], "slot")
        next(chain_m_out)
        grad_mlp_in = mlp_in_grads(words, (order.tie(p_near), p_far), (in_three, x_near, x_far, x_both))
        chain_m_in = halving(order, words, [grad_mlp_in], turned, dp_size, [width], "slot")
        next(chain_m_in)
        branch = mlp_branch(words, (order.tie(h_near), h_far), mlp_out)
        far = after(far, branch[0])

        ga, backs = cross_backward(
            words, out_grad, (keep_near, got_near, far), forward, pool_keys, pool_values, gains
        )
        in_two, o_two, two = forward[5], forward[7], forward[4]
        one_grad, g1, g2, dq_two, dk_two, dv_two, small = backs
        ups = [ga[0]] + [swap(ga[p], "tensor", j, 4) for p, j in ((2, 1), (1, 2), (3, 3))]
        keep_one, send_one = cross_grads(words, attended, o_two, dq_two, in_two, g1, g2)
        got_one = core_swap(send_one)
        order.sent(send_one)
        next(chain_m_out)
        next(chain_m_in)
        far_one = plus(words, keep_one, [order.tie(got_one)])
        ups[1:] = [after(item, far_one) for item in ups[1:]]
        far_one = x_swap(far_one)
        pack_qkv, grad_one = self_backward(words, ups, saved, cosine, sine, start, heads)
        order.sent(pack_qkv)

        results = {}

        def chain_two():
            own = results["small"]
            keep, *send = pool_grads(words, neighbours, order.tie(dk_two), dv_two, own)
            got = [core_swap(part) for part in send]
            order.sent(keep)
            yield None
            send, both = plus_small(words, keep, [order.tie(part) for part in got[2:]], own)
            far = x_swap(order.sent(send))
            yield None
            pack = merged(words, keep, got[:2], order.tie(far), both)
            yield from halving(order, words, [order.sent(pack)], bits, dp_size, [2 * local_width, 64])

        def chain_rows():
            keep, send, small_sums = norm_one(
                words, order.tie(grad_one), qkv_rows, (tokens, tok_near, tok_far, tok_both), small, (sum_near, sum_far), branch
            )
            results["small"] = small_sums
            got = core_swap(order.sent(send))
            yield None
            far = x_swap(order.sent(plus(words, keep, [order.tie(got)])))
            yield None
            far = order.tie(far)
            grad = add(keep[:rows], got[:rows], far[:rows])
            normed, inverse = norm_rows(tokens.astype(F32))
            results["tokens_grad"] = (one_grad + norm_back(grad, normed, inverse, gains[0])).astype(BF)
            branch_sum = add(keep[rows : 2 * rows], got[rows : 2 * rows], far[rows:])
            yield (two + branch_sum + mlp_out_bias.astype(F32)).astype(BF)

        def chain_sets():
            before, mine = sets_grads(words, order.tie(dk_two), dv_two, k_full, v_full)
            back = lax.ppermute(order.sent(before), "tensor", [(i + 1, i) for i in range(3)])
            yield None
            last = add(mine[3], order.tie(back)).astype(BF)
            yield jnp.concatenate([mine[:3], last[None]], 0)

        chain_qkv = halving(order, words, [pack_qkv], bits, dp_size, [3 * local_width])
        chain_one = halving(order, words, [keep_one, got_one, far_one], turned, dp_size, [local_width] * 3)
        plans = {
            "q": (chain_qkv, 0.0, spans(3 * local_width, bits)),
            "o": (chain_m_out, 0.2, spans(width, bits)[2:]),
            "i": (chain_m_in, 0.25, spans(width, turned)[2:]),
            "r": (chain_rows(), 0.3, [36.0, 20.0]),
            "t": (chain_two(), 0.4, [9.0, 20.0] + spans(2 * local_width + 64, bits)),
            "1": (chain_one, 8.0, spans(3 * local_width, turned)),
            "b": (chain_sets(), 14.0, [20.0]),
        }
        steps = []
        for name, (_, moment, lengths) in plans.items():
            steps.append((moment, name))
            for length in lengths:
                moment += length
                steps.append((moment, name))
        steps = [name for _, name in sorted(steps)]
        if len(bits) == 3:
            steps = "qoirt1tbqoi1tqbirro1qtt1oiq1tqt1t"
        for name in steps:
            results[name] = next(plans[name][0])

        sum_one = results["1"]
        sum_two = results["t"]
        sums = sum_two[1]
        return (
            results["r"],
            results["tokens_grad"],
            results["b"],
            sums[:3],
            sums[3:6],
            results["q"][0].reshape(3, local_width, width).transpose(0, 2, 1),
            sum_one[0],
            sum_one[2].T,
            sum_two[0].reshape(2, local_width, width).transpose(0, 2, 1),
            sum_one[1],
            results["i"][0],
            sums[7],
            results["o"][0],
            sums[6],
        )

    return local


def solution(mesh):
    rows = P(("dp", "tensor"), None)
    in_specs = (
        rows,
        rows,
        P("dp", None),
        P("dp", None, None),
        P(),
        P(),
        P(None, None, "tensor"),
        P("tensor", None),
        P(None, "tensor"),
        P(None, None, "tensor"),
        P("tensor", None),
        P(None, "tensor"),
        P("tensor"),
        P("tensor", None),
        P(),
    )
    out_specs = (
        rows,
        rows,
        P(("dp", "tensor"), None, None),
        P(),
        P(),
        P(None, None, "tensor"),
        P("tensor", None),
        P(None, "tensor"),
        P(None, None, "tensor"),
        P("tensor", None),
        P(None, "tensor"),
        P("tensor"),
        P("tensor", None),
        P(),
    )
    return jax.shard_map(
        make_local(mesh.shape["dp"]),
        mesh=mesh,
        in_specs=in_specs,
        out_specs=out_specs,
        check_vma=False,
    )
```
